32 devices in a mesh: section: 2 (over x), dp: 16 (over z, y, core).
Axes of the slice: x: 2, y: 2, z: 4, core: 2. Of those that a mesh axis runs over, the one named last changes fastest.
Arguments:
- ends: bfloat16 [2, 16384, 512], P('section', 'dp'), may hold values from -6 to 6
- lengths: int32 [32], P('dp'), may hold values from 144 to 512, as said below
- seg_group: int32 [32], P('dp'), may hold values from 0 to 1
- norm_gain: float32 [2, 3, 512], P('section'), may hold values from 0.5 to 1.5
- norm_shift: float32 [2, 3, 512], P('section'), may hold values from -1 to 1
- w_query: bfloat16 [2, 512, 512], P('section'), may hold values from -0.25 to 0.25
- w_key: bfloat16 [2, 512, 512], P('section'), may hold values from -0.25 to 0.25
- w_value: bfloat16 [2, 512, 512], P('section'), may hold values from -0.25 to 0.25
- qv_bias: float32 [2, 2, 512], P('section'), may hold values from -1.5 to 1.5
- w_out: bfloat16 [2, 512, 512], P('section'), may hold values from -0.75 to 0.75
- out_bias: float32 [2, 512], P('section'), may hold values from -1.5 to 1.5
- w_up: bfloat16 [2, 512, 2048], P('section'), may hold values from -0.25 to 0.25
- up_bias: float32 [2, 2048], P('section'), may hold values from -2.5 to 2.5
- w_down: bfloat16 [2, 2048, 512], P('section'), may hold values from -0.125 to 0.125
- down_bias: float32 [2, 512], P('section'), may hold values from -1.5 to 1.5
Outputs:
- ends_out: bfloat16 [2, 16384, 512], P('section', 'dp')
- grad_norm_gain: float32 [2, 3, 512], P('section')
- grad_norm_shift: float32 [2, 3, 512], P('section')
- grad_w_query: float32 [2, 512, 512], P('section')
- grad_w_key: float32 [2, 512, 512], P('section')
- grad_w_value: float32 [2, 512, 512], P('section')
- grad_qv_bias: float32 [2, 2, 512], P('section')
- grad_w_out: float32 [2, 512, 512], P('section')
- grad_out_bias: float32 [2, 512], P('section')
- grad_w_up: float32 [2, 512, 2048], P('section')
- grad_up_bias: float32 [2, 2048], P('section')
- grad_w_down: float32 [2, 2048, 512], P('section')
- grad_down_bias: float32 [2, 512], P('section')
The draws below stay inside these ranges and needn't reach their ends.
Inputs may be any that keep to these rules, and one draw needn't show every extreme that they name: `lengths`: frames of each utterance; in every draw one utterance has exactly 512 frames and one exactly 144.
All inputs are finite; a program needn't handle non-finite values.
Results may differ from the reference program's by a relative error of at most 0.02.
Values may be sent and summed in bfloat16 or wider, within the bound.
No kernel may reach another device: no remote copies, remote signals or barrier semaphores. Data moves between devices by JAX's collectives and lax.ppermute only.
A program may use at most 256 MiB of HBM per device.

```python
import jax
import jax.numpy as jnp
from jax import lax

D = 512
H = 8
E = 64
FF = 2048
SLOT = 512
MINLEN = 144
BLOCK = 512
LEFT = 30
RIGHT = 4
MEM = 4
UTTS = 32
TOKENS = 16384


def draw_lengths(key, part):
    key = jax.random.fold_in(key, 7)
    first_key, second_key = jax.random.split(key)
    base = jax.random.randint(first_key, (UTTS,), MINLEN, SLOT + 1, dtype=jnp.int32)
    order = jax.random.permutation(second_key, UTTS)
    base = base.at[order[0]].set(SLOT)
    base = base.at[order[1]].set(MINLEN)
    return base.astype(jnp.int32)


def set_ends(drawn, rng, least, high):
    longest = drawn.shape.index(max(drawn.shape))
    spots = []
    for shift in (0, 1):
        where = [jax.random.randint(jax.random.fold_in(rng, axis), (), 0, length) for axis, length in enumerate(drawn.shape)]
        where[longest] = (where[longest] + shift) % drawn.shape[longest]
        spots.append(tuple(where))
    return drawn.at[spots[0]].set(least).at[spots[1]].set(high)


def block_levels(stream_key, shape, cuts, least, high):
    level = 1.0
    for position, shards_of in cuts:
        heights = jax.random.uniform(jax.random.fold_in(jax.random.fold_in(stream_key, 6), position), (shards_of,), jnp.float32, least / len(cuts), high / len(cuts))
        level = level * jnp.repeat(jnp.exp(heights), shape[position] // shards_of).reshape((-1,) + (1,) * (len(shape) - 1 - position))
    return level


def bell_draw(stream_key, shape, scale, most, cuts=(), kind=jnp.bfloat16):
    entries = jax.random.normal(stream_key, shape, jnp.float32) * scale
    if len(cuts) > 0:
        entries = block_levels(stream_key, shape, cuts, -0.22, 0.18) * entries
    return jnp.clip(entries, min=-most, max=most).astype(kind)


def setup_inputs(seed: int = 0) -> dict:
    splits = jax.random.split(jax.random.key(seed), 16)
    ends = bell_draw(splits[0], (2, TOKENS, D), 1.0, 6.0, ((0, 2), (1, 16)))
    lengths = draw_lengths(jax.random.fold_in(splits[15], 71), 0)
    seg_group = set_ends(jax.random.randint(splits[2], (UTTS,), 0, 2), jax.random.fold_in(splits[2], 1), 0, 1).astype(jnp.int32)
    norm_gain = jnp.clip(1.0 + 0.1 * jax.random.normal(splits[3], (2, 3, D), jnp.float32), 0.5, 1.5)
    norm_shift = bell_draw(splits[4], (2, 3, D), 0.2, 1.0, ((0, 2),), jnp.float32)
    w_query = bell_draw(splits[5], (2, D, D), D ** -0.5, 0.25, ((0, 2),))
    w_key = bell_draw(splits[6], (2, D, D), D ** -0.5, 0.25, ((0, 2),))
    w_value = bell_draw(splits[7], (2, D, D), D ** -0.5, 0.25, ((0, 2),))
    qv_bias = bell_draw(splits[8], (2, 2, D), 0.3, 1.5, ((0, 2),), jnp.float32)
    w_out = bell_draw(splits[9], (2, D, D), (D // 8) ** -0.5, 0.75, ((0, 2),))
    out_bias = bell_draw(splits[10], (2, D), 0.3, 1.5, ((0, 2),), jnp.float32)
    w_up = bell_draw(splits[11], (2, D, FF), D ** -0.5, 0.25, ((0, 2),))
    up_bias = bell_draw(splits[12], (2, FF), 0.5, 2.5, ((0, 2),), jnp.float32)
    w_down = bell_draw(splits[13], (2, FF, D), FF ** -0.5, 0.125, ((0, 2),))
    down_bias = bell_draw(splits[14], (2, D), 0.3, 1.5, ((0, 2),), jnp.float32)
    return dict(ends=ends, lengths=lengths, seg_group=seg_group, norm_gain=norm_gain, norm_shift=norm_shift, w_query=w_query, w_key=w_key, w_value=w_value, qv_bias=qv_bias, w_out=w_out, out_bias=out_bias, w_up=w_up, up_bias=up_bias, w_down=w_down, down_bias=down_bias)


@jax.custom_vjp
def low(v):
    return lax.optimization_barrier(v.astype(jnp.bfloat16)).astype(jnp.float32)

@jax.custom_vjp
def low_back(v):
    return v

def low_keep(v):
    return (low(v), None)

def low_pass(kept, grad):
    return (grad,)

def back_keep(v):
    return (v, None)

def back_low(kept, grad):
    return (low(grad),)
low.defvjp(low_keep, low_pass)
low_back.defvjp(back_keep, back_low)
HIGHEST = lax.Precision.HIGHEST

def norm_rows(value, gain, shift):
    center = value - lax.optimization_barrier(jnp.mean(value, axis=-1, keepdims=True))
    spread = lax.optimization_barrier(jnp.mean(center * center, axis=-1, keepdims=True))
    return center * lax.rsqrt(spread + 1e-05) * gain + shift

def segment_means(value, length, wide):
    rows = value.shape[0] // 8
    width = value.shape[1]
    eight = lax.optimization_barrier(jnp.sum(value.reshape(rows, 8, width), axis=1))
    sixteen = lax.optimization_barrier(jnp.sum(value.reshape(rows // 2, 16, width), axis=1))
    sixteen = jnp.concatenate([sixteen, jnp.zeros((rows // 2, width), value.dtype)], axis=0)
    totals = jnp.where(wide, sixteen, eight)
    segment = jnp.where(wide, 16, 8).astype(jnp.int32)
    count = jnp.clip(length - jnp.arange(rows, dtype=jnp.int32) * segment, 0, segment)
    return totals / jnp.maximum(count, 1).astype(value.dtype)[:, None]

def block_mask(block, length, wide, slot_len):
    rows_summary = BLOCK // 8
    mem_rows = slot_len // 8
    segment = jnp.where(wide, 16, 8).astype(jnp.int32)
    frames = block * BLOCK + jnp.arange(BLOCK, dtype=jnp.int32)
    start = block * BLOCK // segment
    summary_index = start + jnp.arange(rows_summary, dtype=jnp.int32)
    query_segment = jnp.concatenate([frames // segment, summary_index])
    is_frame = jnp.arange(BLOCK + rows_summary, dtype=jnp.int32) < BLOCK
    key_frame = block * BLOCK - 64 + jnp.arange(BLOCK + 128, dtype=jnp.int32)
    lower = query_segment * segment - LEFT
    upper = query_segment * segment + segment + RIGHT
    frame_ok = (key_frame[None, :] >= lower[:, None]) & (key_frame[None, :] < upper[:, None])
    frame_ok = frame_ok & (key_frame[None, :] < length) & (key_frame[None, :] >= 0)
    memory_index = jnp.arange(mem_rows, dtype=jnp.int32)
    memory_ok = (memory_index[None, :] >= query_segment[:, None] - MEM) & (memory_index[None, :] < query_segment[:, None])
    memory_ok = memory_ok & is_frame[:, None]
    summary_ok = jnp.arange(rows_summary, dtype=jnp.int32) < BLOCK // segment
    return (jnp.concatenate([memory_ok, frame_ok], axis=1), start, summary_ok)

def attention(query_frames, query_summary, keys, values, length, wide):
    slot_len, width = query_frames.shape
    mem_rows = slot_len // 8
    scale = E ** (-0.5)
    key_memory = keys[:mem_rows]
    value_memory = values[:mem_rows]
    key_frames = jnp.pad(keys[mem_rows:], ((64, 64), (0, 0)))
    value_frames = jnp.pad(values[mem_rows:], ((64, 64), (0, 0)))
    out_frames = []
    out_summary = jnp.zeros((mem_rows, width), jnp.float32)
    for block in range(slot_len // BLOCK):
        mask, start, summary_ok = block_mask(block, length, wide, slot_len)
        query = jnp.concatenate([query_frames[block * BLOCK:(block + 1) * BLOCK], lax.dynamic_slice_in_dim(query_summary, start, BLOCK // 8, 0)], axis=0).reshape(-1, H, E)
        key = jnp.concatenate([key_memory, key_frames[block * BLOCK:block * BLOCK + BLOCK + 128]], axis=0).reshape(-1, H, E)
        value = jnp.concatenate([value_memory, value_frames[block * BLOCK:block * BLOCK + BLOCK + 128]], axis=0).reshape(-1, H, E)
        scores = low_back(jnp.einsum('rhe,khe->hrk', query, key, precision=HIGHEST) * scale)
        scores = jnp.where(mask[None], scores, -1e+30)
        chance = low(jax.nn.softmax(scores, axis=-1))
        mixed = jnp.einsum('hrk,khe->rhe', chance, value, precision=HIGHEST).reshape(-1, width)
        out_frames.append(mixed[:BLOCK])
        placed = jnp.where(summary_ok[:, None], mixed[BLOCK:], 0.0)
        out_summary = out_summary + lax.dynamic_update_slice_in_dim(jnp.zeros((mem_rows, width), jnp.float32), placed, start, 0)
    return (jnp.concatenate(out_frames, axis=0), out_summary)

def layer(params, inputs, memory, length, wide):
    gain, shift, w_query, w_key, w_value, qv_bias, w_out, out_bias, w_up, up_bias, w_down, down_bias = params
    slot_len = inputs.shape[0]
    valid = (jnp.arange(slot_len, dtype=jnp.int32) < length).astype(jnp.float32)[:, None]
    normed = low(norm_rows(inputs, gain[0], shift[0]))
    summary = low(segment_means(normed * valid, length, wide))
    query = low(low_back(jnp.dot(jnp.concatenate([normed, summary], axis=0), w_query, precision=HIGHEST) + qv_bias[0]))
    sources = jnp.concatenate([memory, normed], axis=0)
    keys = low(low_back(jnp.dot(sources, w_key, precision=HIGHEST)))
    values = low(low_back(jnp.dot(sources, w_value, precision=HIGHEST) + qv_bias[1]))
    mixed_frames, mixed_summary = attention(query[:slot_len], query[slot_len:], keys, values, length, wide)
    mixed = low(low_back(jnp.concatenate([mixed_frames, mixed_summary], axis=0)))
    branch = low_back(jnp.dot(mixed, w_out, precision=HIGHEST) + out_bias)
    after = inputs + branch[:slot_len]
    memory_out = low(branch[slot_len:])
    hidden_in = low(norm_rows(after, gain[1], shift[1]))
    hidden = low_back(jnp.dot(hidden_in, w_up, precision=HIGHEST) + up_bias)
    active = low(jax.nn.gelu(hidden, approximate=False))
    update = low_back(jnp.dot(active, w_down, precision=HIGHEST) + down_bias)
    return (norm_rows(after + update, gain[2], shift[2]) * valid, memory_out)

def layer_pair(params, first_in, length, wide):
    lower_params = tuple((item[0] for item in params))
    upper_params = tuple((item[1] for item in params))
    valid = (jnp.arange(first_in.shape[0], dtype=jnp.int32) < length).astype(jnp.float32)[:, None]
    memory = low(segment_means(first_in * valid, length, wide))
    middle, middle_memory = layer(lower_params, first_in, memory, length, wide)
    final, spare = layer(upper_params, low(low_back(middle)), middle_memory, length, wide)
    return final

def reference(ends, lengths, seg_group, norm_gain, norm_shift, w_query, w_key, w_value, qv_bias, w_out, out_bias, w_up, up_bias, w_down, down_bias):
    params = tuple((item.astype(jnp.float32) for item in (norm_gain, norm_shift, w_query, w_key, w_value, qv_bias, w_out, out_bias, w_up, up_bias, w_down, down_bias)))
    width = ends.shape[2]
    inputs = ends[0].astype(jnp.float32).reshape(UTTS, SLOT, width)
    cotangent = ends[1].astype(jnp.float32).reshape(UTTS, SLOT, width)

    def visit(totals, item):
        first_in, cot_in, length, group = item
        wide = group == 1
        final, back = jax.vjp(lambda weights_in, frames_in: layer_pair(weights_in, frames_in, length, wide), params, first_in)
        grad_params, grad_in = back(cot_in)
        totals = tuple((total + grad for total, grad in zip(totals, grad_params)))
        return (totals, (final.astype(jnp.bfloat16), grad_in.astype(jnp.bfloat16)))
    start_totals = tuple((jnp.zeros_like(item) for item in params))
    totals, outputs = lax.scan(visit, start_totals, (inputs, cotangent, lengths, seg_group))
    finals, grads_in = outputs
    ends_out = jnp.stack([grads_in.reshape(TOKENS, width), finals.reshape(TOKENS, width)])
    return (ends_out, totals[0], totals[1], totals[2], totals[3], totals[4], totals[5], totals[6], totals[7], totals[8], totals[9], totals[10], totals[11])
```

```python
import functools
import jax
import jax.numpy as jnp
from jax import lax
from jax.experimental import pallas as pl
from jax.experimental.pallas import tpu as pltpu
from jax.sharding import PartitionSpec as P

LEFT = 30
RIGHT = 4
MEM = 4
TILE = 64
KEYS = 128
ROWS = 80
FRONT = 32
BF = jnp.bfloat16
F32 = jnp.float32
VMEM_LIMIT = 56 * 1024 * 1024


def dot(a, b):
    return lax.dot_general(a, b, (((1,), (0,)), ((), ())), preferred_element_type=F32)


def dot_nt(a, b):
    return lax.dot_general(a, b, (((1,), (1,)), ((), ())), preferred_element_type=F32)


def dot_tn(a, b):
    return lax.dot_general(a, b, (((0,), (0,)), ((), ())), preferred_element_type=F32)


def normed(value):
    center = value - jnp.mean(value, axis=-1, keepdims=True)
    rs = lax.rsqrt(jnp.mean(center * center, axis=-1, keepdims=True) + 1e-05)
    return center * rs, rs


def norm_back(w, xhat, rs):
    return (w - jnp.mean(w, axis=-1, keepdims=True) - xhat * jnp.mean(w * xhat, axis=-1, keepdims=True)) * rs


def fold8(value):
    rows, width = value.shape
    return jnp.sum(value.reshape(rows // 8, 8, width), axis=0)


def gelu_parts(f):
    half = jnp.exp(f * f * -0.5)
    t = 1.0 / (1.0 + jnp.abs(f) * (0.3275911 * 0.7071067811865476))
    poly = t * (0.5 * 0.254829592 + t * (0.5 * -0.284496736 + t * (0.5 * 1.421413741 + t * (0.5 * -1.453152027 + t * (0.5 * 1.061405429)))))
    tail = poly * half
    phi = jnp.where(f >= 0, 1.0 - tail, tail)
    return f * phi, phi + f * half * 0.3989422804014327


def seg_sizes(wide):
    return jnp.where(wide, 16, 8).astype(jnp.int32), jnp.where(wide, 4, 8).astype(jnp.int32)


def pool_matrix(length, wide, slot):
    seg, per = seg_sizes(wide)
    rows = slot // 8
    e = lax.broadcasted_iota(jnp.int32, (rows, slot), 0)
    t = lax.broadcasted_iota(jnp.int32, (rows, slot), 1)
    r = jnp.bitwise_and(e, 7)
    start = jnp.right_shift(e, 3) * TILE + r * seg
    inside = (t >= start) & (t < start + seg) & (t < length) & (r < per)
    e1 = lax.broadcasted_iota(jnp.int32, (rows, 1), 0)
    r1 = jnp.bitwise_and(e1, 7)
    start1 = jnp.right_shift(e1, 3) * TILE + r1 * seg
    count = jnp.where(r1 < per, jnp.clip(length - start1, 0, seg), 0)
    inverse = 1.0 / jnp.maximum(count, 1).astype(F32)
    return jnp.where(inside, 1.0, 0.0).astype(BF), inverse


def unpool(matrix, value):
    high = value.astype(BF)
    low = (value - high.astype(F32)).astype(BF)
    return dot_tn(jnp.concatenate([matrix, matrix], axis=0), jnp.concatenate([high, low], axis=0))


def tile_bias(tile, odd, length, wide):
    seg, per = seg_sizes(wide)
    row = lax.broadcasted_iota(jnp.int32, (ROWS, 1), 0)
    col = lax.broadcasted_iota(jnp.int32, (1, KEYS), 1)
    anchor = tile * TILE
    is_frame = row < TILE
    extra = row - TILE
    shift = jnp.where(wide, 4, 3).astype(jnp.int32)
    r = jnp.where(is_frame, jnp.right_shift(row, shift), jnp.bitwise_and(extra, 7))
    owned = is_frame | ((jnp.right_shift(extra, 3) == odd) & (r < per))
    key = col - (16 + FRONT)
    low = jnp.where(owned, r * seg - LEFT, 100000)
    high = jnp.minimum(r * seg + seg + RIGHT, length - anchor)
    frame_ok = (key >= jnp.maximum(low, -anchor)) & (key < high) & (col >= 16)
    c = jnp.bitwise_and(col, 7)
    slot = jnp.where((col < 16) & (c < per), jnp.where(col < 8, c - per, c), -100000)
    slot = jnp.where((col < 8) & (anchor == 0), -100000, slot)
    mem_ok = (slot >= r - MEM) & (slot < jnp.where(is_frame, r, -100000))
    return jnp.where(frame_ok | mem_ok, 0.0, -1e30).astype(F32)


def head_masks(rows):
    lane = jnp.right_shift(lax.broadcasted_iota(jnp.int32, (rows, 256), 1), 6)
    return [lane == h for h in range(4)]


def spread_heads(tile, masks):
    zero = jnp.zeros_like(tile)
    return jnp.concatenate([jnp.where(m, tile, zero) for m in masks], axis=0)


def gather_heads(stack, masks):
    total = jnp.where(masks[0], stack[:ROWS], 0.0)
    for h in range(1, 4):
        total = jnp.where(masks[h], stack[h * ROWS : (h + 1) * ROWS], total)
    return total


def key_window(pair, odd, lanes, frames_ref, even_ref, pad_ref):
    first = pl.multiple_of(pair * 16, 16)
    memory = even_ref[pl.ds(first, 16), lanes] if odd else pad_ref[pl.ds(first, 16), lanes]
    start = pl.multiple_of(pair * 128 + odd * 64, 64)
    return jnp.concatenate([memory, frames_ref[pl.ds(start, KEYS - 16), lanes]], axis=0)


def fill_windows(all_rows, frames_ref, even_ref, pad_ref, mem_rows, slot):
    width = all_rows.shape[1]
    memory = all_rows[:mem_rows].astype(F32)
    blank = jnp.zeros((8, width), F32)
    even_ref[...] = memory.astype(BF)
    pad_ref[...] = jnp.concatenate([blank, memory, blank], axis=0).astype(BF)
    frames_ref[:FRONT] = jnp.zeros((FRONT, width), BF)
    frames_ref[FRONT : FRONT + slot] = all_rows[mem_rows:].astype(BF)
    frames_ref[FRONT + slot :] = jnp.zeros((16, width), BF)


def attention_in(utt, lower, slot, pos_ref, len_ref, grp_ref, x_ref, mem_ref, gain, shift, wq, wk, wv, qvb, wo, ob,
                 *refs):
    (uc, mem, q, k, v, prob, mix, xh0, xh1, h, rs, after, memnext, kf, ke, kp, vf, ve, vp) = refs[-19:]
    mem_rows = slot // 8
    length = len_ref[utt]
    wide = grp_ref[utt] == 1
    g0, s0 = gain[0:1], shift[0:1]
    lane = lax.broadcasted_iota(jnp.int32, (1, 128), 1)

    def rows_in(i, carry):
        r = pl.ds(pl.multiple_of(i * 32, 32), 32)
        xhat, scale = normed(x_ref[r].astype(F32))
        xh0[0, r] = xhat.astype(BF)
        uc[0, r] = (xhat * g0 + s0).astype(BF)
        rs[0, r] = jnp.broadcast_to(scale, (32, 128))
        return carry

    lax.fori_loop(0, slot // 32, rows_in, 0, unroll=2)
    pm, inverse = pool_matrix(length, wide, slot)
    uc[0, slot:] = (dot(pm, uc[0, :slot]) * inverse).astype(BF)
    if lower:
        mem[0] = (dot(pm, x_ref[...]) * inverse).astype(BF)
    else:
        mem[0] = mem_ref[...]
    q[0] = (dot(uc[0], wq[...]) + qvb[0:1]).astype(BF)
    k[0, :mem_rows] = dot(mem[0], wk[...]).astype(BF)
    k[0, mem_rows:] = dot(uc[0, :slot], wk[...]).astype(BF)
    v[0, :mem_rows] = (dot(mem[0], wv[...]) + qvb[1:2]).astype(BF)
    v[0, mem_rows:] = (dot(uc[0, :slot], wv[...]) + qvb[1:2]).astype(BF)
    fill_windows(k[0], kf, ke, kp, mem_rows, slot)
    fill_windows(v[0], vf, ve, vp, mem_rows, slot)
    masks = head_masks(ROWS)

    def pair_step(pair, carry):
        for quad in range(2):
            lanes = slice(quad * 256, quad * 256 + 256)
            extra = None
            for odd in range(2):
                rows = pl.ds(pl.multiple_of(pair * 128 + odd * 64, 64), 64)
                srows = pl.ds(pl.multiple_of(slot + pair * 16, 16), 16)
                bias = tile_bias(pair * 2 + odd, odd, length, wide)
                qs = spread_heads(jnp.concatenate([q[0, rows, lanes], q[0, srows, lanes]], axis=0), masks)
                kw = key_window(pair, odd, lanes, kf, ke, kp)
                vw = key_window(pair, odd, lanes, vf, ve, vp)
                s = dot_nt(qs, kw).reshape(4, ROWS, KEYS) * 0.125 + bias[None]
                peak = jnp.maximum(jnp.max(s, axis=-1, keepdims=True), -1e29)
                e = jnp.exp(s - peak)
                total = jnp.sum(e, axis=-1, keepdims=True)
                p = (e * (1.0 / jnp.maximum(total, 1e-30))).astype(BF).reshape(4 * ROWS, KEYS)
                prob[0, pair * 4 + quad * 2 + odd] = p
                o = gather_heads(dot(p, vw), masks)
                mix[0, rows, lanes] = o[:TILE].astype(BF)
                extra = o[TILE:] if extra is None else extra + o[TILE:]
            mix[0, srows, lanes] = extra.astype(BF)
        return carry

    lax.fori_loop(0, slot // 128, pair_step, 0)
    z = dot(mix[0], wo[...]) + ob[...]
    memnext[...] = z[slot:].astype(BF)
    after[...] = z[:slot]
    g1, s1 = gain[1:2], shift[1:2]

    def rows_out(i, carry):
        r = pl.ds(pl.multiple_of(i * 32, 32), 32)
        a = x_ref[r].astype(F32) + after[r]
        after[r] = a
        xhat, scale = normed(a)
        xh1[0, r] = xhat.astype(BF)
        h[0, r] = (xhat * g1 + s1).astype(BF)
        rs[0, r] = jnp.where(lane == 0, rs[0, r], jnp.broadcast_to(scale, (32, 128)))
        return carry

    lax.fori_loop(0, slot // 32, rows_out, 0, unroll=2)


def ffn_in(utt, block, pos_ref, len_ref, h, after, gain, shift, wu, ub, wd, db, *refs):
    g, gp, xh2, rs2, y = refs[-5:]
    width = after.shape[1]
    total = after[...] + db[...]
    hid = h[0]
    for c in range(wu.shape[1] // 512):
        cols = slice(c * 512, c * 512 + 512)
        act, slope = gelu_parts(dot(hid, wu[:, cols]) + ub[:, cols])
        act = act.astype(BF)
        g[0, :, cols] = act
        gp[0, :, cols] = slope.astype(BF)
        total = total + dot(act, wd[cols])
    xhat, scale = normed(total)
    xh2[0] = xhat.astype(BF)
    rs2[0] = jnp.broadcast_to(scale, (block, 128))
    t = lax.broadcasted_iota(jnp.int32, (block, 1), 0) + pl.program_id(0) * block
    valid = jnp.where(t < len_ref[utt], 1.0, 0.0)
    y[...] = ((xhat * gain[2:3] + shift[2:3]) * valid).astype(BF)


def ffn_back(utt, block, pos_ref, len_ref, cot, xh2, rs2, gp, xh1, rs, gain, wu, wd, *refs):
    gd, gf, gz, ga, small, acc = refs[-6:]
    step = pl.program_id(0)
    t = lax.broadcasted_iota(jnp.int32, (block, 1), 0) + step * block
    valid = jnp.where(t < len_ref[utt], 1.0, 0.0)

    @pl.when(step == 0)
    def _():
        acc[...] = jnp.zeros_like(acc)

    gv = cot[...].astype(F32) * valid
    xhat = xh2[0].astype(F32)
    acc[0] += fold8(gv * xhat)
    acc[1] += fold8(gv)
    ga2 = norm_back(gv * gain[2:3], xhat, rs2[0, :, 0:1])
    gdl = ga2.astype(BF)
    gd[0] = gdl
    acc[2] += fold8(gdl.astype(F32))
    back = None
    for c in range(wu.shape[1] // 512):
        cols = slice(c * 512, c * 512 + 512)
        gfl = (dot_nt(gdl, wd[cols]) * gp[0, :, cols].astype(F32)).astype(BF)
        gf[0, :, cols] = gfl
        acc[6 + c] += fold8(gfl.astype(F32))
        part = dot_nt(gfl, wu[:, cols])
        back = part if back is None else back + part
    xhat = xh1[0].astype(F32)
    acc[3] += fold8(back * xhat)
    acc[4] += fold8(back)
    total = ga2 + norm_back(back * gain[1:2], xhat, rs[0, :, 1:2])
    ga[...] = total
    gzl = total.astype(BF)
    gz[0] = gzl
    acc[5] += fold8(gzl.astype(F32))

    @pl.when(step == pl.num_programs(0) - 1)
    def _():
        small[...] = jnp.sum(acc[...], axis=1)


def attention_back(utt, lower, slot, pos_ref, len_ref, grp_ref, gz, gmem, ga, q, k, v, prob, xh0, rs, gain,
                   wq, wk, wv, wo, *refs):
    (gq, gk, gv, gzs, gx, gm, small, kf, ke, kp, vf, ve, vp, gof, gos, akf, akm, avf, avm, gu, acc) = refs[-21:]
    mem_rows = slot // 8
    width = gu.shape[1]
    length = len_ref[utt]
    wide = grp_ref[utt] == 1
    fill_windows(k[0], kf, ke, kp, mem_rows, slot)
    fill_windows(v[0], vf, ve, vp, mem_rows, slot)
    gof[...] = dot_nt(gz[0], wo[...]).astype(BF)
    if lower:
        gzs[0] = gmem[...]
        gos[...] = dot_nt(gmem[...], wo[...]).astype(BF)
    else:
        gzs[0] = jnp.zeros_like(gzs[0])
        gos[...] = jnp.zeros_like(gos)
    for ref in (akf, akm, avf, avm):
        ref[...] = jnp.zeros_like(ref)
    masks = head_masks(ROWS)

    def pair_step(pair, carry):
        for quad in range(2):
            lanes = slice(quad * 256, quad * 256 + 256)
            extra = None
            srows = pl.ds(pl.multiple_of(slot + pair * 16, 16), 16)
            for odd in range(2):
                rows = pl.ds(pl.multiple_of(pair * 128 + odd * 64, 64), 64)
                qs = spread_heads(jnp.concatenate([q[0, rows, lanes], q[0, srows, lanes]], axis=0), masks)
                gos_rows = gos[pl.ds(pl.multiple_of(pair * 16, 16), 16), lanes]
                go = spread_heads(jnp.concatenate([gof[rows, lanes], gos_rows], axis=0), masks)
                kw = key_window(pair, odd, lanes, kf, ke, kp)
                vw = key_window(pair, odd, lanes, vf, ve, vp)
                p = prob[0, pair * 4 + quad * 2 + odd]
                gprob = dot_nt(go, vw) * p.astype(F32)
                gs = (gprob - p.astype(F32) * jnp.sum(gprob, axis=-1, keepdims=True)).astype(BF)
                gqt = gather_heads(dot(gs, kw), masks) * 0.125
                gkt = dot_tn(gs, qs) * 0.125
                gvt = dot_tn(p, go)
                gq[0, rows, lanes] = gqt[:TILE].astype(BF)
                extra = gqt[TILE:] if extra is None else extra + gqt[TILE:]
                mrows = pl.ds(pl.multiple_of(pair * 16 + odd * 8, 8), 16)
                frows = pl.ds(pl.multiple_of(pair * 128 + odd * 64, 64), KEYS - 16)
                akm[mrows, lanes] += gkt[:16]
                akf[frows, lanes] += gkt[16:]
                avm[mrows, lanes] += gvt[:16]
                avf[frows, lanes] += gvt[16:]
            gq[0, srows, lanes] = extra.astype(BF)
        return carry

    lax.fori_loop(0, slot // 128, pair_step, 0)
    for out, am, af in ((gk, akm, akf), (gv, avm, avf)):
        out[0, :mem_rows] = am[8 : 8 + mem_rows].astype(BF)
        out[0, mem_rows:] = af[FRONT : FRONT + slot].astype(BF)
    pm, inverse = pool_matrix(length, wide, slot)
    gmf = dot_nt(gk[0, :mem_rows], wk[...]) + dot_nt(gv[0, :mem_rows], wv[...])
    gm[...] = gmf.astype(BF)
    gc = dot_nt(gq[0, slot:], wq[...]) * inverse
    gu[...] = (dot_nt(gk[0, mem_rows:], wk[...]) + dot_nt(gv[0, mem_rows:], wv[...])
               + dot_nt(gq[0, :slot], wq[...]) + unpool(pm, gc))
    acc[...] = jnp.zeros_like(acc)
    if lower:
        akf[:slot] = unpool(pm, gmf * inverse)
    g0 = gain[0:1]

    def rows_out(i, carry):
        r = pl.ds(pl.multiple_of(i * 32, 32), 32)
        w = gu[r]
        xhat = xh0[0, r].astype(F32)
        acc[0] += fold8(w * xhat)
        acc[1] += fold8(w)
        total = ga[r] + norm_back(w * g0, xhat, rs[0, r, 0:1])
        if lower:
            total = total + akf[r]
        gx[r] = total.astype(BF)
        return carry

    lax.fori_loop(0, slot // 32, rows_out, 0, unroll=2)
    acc[2] = fold8(gq[0].astype(F32))
    acc[3] = fold8(gv[0].astype(F32))
    acc[4] = fold8(gzs[0].astype(F32))
    small[...] = jnp.sum(acc[...], axis=1)


def full(shape):
    return pl.BlockSpec(shape, lambda *_: (0,) * len(shape))


def slotted(shape):
    return pl.BlockSpec((1,) + shape, lambda i, pos, *_: (pos[0],) + (0,) * len(shape))


def slotted_rows(shape):
    return pl.BlockSpec((1,) + shape, lambda i, pos, *_: (pos[0], i) + (0,) * (len(shape) - 1))


def rows_of(shape):
    return pl.BlockSpec(shape, lambda i, *_: (i,) + (0,) * (len(shape) - 1))


def sds(shape, dtype):
    return jax.ShapeDtypeStruct(shape, dtype)


def run(body, grid, scalars, inputs, kept, outs, scratch, cost):
    extra = list(kept) if kept is not None else []
    aliases = {len(scalars) + len(inputs) + i: i for i in range(len(extra))}
    return pl.pallas_call(
        body,
        grid_spec=pltpu.PrefetchScalarGridSpec(
            num_scalar_prefetch=len(scalars),
            grid=grid,
            in_specs=[spec for _, spec in inputs] + [pl.BlockSpec(memory_space=pl.ANY)] * len(extra),
            out_specs=[spec for _, spec in outs],
            scratch_shapes=scratch,
        ),
        out_shape=[shape for shape, _ in outs],
        input_output_aliases=aliases,
        compiler_params=pltpu.CompilerParams(vmem_limit_bytes=VMEM_LIMIT, dimension_semantics=("arbitrary",)),
        cost_estimate=cost,
    )(*scalars, *[a for a, _ in inputs], *extra)


def cost_of(flops, moved, special=0):
    return pl.CostEstimate(flops=int(flops), bytes_accessed=int(moved), transcendentals=int(special))


def window_scratch(slot, width):
    mem_rows = slot // 8
    one = [
        pltpu.VMEM((FRONT + slot + 16, width), BF),
        pltpu.VMEM((mem_rows, width), BF),
        pltpu.VMEM((mem_rows + 16, width), BF),
    ]
    return one + one


ROOMS = 3


def forward(weights, utt, lower, scalars, frames, memory, kept):
    (gain, shift, wq, wk, wv, qvb, wo, ob, wu, ub, wd, db) = weights
    slot, width = frames.shape
    hid = wu.shape[1]
    mem_rows = slot // 8
    every = slot + mem_rows
    pairs = slot // 128
    kept_a, kept_f = kept if kept is not None else (None, None)
    low = lambda *s: sds((ROOMS,) + s, BF)
    outs = [(low(*s), slotted(s)) for s in (
        (every, width), (mem_rows, width), (every, width), (every, width), (every, width),
        (pairs * 4, 4 * ROWS, KEYS), (every, width), (slot, width), (slot, width), (slot, width))]
    outs.append((sds((ROOMS, slot, 128), F32), slotted((slot, 128))))
    n_kept = len(outs)
    outs.append((sds((slot, width), F32), full((slot, width))))
    outs.append((sds((mem_rows, width), BF), full((mem_rows, width))))
    ins = [(a, full(a.shape)) for a in (frames, memory, gain, shift, wq, wk, wv, qvb, wo, ob)]
    res = run(
        functools.partial(attention_in, utt, lower, slot), (1,), scalars, ins, kept_a, outs,
        window_scratch(slot, width), cost_of(8 * every * width * width, 12 * every * width * 2, 8 * slot * 128))
    kept_a, (after, memnext) = res[:n_kept], res[n_kept:]
    h = kept_a[9]
    block = slot // 2
    ins = [(h, slotted_rows((block, width))), (after, rows_of((block, width)))]
    ins += [(a, full(a.shape)) for a in (gain, shift, wu, ub, wd, db)]
    outs = [(low(slot, hid), slotted_rows((block, hid))), (low(slot, hid), slotted_rows((block, hid))),
            (low(slot, width), slotted_rows((block, width))),
            (sds((ROOMS, slot, 128), F32), slotted_rows((block, 128))),
            (sds((slot, width), BF), rows_of((block, width)))]
    res = run(functools.partial(ffn_in, utt, block), (slot // block,), scalars[:2], ins, kept_f, outs, [],
              cost_of(4 * slot * width * hid, 4 * slot * hid + 4 * width * hid, slot * hid * 2))
    return res[4], memnext, (kept_a, res[:4])


def backward_ffn(weights, utt, scalars, cot, kept, grads):
    (gain, shift, wq, wk, wv, qvb, wo, ob, wu, ub, wd, db) = weights
    slot, width = cot.shape
    hid = wu.shape[1]
    block = slot // 2
    kept_a, kept_f = kept
    ins = [(cot, rows_of((block, width))), (kept_f[2], slotted_rows((block, width))),
           (kept_f[3], slotted_rows((block, 128))), (kept_f[1], slotted_rows((block, hid))),
           (kept_a[8], slotted_rows((block, width))), (kept_a[10], slotted_rows((block, 128)))]
    ins += [(a, full(a.shape)) for a in (gain, wu, wd)]
    low = lambda *s: sds((ROOMS,) + s, BF)
    outs = [(low(slot, width), slotted_rows((block, width))), (low(slot, hid), slotted_rows((block, hid))),
            (low(slot, width), slotted_rows((block, width))), (sds((slot, width), F32), rows_of((block, width))),
            (sds((16, width), F32), full((16, width)))]
    res = run(functools.partial(ffn_back, utt, block), (slot // block,), scalars[:2], ins, grads, outs,
              [pltpu.VMEM((16, 8, width), F32)],
              cost_of(4 * slot * width * hid, 4 * slot * hid + 4 * width * hid))
    return res[:3], res[3], res[4]


def backward_attention(weights, utt, lower, scalars, gz, gmem, ga, kept, grads):
    (gain, shift, wq, wk, wv, qvb, wo, ob, wu, ub, wd, db) = weights
    slot, width = ga.shape
    mem_rows = slot // 8
    every = slot + mem_rows
    (uc, mem, q, k, v, prob, mix, xh0, xh1, h, rs), _ = kept
    ins = [(gz, slotted((slot, width))), (gmem, full(gmem.shape)), (ga, full(ga.shape))]
    ins += [(a, slotted(a.shape[1:])) for a in (q, k, v, prob, xh0, rs)]
    ins += [(a, full(a.shape)) for a in (gain, wq, wk, wv, wo)]
    low = lambda *s: sds((ROOMS,) + s, BF)
    outs = [(low(*s), slotted(s)) for s in ((every, width),) * 3 + ((mem_rows, width),)]
    outs += [(sds((slot, width), BF), full((slot, width))), (sds((mem_rows, width), BF), full((mem_rows, width))),
             (sds((16, width), F32), full((16, width)))]
    scratch = window_scratch(slot, width) + [
        pltpu.VMEM((slot, width), BF), pltpu.VMEM((mem_rows, width), BF),
        pltpu.VMEM((FRONT + slot + 16, width), F32), pltpu.VMEM((mem_rows + 16, width), F32),
        pltpu.VMEM((FRONT + slot + 16, width), F32), pltpu.VMEM((mem_rows + 16, width), F32),
        pltpu.VMEM((slot, width), F32), pltpu.VMEM((16, 8, width), F32)]
    res = run(functools.partial(attention_back, utt, lower, slot), (1,), scalars, ins, grads, outs, scratch,
              cost_of(8 * every * width * width, 12 * every * width * 2))
    return res[:4], res[4], res[5], res[6]


def ffn_weights(g, gd, h, gf, out):
    step = pl.program_id(0)
    half = pl.num_programs(0) // 2

    @pl.when(step < half)
    def _():
        out[0] = sum(dot_tn(g[u], gd[u]) for u in range(g.shape[0])).astype(out.dtype)

    @pl.when(step >= half)
    def _():
        out[0] = sum(dot_tn(h[u], gf[u]) for u in range(h.shape[0])).astype(out.dtype)


def weight_grads_ffn(slots, g, gd, h, gf):
    _, slot, hid = g.shape
    width = gd.shape[2]
    blocks = hid // width
    spec = lambda index: pl.BlockSpec((slots, slot, width), index)
    return pl.pallas_call(
        ffn_weights,
        grid=(2 * blocks,),
        in_specs=[spec(lambda j: (0, 0, jnp.minimum(j, blocks - 1))), spec(lambda j: (0, 0, 0)),
                  spec(lambda j: (0, 0, 0)), spec(lambda j: (0, 0, jnp.maximum(j - blocks, 0)))],
        out_specs=pl.BlockSpec((1, width, width), lambda j: (j, 0, 0)),
        out_shape=sds((2 * blocks, width, width), BF),
        compiler_params=pltpu.CompilerParams(vmem_limit_bytes=VMEM_LIMIT, dimension_semantics=("arbitrary",)),
        cost_estimate=cost_of(4 * slots * slot * hid * width, 4 * slots * slot * hid + 4 * hid * width),
    )(g, gd, h, gf)


def attention_weights(uc, mem, mix, gq, gk, gv, gz, gzs, out):
    step = pl.program_id(0)
    slots, every, width = uc.shape
    slot = gz.shape[1]
    mem_rows = every - slot

    @pl.when(step == 0)
    def _():
        out[0] = sum(dot_tn(uc[u], gq[u]) for u in range(slots)).astype(out.dtype)

    for place, ref in ((1, gk), (2, gv)):
        @pl.when(step == place)
        def _():
            out[0] = sum(dot_tn(mem[u], ref[u, :mem_rows]) + dot_tn(uc[u, :slot], ref[u, mem_rows:])
                         for u in range(slots)).astype(out.dtype)

    @pl.when(step == 3)
    def _():
        out[0] = sum(dot_tn(mix[u, :slot], gz[u]) + dot_tn(mix[u, slot:], gzs[u])
                     for u in range(slots)).astype(out.dtype)


def weight_grads_attention(slots, *arrays):
    _, every, width = arrays[0].shape
    return pl.pallas_call(
        attention_weights,
        grid=(4,),
        in_specs=[pl.BlockSpec((slots,) + a.shape[1:], lambda j: (0, 0, 0)) for a in arrays],
        out_specs=pl.BlockSpec((1, width, width), lambda j: (j, 0, 0)),
        out_shape=sds((4, width, width), BF),
        compiler_params=pltpu.CompilerParams(vmem_limit_bytes=VMEM_LIMIT, dimension_semantics=("arbitrary",)),
        cost_estimate=cost_of(8 * slots * every * width * width, 16 * slots * every * width),
    )(*arrays)


def shifted(block, axis, distance):
    devices = range(lax.axis_size(axis))
    route = [(i - distance, i) for i in devices if i - distance in devices]
    return lax.ppermute(block, axis, route)


def on_device(ends, lengths, seg_group, norm_gain, norm_shift, w_query, w_key, w_value, qv_bias, w_out, out_bias,
              w_up, up_bias, w_down, down_bias):
    weights = (norm_gain[0], norm_shift[0], w_query[0], w_key[0], w_value[0], qv_bias[0], w_out[0], out_bias,
               w_up[0], up_bias, w_down[0], down_bias)
    section = lax.axis_index("section")
    first = section == 0
    slots = lengths.shape[0]
    width = ends.shape[2]
    slot = ends.shape[1] // slots
    mem_rows = slot // 8
    hid = w_up.shape[2]
    local = ends[0].reshape(slots, slot, width)
    lower = [(jnp.where(first, b, ROOMS - 1).astype(jnp.int32).reshape(1), lengths, seg_group) for b in range(slots)]
    upper = [(jnp.where(first, ROOMS - 1, b).astype(jnp.int32).reshape(1), lengths, seg_group) for b in range(slots)]
    blank = jnp.zeros((mem_rows, width), BF)

    kept = None
    sent = []
    for b in range(slots):
        y, memory, kept = forward(weights, b, True, lower[b], local[b], blank, kept)
        sent.append(shifted((y, memory), "section", 1))
    finals = []
    for b in range(slots):
        y, _, kept = forward(weights, b, False, upper[b], sent[b][0], sent[b][1], kept)
        finals.append(y)

    kept_a, kept_f = kept
    grads_f = grads_a = None
    smalls = [[], []]
    sent = []
    for b in range(slots):
        grads_f, ga, small_f = backward_ffn(weights, b, upper[b], local[b], kept, grads_f)
        grads_a, gx, gm, small_a = backward_attention(weights, b, False, upper[b], grads_f[2], blank, ga, kept, grads_a)
        smalls[1].append((small_f, small_a))
        sent.append(shifted((gx, gm), "section", -1))
    inputs_back = []
    held = []
    for b in range(slots):
        grads_f, ga, small_f = backward_ffn(weights, b, lower[b], sent[b][0], kept, grads_f)
        if b == slots - 1:
            wide_sums = weight_grads_ffn(slots, kept_f[0], grads_f[0], kept_a[9], grads_f[1])
            wide_sums = lax.psum(wide_sums, "dp")
        grads_a, gx, gm, small_a = backward_attention(weights, b, True, lower[b], grads_f[2], sent[b][1], ga, kept, grads_a)
        smalls[0].append((small_f, small_a))
        inputs_back.append(gx)
    square = weight_grads_attention(slots, kept_a[0], kept_a[1], kept_a[6], grads_a[0], grads_a[1], grads_a[2],
                                    grads_f[2], grads_a[3])
    square = lax.psum(square, "dp")

    def total(side, part):
        return sum(smalls[side][b][part] for b in range(slots))

    small_f = jnp.where(first, total(0, 0), total(1, 0))
    small_a = jnp.where(first, total(0, 1), total(1, 1))
    small = jnp.concatenate([
        jnp.stack([small_a[0], small_f[3], small_f[0], small_a[1], small_f[4], small_f[1], small_a[2], small_a[3],
                   small_f[5] + small_a[4], small_f[2]]), small_f[6 : 6 + hid // width]], axis=0)
    small = lax.psum(small, "dp")
    ends_out = jnp.where(first, jnp.stack(inputs_back), jnp.stack(finals)).reshape(1, slots * slot, width)
    blocks = hid // width
    down = wide_sums[:blocks].astype(F32).reshape(1, hid, width)
    up = jnp.transpose(wide_sums[blocks:].astype(F32), (1, 0, 2)).reshape(1, width, hid)
    square = square.astype(F32)
    return (ends_out, small[None, 0:3], small[None, 3:6], square[0:1], square[1:2], square[2:3], small[None, 6:8],
            square[3:4], small[8:9], up, small[10:].reshape(1, hid), down, small[9:10])


def solution(mesh):
    placed = (
        P("section", "dp", None), P("dp"), P("dp"),
        P("section", None, None), P("section", None, None), P("section", None, None), P("section", None, None),
        P("section", None, None), P("section", None, None), P("section", None, None), P("section", None),
        P("section", None, None), P("section", None), P("section", None, None), P("section", None),
    )
    return jax.shard_map(
        on_device,
        mesh=mesh,
        in_specs=placed,
        out_specs=(
            P("section", "dp", None), P("section", None, None), P("section", None, None), P("section", None, None),
            P("section", None, None), P("section", None, None), P("section", None, None), P("section", None, None),
            P("section", None), P("section", None, None), P("section", None), P("section", None, None),
            P("section", None),
        ),
        check_vma=False,
    )
```

```python
import functools
import jax
import jax.numpy as jnp
from jax import lax
from jax.experimental import pallas as pl
from jax.experimental.pallas import tpu as pltpu
from jax.sharding import PartitionSpec as P

LEFT = 30
RIGHT = 4
MEM = 4
TILE = 64
KEYS = 128
ROWS = 80
FRONT = 32
BF = jnp.bfloat16
F32 = jnp.float32
VMEM_LIMIT = 56 * 1024 * 1024


def dot(a, b):
    return lax.dot_general(a, b, (((1,), (0,)), ((), ())), preferred_element_type=F32)


def dot_nt(a, b):
    return lax.dot_general(a, b, (((1,), (1,)), ((), ())), preferred_element_type=F32)


def dot_tn(a, b):
    return lax.dot_general(a, b, (((0,), (0,)), ((), ())), preferred_element_type=F32)


def normed(value):
    center = value - jnp.mean(value, axis=-1, keepdims=True)
    rs = lax.rsqrt(jnp.mean(center * center, axis=-1, keepdims=True) + 1e-05)
    return center * rs, rs


def norm_back(w, xhat, rs):
    return (w - jnp.mean(w, axis=-1, keepdims=True) - xhat * jnp.mean(w * xhat, axis=-1, keepdims=True)) * rs


def fold8(value):
    rows, width = value.shape
    return jnp.sum(value.reshape(rows // 8, 8, width), axis=0)


def gelu_parts(f):
    half = jnp.exp(f * f * -0.5)
    t = 1.0 / (1.0 + jnp.abs(f) * (0.3275911 * 0.7071067811865476))
    poly = t * (0.5 * 0.254829592 + t * (0.5 * -0.284496736 + t * (0.5 * 1.421413741 + t * (0.5 * -1.453152027 + t * (0.5 * 1.061405429)))))
    tail = poly * half
    phi = jnp.where(f >= 0, 1.0 - tail, tail)
    return f * phi, phi + f * half * 0.3989422804014327


def seg_sizes(wide):
    return jnp.where(wide, 16, 8).astype(jnp.int32), jnp.where(wide, 4, 8).astype(jnp.int32)


def pool_matrix(length, wide, slot):
    seg, per = seg_sizes(wide)
    rows = slot // 8
    e = lax.broadcasted_iota(jnp.int32, (rows, slot), 0)
    t = lax.broadcasted_iota(jnp.int32, (rows, slot), 1)
    r = jnp.bitwise_and(e, 7)
    start = jnp.right_shift(e, 3) * TILE + r * seg
    inside = (t >= start) & (t < start + seg) & (t < length) & (r < per)
    e1 = lax.broadcasted_iota(jnp.int32, (rows, 1), 0)
    r1 = jnp.bitwise_and(e1, 7)
    start1 = jnp.right_shift(e1, 3) * TILE + r1 * seg
    count = jnp.where(r1 < per, jnp.clip(length - start1, 0, seg), 0)
    inverse = 1.0 / jnp.maximum(count, 1).astype(F32)
    return jnp.where(inside, 1.0, 0.0).astype(BF), inverse


def unpool(matrix, value):
    high = value.astype(BF)
    low = (value - high.astype(F32)).astype(BF)
    return dot_tn(jnp.concatenate([matrix, matrix], axis=0), jnp.concatenate([high, low], axis=0))


def tile_bias(tile, odd, length, wide):
    seg, per = seg_sizes(wide)
    row = lax.broadcasted_iota(jnp.int32, (ROWS, 1), 0)
    col = lax.broadcasted_iota(jnp.int32, (1, KEYS), 1)
    anchor = tile * TILE
    is_frame = row < TILE
    extra = row - TILE
    shift = jnp.where(wide, 4, 3).astype(jnp.int32)
    r = jnp.where(is_frame, jnp.right_shift(row, shift), jnp.bitwise_and(extra, 7))
    owned = is_frame | ((jnp.right_shift(extra, 3) == odd) & (r < per))
    key = col - (16 + FRONT)
    low = jnp.where(owned, r * seg - LEFT, 100000)
    high = jnp.minimum(r * seg + seg + RIGHT, length - anchor)
    frame_ok = (key >= jnp.maximum(low, -anchor)) & (key < high) & (col >= 16)
    c = jnp.bitwise_and(col, 7)
    slot = jnp.where((col < 16) & (c < per), jnp.where(col < 8, c - per, c), -100000)
    slot = jnp.where((col < 8) & (anchor == 0), -100000, slot)
    mem_ok = (slot >= r - MEM) & (slot < jnp.where(is_frame, r, -100000))
    return jnp.where(frame_ok | mem_ok, 0.0, -1e30).astype(F32)


def head_masks(rows):
    lane = jnp.right_shift(lax.broadcasted_iota(jnp.int32, (rows, 256), 1), 6)
    return [lane == h for h in range(4)]


def spread_heads(tile, masks):
    zero = jnp.zeros_like(tile)
    return jnp.concatenate([jnp.where(m, tile, zero) for m in masks], axis=0)


def gather_heads(stack, masks):
    total = jnp.where(masks[0], stack[:ROWS], 0.0)
    for h in range(1, 4):
        total = jnp.where(masks[h], stack[h * ROWS : (h + 1) * ROWS], total)
    return total


def key_window(pair, odd, lanes, frames_ref, even_ref, pad_ref):
    first = pl.multiple_of(pair * 16, 16)
    memory = even_ref[pl.ds(first, 16), lanes] if odd else pad_ref[pl.ds(first, 16), lanes]
    start = pl.multiple_of(pair * 128 + odd * 64, 64)
    return jnp.concatenate([memory, frames_ref[pl.ds(start, KEYS - 16), lanes]], axis=0)


def fill_windows(all_rows, frames_ref, even_ref, pad_ref, mem_rows, slot):
    width = all_rows.shape[1]
    memory = all_rows[:mem_rows].astype(F32)
    blank = jnp.zeros((8, width), F32)
    even_ref[...] = memory.astype(BF)
    pad_ref[...] = jnp.concatenate([blank, memory, blank], axis=0).astype(BF)
    frames_ref[:FRONT] = jnp.zeros((FRONT, width), BF)
    frames_ref[FRONT : FRONT + slot] = all_rows[mem_rows:].astype(BF)
    frames_ref[FRONT + slot :] = jnp.zeros((16, width), BF)


def attention_in(utt, lower, slot, pos_ref, len_ref, grp_ref, x_ref, mem_ref, gain, shift, wq, wk, wv, qvb, wo, ob,
                 *refs):
    (uc, mem, q, k, v, prob, mix, xh0, xh1, h, rs, after, memnext, kf, ke, kp, vf, ve, vp) = refs[-19:]
    mem_rows = slot // 8
    length = len_ref[utt]
    wide = grp_ref[utt] == 1
    g0, s0 = gain[0:1], shift[0:1]
    lane = lax.broadcasted_iota(jnp.int32, (1, 128), 1)

    def rows_in(i, carry):
        r = pl.ds(pl.multiple_of(i * 32, 32), 32)
        xhat, scale = normed(x_ref[r].astype(F32))
        xh0[0, r] = xhat.astype(BF)
        uc[0, r] = (xhat * g0 + s0).astype(BF)
        rs[0, r] = jnp.broadcast_to(scale, (32, 128))
        return carry

    lax.fori_loop(0, slot // 32, rows_in, 0, unroll=2)
    pm, inverse = pool_matrix(length, wide, slot)
    uc[0, slot:] = (dot(pm, uc[0, :slot]) * inverse).astype(BF)
    if lower:
        mem[0] = (dot(pm, x_ref[...]) * inverse).astype(BF)
    else:
        mem[0] = mem_ref[...]
    q[0] = (dot(uc[0], wq[...]) + qvb[0:1]).astype(BF)
    k[0, :mem_rows] = dot(mem[0], wk[...]).astype(BF)
    k[0, mem_rows:] = dot(uc[0, :slot], wk[...]).astype(BF)
    v[0, :mem_rows] = (dot(mem[0], wv[...]) + qvb[1:2]).astype(BF)
    v[0, mem_rows:] = (dot(uc[0, :slot], wv[...]) + qvb[1:2]).astype(BF)
    fill_windows(k[0], kf, ke, kp, mem_rows, slot)
    fill_windows(v[0], vf, ve, vp, mem_rows, slot)
    masks = head_masks(ROWS)

    def pair_step(pair, carry):
        for quad in range(2):
            lanes = slice(quad * 256, quad * 256 + 256)
            extra = None
            for odd in range(2):
                rows = pl.ds(pl.multiple_of(pair * 128 + odd * 64, 64), 64)
                srows = pl.ds(pl.multiple_of(slot + pair * 16, 16), 16)
                bias = tile_bias(pair * 2 + odd, odd, length, wide)
                qs = spread_heads(jnp.concatenate([q[0, rows, lanes], q[0, srows, lanes]], axis=0), masks)
                kw = key_window(pair, odd, lanes, kf, ke, kp)
                vw = key_window(pair, odd, lanes, vf, ve, vp)
                s = dot_nt(qs, kw).reshape(4, ROWS, KEYS) * 0.125 + bias[None]
                peak = jnp.maximum(jnp.max(s, axis=-1, keepdims=True), -1e29)
                e = jnp.exp(s - peak)
                total = jnp.sum(e, axis=-1, keepdims=True)
                p = (e * (1.0 / jnp.maximum(total, 1e-30))).astype(BF).reshape(4 * ROWS, KEYS)
                prob[0, pair * 4 + quad * 2 + odd] = p
                o = gather_heads(dot(p, vw), masks)
                mix[0, rows, lanes] = o[:TILE].astype(BF)
                extra = o[TILE:] if extra is None else extra + o[TILE:]
            mix[0, srows, lanes] = extra.astype(BF)
        return carry

    lax.fori_loop(0, slot // 128, pair_step, 0)
    z = dot(mix[0], wo[...]) + ob[...]
    memnext[...] = z[slot:].astype(BF)
    after[...] = z[:slot]
    g1, s1 = gain[1:2], shift[1:2]

    def rows_out(i, carry):
        r = pl.ds(pl.multiple_of(i * 32, 32), 32)
        a = x_ref[r].astype(F32) + after[r]
        after[r] = a
        xhat, scale = normed(a)
        xh1[0, r] = xhat.astype(BF)
        h[0, r] = (xhat * g1 + s1).astype(BF)
        rs[0, r] = jnp.where(lane == 0, rs[0, r], jnp.broadcast_to(scale, (32, 128)))
        return carry

    lax.fori_loop(0, slot // 32, rows_out, 0, unroll=2)


def ffn_in(utt, block, pos_ref, len_ref, h, after, gain, shift, wu, ub, wd, db, *refs):
    g, gp, xh2, rs2, y = refs[-5:]
    width = after.shape[1]
    total = after[...] + db[...]
    hid = h[0]
    for c in range(wu.shape[1] // 512):
        cols = slice(c * 512, c * 512 + 512)
        act, slope = gelu_parts(dot(hid, wu[:, cols]) + ub[:, cols])
        act = act.astype(BF)
        g[0, :, cols] = act
        gp[0, :, cols] = slope.astype(BF)
        total = total + dot(act, wd[cols])
    xhat, scale = normed(total)
    xh2[0] = xhat.astype(BF)
    rs2[0] = jnp.broadcast_to(scale, (block, 128))
    t = lax.broadcasted_iota(jnp.int32, (block, 1), 0) + pl.program_id(0) * block
    valid = jnp.where(t < len_ref[utt], 1.0, 0.0)
    y[...] = ((xhat * gain[2:3] + shift[2:3]) * valid).astype(BF)


def ffn_back(utt, block, pos_ref, len_ref, cot, xh2, rs2, gp, xh1, rs, gain, wu, wd, *refs):
    gd, gf, gz, ga, small, acc = refs[-6:]
    step = pl.program_id(0)
    t = lax.broadcasted_iota(jnp.int32, (block, 1), 0) + step * block
    valid = jnp.where(t < len_ref[utt], 1.0, 0.0)

    @pl.when(step == 0)
    def _():
        acc[...] = jnp.zeros_like(acc)

    gv = cot[...].astype(F32) * valid
    xhat = xh2[0].astype(F32)
    acc[0] += fold8(gv * xhat)
    acc[1] += fold8(gv)
    ga2 = norm_back(gv * gain[2:3], xhat, rs2[0, :, 0:1])
    gdl = ga2.astype(BF)
    gd[0] = gdl
    acc[2] += fold8(gdl.astype(F32))
    back = None
    for c in range(wu.shape[1] // 512):
        cols = slice(c * 512, c * 512 + 512)
        gfl = (dot_nt(gdl, wd[cols]) * gp[0, :, cols].astype(F32)).astype(BF)
        gf[0, :, cols] = gfl
        acc[6 + c] += fold8(gfl.astype(F32))
        part = dot_nt(gfl, wu[:, cols])
        back = part if back is None else back + part
    xhat = xh1[0].astype(F32)
    acc[3] += fold8(back * xhat)
    acc[4] += fold8(back)
    total = ga2 + norm_back(back * gain[1:2], xhat, rs[0, :, 1:2])
    ga[...] = total
    gzl = total.astype(BF)
    gz[0] = gzl
    acc[5] += fold8(gzl.astype(F32))

    @pl.when(step == pl.num_programs(0) - 1)
    def _():
        small[...] = jnp.sum(acc[...], axis=1)


def attention_back(utt, lower, slot, pos_ref, len_ref, grp_ref, gz, gmem, ga, q, k, v, prob, xh0, rs, gain,
                   wq, wk, wv, wo, *refs):
    (gq, gk, gv, gzs, gx, gm, small, kf, ke, kp, vf, ve, vp, gof, gos, akf, akm, avf, avm, gu, acc) = refs[-21:]
    mem_rows = slot // 8
    width = gu.shape[1]
    length = len_ref[utt]
    wide = grp_ref[utt] == 1
    fill_windows(k[0], kf, ke, kp, mem_rows, slot)
    fill_windows(v[0], vf, ve, vp, mem_rows, slot)
    gof[...] = dot_nt(gz[0], wo[...]).astype(BF)
    if lower:
        gzs[0] = gmem[...]
        gos[...] = dot_nt(gmem[...], wo[...]).astype(BF)
    else:
        gzs[0] = jnp.zeros_like(gzs[0])
        gos[...] = jnp.zeros_like(gos)
    for ref in (akf, akm, avf, avm):
        ref[...] = jnp.zeros_like(ref)
    masks = head_masks(ROWS)

    def pair_step(pair, carry):
        for quad in range(2):
            lanes = slice(quad * 256, quad * 256 + 256)
            extra = None
            srows = pl.ds(pl.multiple_of(slot + pair * 16, 16), 16)
            for odd in range(2):
                rows = pl.ds(pl.multiple_of(pair * 128 + odd * 64, 64), 64)
                qs = spread_heads(jnp.concatenate([q[0, rows, lanes], q[0, srows, lanes]], axis=0), masks)
                gos_rows = gos[pl.ds(pl.multiple_of(pair * 16, 16), 16), lanes]
                go = spread_heads(jnp.concatenate([gof[rows, lanes], gos_rows], axis=0), masks)
                kw = key_window(pair, odd, lanes, kf, ke, kp)
                vw = key_window(pair, odd, lanes, vf, ve, vp)
                p = prob[0, pair * 4 + quad * 2 + odd]
                gprob = dot_nt(go, vw) * p.astype(F32)
                gs = (gprob - p.astype(F32) * jnp.sum(gprob, axis=-1, keepdims=True)).astype(BF)
                gqt = gather_heads(dot(gs, kw), masks) * 0.125
                gkt = dot_tn(gs, qs) * 0.125
                gvt = dot_tn(p, go)
                gq[0, rows, lanes] = gqt[:TILE].astype(BF)
                extra = gqt[TILE:] if extra is None else extra + gqt[TILE:]
                mrows = pl.ds(pl.multiple_of(pair * 16 + odd * 8, 8), 16)
                frows = pl.ds(pl.multiple_of(pair * 128 + odd * 64, 64), KEYS - 16)
                akm[mrows, lanes] += gkt[:16]
                akf[frows, lanes] += gkt[16:]
                avm[mrows, lanes] += gvt[:16]
                avf[frows, lanes] += gvt[16:]
            gq[0, srows, lanes] = extra.astype(BF)
        return carry

    lax.fori_loop(0, slot // 128, pair_step, 0)
    for out, am, af in ((gk, akm, akf), (gv, avm, avf)):
        out[0, :mem_rows] = am[8 : 8 + mem_rows].astype(BF)
        out[0, mem_rows:] = af[FRONT : FRONT + slot].astype(BF)
    pm, inverse = pool_matrix(length, wide, slot)
    gmf = dot_nt(gk[0, :mem_rows], wk[...]) + dot_nt(gv[0, :mem_rows], wv[...])
    gm[...] = gmf.astype(BF)
    gc = dot_nt(gq[0, slot:], wq[...]) * inverse
    gu[...] = (dot_nt(gk[0, mem_rows:], wk[...]) + dot_nt(gv[0, mem_rows:], wv[...])
               + dot_nt(gq[0, :slot], wq[...]) + unpool(pm, gc))
    acc[...] = jnp.zeros_like(acc)
    if lower:
        akf[:slot] = unpool(pm, gmf * inverse)
    g0 = gain[0:1]

    def rows_out(i, carry):
        r = pl.ds(pl.multiple_of(i * 32, 32), 32)
        w = gu[r]
        xhat = xh0[0, r].astype(F32)
        acc[0] += fold8(w * xhat)
        acc[1] += fold8(w)
        total = ga[r] + norm_back(w * g0, xhat, rs[0, r, 0:1])
        if lower:
            total = total + akf[r]
        gx[r] = total.astype(BF)
        return carry

    lax.fori_loop(0, slot // 32, rows_out, 0, unroll=2)
    acc[2] = fold8(gq[0].astype(F32))
    acc[3] = fold8(gv[0].astype(F32))
    acc[4] = fold8(gzs[0].astype(F32))
    small[...] = jnp.sum(acc[...], axis=1)


def full(shape):
    return pl.BlockSpec(shape, lambda *_: (0,) * len(shape))


def slotted(shape):
    return pl.BlockSpec((1,) + shape, lambda i, pos, *_: (pos[0],) + (0,) * len(shape))


def slotted_rows(shape):
    return pl.BlockSpec((1,) + shape, lambda i, pos, *_: (pos[0], i) + (0,) * (len(shape) - 1))


def rows_of(shape):
    return pl.BlockSpec(shape, lambda i, *_: (i,) + (0,) * (len(shape) - 1))


def sds(shape, dtype):
    return jax.ShapeDtypeStruct(shape, dtype)


def run(body, grid, scalars, inputs, kept, outs, scratch, cost):
    extra = list(kept) if kept is not None else []
    aliases = {len(scalars) + len(inputs) + i: i for i in range(len(extra))}
    return pl.pallas_call(
        body,
        grid_spec=pltpu.PrefetchScalarGridSpec(
            num_scalar_prefetch=len(scalars),
            grid=grid,
            in_specs=[spec for _, spec in inputs] + [pl.BlockSpec(memory_space=pl.ANY)] * len(extra),
            out_specs=[spec for _, spec in outs],
            scratch_shapes=scratch,
        ),
        out_shape=[shape for shape, _ in outs],
        input_output_aliases=aliases,
        compiler_params=pltpu.CompilerParams(vmem_limit_bytes=VMEM_LIMIT, dimension_semantics=("arbitrary",)),
        cost_estimate=cost,
    )(*scalars, *[a for a, _ in inputs], *extra)


def cost_of(flops, moved, special=0):
    return pl.CostEstimate(flops=int(flops), bytes_accessed=int(moved), transcendentals=int(special))


def window_scratch(slot, width):
    mem_rows = slot // 8
    one = [
        pltpu.VMEM((FRONT + slot + 16, width), BF),
        pltpu.VMEM((mem_rows, width), BF),
        pltpu.VMEM((mem_rows + 16, width), BF),
    ]
    return one + one


ROOMS = 3


def forward(weights, utt, lower, scalars, frames, memory, kept):
    (gain, shift, wq, wk, wv, qvb, wo, ob, wu, ub, wd, db) = weights
    slot, width = frames.shape
    hid = wu.shape[1]
    mem_rows = slot // 8
    every = slot + mem_rows
    pairs = slot // 128
    kept_a, kept_f = kept if kept is not None else (None, None)
    low = lambda *s: sds((ROOMS,) + s, BF)
    outs = [(low(*s), slotted(s)) for s in (
        (every, width), (mem_rows, width), (every, width), (every, width), (every, width),
        (pairs * 4, 4 * ROWS, KEYS), (every, width), (slot, width), (slot, width), (slot, width))]
    outs.append((sds((ROOMS, slot, 128), F32), slotted((slot, 128))))
    n_kept = len(outs)
    outs.append((sds((slot, width), F32), full((slot, width))))
    outs.append((sds((mem_rows, width), BF), full((mem_rows, width))))
    ins = [(a, full(a.shape)) for a in (frames, memory, gain, shift, wq, wk, wv, qvb, wo, ob)]
    res = run(
        functools.partial(attention_in, utt, lower, slot), (1,), scalars, ins, kept_a, outs,
        window_scratch(slot, width), cost_of(8 * every * width * width, 12 * every * width * 2, 8 * slot * 128))
    kept_a, (after, memnext) = res[:n_kept], res[n_kept:]
    h = kept_a[9]
    block = slot // 2
    ins = [(h, slotted_rows((block, width))), (after, rows_of((block, width)))]
    ins += [(a, full(a.shape)) for a in (gain, shift, wu, ub, wd, db)]
    outs = [(low(slot, hid), slotted_rows((block, hid))), (low(slot, hid), slotted_rows((block, hid))),
            (low(slot, width), slotted_rows((block, width))),
            (sds((ROOMS, slot, 128), F32), slotted_rows((block, 128))),
            (sds((slot, width), BF), rows_of((block, width)))]
    res = run(functools.partial(ffn_in, utt, block), (slot // block,), scalars[:2], ins, kept_f, outs, [],
              cost_of(4 * slot * width * hid, 4 * slot * hid + 4 * width * hid, slot * hid * 2))
    return res[4], memnext, (kept_a, res[:4])


def backward_ffn(weights, utt, scalars, cot, kept, grads):
    (gain, shift, wq, wk, wv, qvb, wo, ob, wu, ub, wd, db) = weights
    slot, width = cot.shape
    hid = wu.shape[1]
    block = slot // 2
    kept_a, kept_f = kept
    ins = [(cot, rows_of((block, width))), (kept_f[2], slotted_rows((block, width))),
           (kept_f[3], slotted_rows((block, 128))), (kept_f[1], slotted_rows((block, hid))),
           (kept_a[8], slotted_rows((block, width))), (kept_a[10], slotted_rows((block, 128)))]
    ins += [(a, full(a.shape)) for a in (gain, wu, wd)]
    low = lambda *s: sds((ROOMS,) + s, BF)
    outs = [(low(slot, width), slotted_rows((block, width))), (low(slot, hid), slotted_rows((block, hid))),
            (low(slot, width), slotted_rows((block, width))), (sds((slot, width), F32), rows_of((block, width))),
            (sds((16, width), F32), full((16, width)))]
    res = run(functools.partial(ffn_back, utt, block), (slot // block,), scalars[:2], ins, grads, outs,
              [pltpu.VMEM((16, 8, width), F32)],
              cost_of(4 * slot * width * hid, 4 * slot * hid + 4 * width * hid))
    return res[:3], res[3], res[4]


def backward_attention(weights, utt, lower, scalars, gz, gmem, ga, kept, grads):
    (gain, shift, wq, wk, wv, qvb, wo, ob, wu, ub, wd, db) = weights
    slot, width = ga.shape
    mem_rows = slot // 8
    every = slot + mem_rows
    (uc, mem, q, k, v, prob, mix, xh0, xh1, h, rs), _ = kept
    ins = [(gz, slotted((slot, width))), (gmem, full(gmem.shape)), (ga, full(ga.shape))]
    ins += [(a, slotted(a.shape[1:])) for a in (q, k, v, prob, xh0, rs)]
    ins += [(a, full(a.shape)) for a in (gain, wq, wk, wv, wo)]
    low = lambda *s: sds((ROOMS,) + s, BF)
    outs = [(low(*s), slotted(s)) for s in ((every, width),) * 3 + ((mem_rows, width),)]
    outs += [(sds((slot, width), BF), full((slot, width))), (sds((mem_rows, width), BF), full((mem_rows, width))),
             (sds((16, width), F32), full((16, width)))]
    scratch = window_scratch(slot, width) + [
        pltpu.VMEM((slot, width), BF), pltpu.VMEM((mem_rows, width), BF),
        pltpu.VMEM((FRONT + slot + 16, width), F32), pltpu.VMEM((mem_rows + 16, width), F32),
        pltpu.VMEM((FRONT + slot + 16, width), F32), pltpu.VMEM((mem_rows + 16, width), F32),
        pltpu.VMEM((slot, width), F32), pltpu.VMEM((16, 8, width), F32)]
    res = run(functools.partial(attention_back, utt, lower, slot), (1,), scalars, ins, grads, outs, scratch,
              cost_of(8 * every * width * width, 12 * every * width * 2))
    return res[:4], res[4], res[5], res[6]


LANES_OUT = 4
STAGES = 4


def emit_group(value, me, more, out, part):
    part[...] = value
    sub = jnp.bitwise_and(me, LANES_OUT - 1)
    rows = value.shape[0] // LANES_OUT
    for r in range(LANES_OUT):
        got = part[pl.ds(pl.multiple_of(jnp.bitwise_xor(sub, r) * rows, rows), rows)]
        if more is not None:
            got = got + more[0, r].astype(F32)
        out[0, r] = got.astype(out.dtype)


def pair_weights(has_more, me_ref, left, right, *refs):
    more = refs[0] if has_more else None
    out, part = refs[-2:]
    emit_group(sum(dot_tn(left[u], right[u]) for u in range(left.shape[0])), me_ref[0], more, out, part)


def ffn_group_grads(slots, groups, chunk_left, me, left, right, more):
    _, slot, _ = left.shape
    width = min(left.shape[2], right.shape[2])
    low, count = groups
    place = lambda j, me: jnp.bitwise_xor(j + low, jnp.right_shift(me[0], 2))
    whole = pl.BlockSpec((slots, slot, width), lambda j, me: (0, 0, 0))
    chunk = pl.BlockSpec((slots, slot, width), lambda j, me: (0, 0, place(j, me)))
    block = (1, LANES_OUT, width // LANES_OUT, width)
    out_spec = pl.BlockSpec(block, lambda j, me: (j, 0, 0, 0))
    extra = [] if more is None else [more]
    return pl.pallas_call(
        functools.partial(pair_weights, more is not None),
        grid_spec=pltpu.PrefetchScalarGridSpec(
            num_scalar_prefetch=1, grid=(count,),
            in_specs=[chunk if chunk_left else whole, whole if chunk_left else chunk] + [out_spec] * len(extra),
            out_specs=out_spec,
            scratch_shapes=[pltpu.VMEM((width, width), F32)]),
        out_shape=sds((count,) + block[1:], BF),
        compiler_params=pltpu.CompilerParams(vmem_limit_bytes=VMEM_LIMIT, dimension_semantics=("arbitrary",)),
        cost_estimate=cost_of(2 * slots * slot * count * width * width, 2 * slots * slot * (count + 1) * width),
    )(me, left, right, *extra)


def attention_weights(low, has_more, me_ref, uc, mem, mix, gq, gk, gv, gz, gzs, *refs):
    more = refs[0] if has_more else None
    out, part = refs[-2:]
    slots, every, width = uc.shape
    slot = gz.shape[1]
    mem_rows = every - slot
    me = me_ref[0]
    which = jnp.bitwise_xor(pl.program_id(0) + low, jnp.right_shift(me, 2))

    @pl.when(which == 0)
    def _():
        part[...] = sum(dot_tn(uc[u], gq[u]) for u in range(slots))

    for place, ref in ((1, gk), (2, gv)):
        @pl.when(which == place)
        def _():
            part[...] = sum(dot_tn(mem[u], ref[u, :mem_rows]) + dot_tn(uc[u, :slot], ref[u, mem_rows:])
                            for u in range(slots))

    @pl.when(which == 3)
    def _():
        part[...] = sum(dot_tn(mix[u, :slot], gz[u]) + dot_tn(mix[u, slot:], gzs[u]) for u in range(slots))

    sub = jnp.bitwise_and(me, LANES_OUT - 1)
    rows = width // LANES_OUT
    for r in range(LANES_OUT):
        got = part[pl.ds(pl.multiple_of(jnp.bitwise_xor(sub, r) * rows, rows), rows)]
        if more is not None:
            got = got + more[0, r].astype(F32)
        out[0, r] = got.astype(out.dtype)


def attention_group_grads(slots, groups, me, arrays, more):
    _, every, width = arrays[0].shape
    low, count = groups
    block = (1, LANES_OUT, width // LANES_OUT, width)
    out_spec = pl.BlockSpec(block, lambda j, me: (j, 0, 0, 0))
    extra = [] if more is None else [more]
    return pl.pallas_call(
        functools.partial(attention_weights, low, more is not None),
        grid_spec=pltpu.PrefetchScalarGridSpec(
            num_scalar_prefetch=1, grid=(count,),
            in_specs=[pl.BlockSpec((slots,) + a.shape[1:], lambda j, me: (0, 0, 0)) for a in arrays]
            + [out_spec] * len(extra),
            out_specs=out_spec,
            scratch_shapes=[pltpu.VMEM((width, width), F32)]),
        out_shape=sds((count,) + block[1:], BF),
        compiler_params=pltpu.CompilerParams(vmem_limit_bytes=VMEM_LIMIT, dimension_semantics=("arbitrary",)),
        cost_estimate=cost_of(2 * count * slots * every * width * width, 16 * slots * every * width),
    )(me, *arrays, *extra)


def restore_group(own, far, me, value):
    gme = jnp.right_shift(me, 2)
    sub = jnp.bitwise_and(me, LANES_OUT - 1)
    rows = own.shape[2]
    place = jnp.bitwise_xor(pl.program_id(0), gme)
    half = own.shape[0]
    for ref, low in ((own, 0), (far, half)):
        @pl.when((place >= low) & (place < low + half))
        def _():
            for r in range(LANES_OUT):
                value(r, ref[place - low, jnp.bitwise_xor(sub, r)].astype(F32))


def restore_wide(me_ref, own, far, out):
    rows = own.shape[2]

    def put(r, got):
        out[0, r * rows : (r + 1) * rows] = got

    restore_group(own, far, me_ref[0], put)


def restore_square(me_ref, own, far, *outs):
    rows = own.shape[2]

    def put(r, got):
        for matrix, out in enumerate(outs):
            @pl.when(pl.program_id(0) == matrix)
            def _():
                out[0, r * rows : (r + 1) * rows] = got

    restore_group(own, far, me_ref[0], put)


def restore(me, own, far, kind):
    half, _, rows, width = own.shape
    whole = pl.BlockSpec(own.shape, lambda j, me: (0, 0, 0, 0))
    groups = 2 * half
    if kind == "down":
        body, shapes = restore_wide, [(1, groups * width, width)]
        specs = [pl.BlockSpec((1, width, width), lambda j, me: (0, j, 0))]
    elif kind == "up":
        body, shapes = restore_wide, [(1, width, groups * width)]
        specs = [pl.BlockSpec((1, width, width), lambda j, me: (0, 0, j))]
    else:
        body, shapes = restore_square, [(1, width, width)] * groups
        specs = [pl.BlockSpec((1, width, width), lambda j, me: (0, 0, 0))] * groups
    return pl.pallas_call(
        body,
        grid_spec=pltpu.PrefetchScalarGridSpec(num_scalar_prefetch=1, grid=(groups,), in_specs=[whole, whole],
                                               out_specs=specs),
        out_shape=[sds(s, F32) for s in shapes],
        compiler_params=pltpu.CompilerParams(vmem_limit_bytes=VMEM_LIMIT, dimension_semantics=("arbitrary",)),
        cost_estimate=cost_of(0, 6 * groups * width * width),
    )(me, own, far)


def swap(value, bit):
    n = lax.axis_size("dp")
    return lax.ppermute(value, "dp", [(i, i ^ (1 << bit)) for i in range(n)])


def finish_sum(value, extra_bits):
    added = lambda a, b: (a.astype(F32) + b.astype(F32)).astype(BF)
    for bit in range(1, STAGES):
        half = value.shape[0] // 2
        value = added(value[:half], swap(value[half:], bit))
    for bit in extra_bits:
        value = added(value, swap(value, bit))
    for bit in reversed(range(1, STAGES)):
        value = jnp.concatenate([value, swap(value, bit)], axis=0)
    return value


def shifted(block, axis, distance):
    devices = range(lax.axis_size(axis))
    route = [(i - distance, i) for i in devices if i - distance in devices]
    return lax.ppermute(block, axis, route)


def on_device(ends, lengths, seg_group, norm_gain, norm_shift, w_query, w_key, w_value, qv_bias, w_out, out_bias,
              w_up, up_bias, w_down, down_bias):
    weights = (norm_gain[0], norm_shift[0], w_query[0], w_key[0], w_value[0], qv_bias[0], w_out[0], out_bias,
               w_up[0], up_bias, w_down[0], down_bias)
    section = lax.axis_index("section")
    first = section == 0
    slots = lengths.shape[0]
    width = ends.shape[2]
    slot = ends.shape[1] // slots
    mem_rows = slot // 8
    hid = w_up.shape[2]
    local = ends[0].reshape(slots, slot, width)
    lower = [(jnp.where(first, b, ROOMS - 1).astype(jnp.int32).reshape(1), lengths, seg_group) for b in range(slots)]
    upper = [(jnp.where(first, ROOMS - 1, b).astype(jnp.int32).reshape(1), lengths, seg_group) for b in range(slots)]
    blank = jnp.zeros((mem_rows, width), BF)

    bits = lax.axis_size("dp").bit_length() - 1
    place = lax.axis_index("dp").astype(jnp.int32)
    me = sum((jnp.bitwise_and(jnp.right_shift(place, s), 1) << (STAGES - 1 - s)) for s in range(STAGES)).reshape(1)

    def sum_groups(value):
        shape = value.shape
        return finish_sum(value.reshape((-1,) + shape[2:]), range(STAGES, bits)).reshape(shape)

    def ffn_sum(chunk_left, left, right):
        away = ffn_group_grads(slots, (2, 2), chunk_left, me, left, right, None)
        return sum_groups(ffn_group_grads(slots, (0, 2), chunk_left, me, left, right, swap(away, 0)))

    kept = None
    sent = []
    for b in range(slots):
        y, memory, kept = forward(weights, b, True, lower[b], local[b], blank, kept)
        sent.append(shifted((y, memory), "section", 1))
    finals = []
    for b in range(slots):
        y, _, kept = forward(weights, b, False, upper[b], sent[b][0], sent[b][1], kept)
        finals.append(y)

    kept_a, kept_f = kept
    grads_f = grads_a = None
    smalls = [[], []]
    sent = []
    for b in range(slots):
        grads_f, ga, small_f = backward_ffn(weights, b, upper[b], local[b], kept, grads_f)
        grads_a, gx, gm, small_a = backward_attention(weights, b, False, upper[b], grads_f[2], blank, ga, kept, grads_a)
        smalls[1].append((small_f, small_a))
        sent.append(shifted((gx, gm), "section", -1))
    inputs_back = []
    held = []
    for b in range(slots):
        grads_f, ga, small_f = backward_ffn(weights, b, lower[b], sent[b][0], kept, grads_f)
        if b == slots - 1:
            down = ffn_sum(True, kept_f[0], grads_f[0])
            up = ffn_sum(False, kept_a[9], grads_f[1])
        grads_a, gx, gm, small_a = backward_attention(weights, b, True, lower[b], grads_f[2], sent[b][1], ga, kept, grads_a)
        smalls[0].append((small_f, small_a))
        inputs_back.append(gx)
    arrays = (kept_a[0], kept_a[1], kept_a[6], grads_a[0], grads_a[1], grads_a[2], grads_f[2], grads_a[3])
    away = attention_group_grads(slots, (2, 2), me, arrays, None)
    square = sum_groups(attention_group_grads(slots, (0, 2), me, arrays, swap(away, 0)))

    def total(side, part):
        return sum(smalls[side][b][part] for b in range(slots))

    small_f = jnp.where(first, total(0, 0), total(1, 0))
    small_a = jnp.where(first, total(0, 1), total(1, 1))
    small = jnp.concatenate([
        jnp.stack([small_a[0], small_f[3], small_f[0], small_a[1], small_f[4], small_f[1], small_a[2], small_a[3],
                   small_f[5] + small_a[4], small_f[2]]), small_f[6 : 6 + hid // width]], axis=0)
    for bit in range(bits):
        small = small + swap(small, bit)
    ends_out = jnp.where(first, jnp.stack(inputs_back), jnp.stack(finals)).reshape(1, slots * slot, width)
    (down,) = restore(me, down, swap(down, 0), "down")
    (up,) = restore(me, up, swap(up, 0), "up")
    grad_q, grad_k, grad_v, grad_o = restore(me, square, swap(square, 0), "square")
    return (ends_out, small[None, 0:3], small[None, 3:6], grad_q, grad_k, grad_v, small[None, 6:8],
            grad_o, small[8:9], up, small[10:].reshape(1, hid), down, small[9:10])


def solution(mesh):
    placed = (
        P("section", "dp", None), P("dp"), P("dp"),
        P("section", None, None), P("section", None, None), P("section", None, None), P("section", None, None),
        P("section", None, None), P("section", None, None), P("section", None, None), P("section", None),
        P("section", None, None), P("section", None), P("section", None, None), P("section", None),
    )
    return jax.shard_map(
        on_device,
        mesh=mesh,
        in_specs=placed,
        out_specs=(
            P("section", "dp", None), P("section", None, None), P("section", None, None), P("section", None, None),
            P("section", None, None), P("section", None, None), P("section", None, None), P("section", None, None),
            P("section", None), P("section", None, None), P("section", None), P("section", None, None),
            P("section", None),
        ),
        check_vma=False,
    )
```

```python
import functools
import jax
import jax.numpy as jnp
from jax import lax
from jax.experimental import pallas as pl
from jax.experimental.pallas import tpu as pltpu
from jax.sharding import PartitionSpec as P

LEFT = 30
RIGHT = 4
MEM = 4
TILE = 64
KEYS = 128
ROWS = 80
FRONT = 32
BF = jnp.bfloat16
F32 = jnp.float32
VMEM_LIMIT = 56 * 1024 * 1024


def dot(a, b):
    return lax.dot_general(a, b, (((1,), (0,)), ((), ())), preferred_element_type=F32)


def dot_nt(a, b):
    return lax.dot_general(a, b, (((1,), (1,)), ((), ())), preferred_element_type=F32)


def dot_tn(a, b):
    return lax.dot_general(a, b, (((0,), (0,)), ((), ())), preferred_element_type=F32)


def normed(value):
    center = value - jnp.mean(value, axis=-1, keepdims=True)
    rs = lax.rsqrt(jnp.mean(center * center, axis=-1, keepdims=True) + 1e-05)
    return center * rs, rs


def norm_back(w, xhat, rs):
    return (w - jnp.mean(w, axis=-1, keepdims=True) - xhat * jnp.mean(w * xhat, axis=-1, keepdims=True)) * rs


def fold8(value):
    rows, width = value.shape
    return jnp.sum(value.reshape(rows // 8, 8, width), axis=0)


def gelu_parts(f):
    phi = 0.5 + 0.5 * lax.erf(f * 0.7071067811865476)
    return f * phi, phi + f * (jnp.exp(f * f * -0.5) * 0.3989422804014327)


def seg_sizes(wide):
    return jnp.where(wide, 16, 8).astype(jnp.int32), jnp.where(wide, 4, 8).astype(jnp.int32)


def pool_matrix(length, wide, slot):
    seg, per = seg_sizes(wide)
    rows = slot // 8
    e = lax.broadcasted_iota(jnp.int32, (rows, slot), 0)
    t = lax.broadcasted_iota(jnp.int32, (rows, slot), 1)
    r = jnp.bitwise_and(e, 7)
    start = jnp.right_shift(e, 3) * TILE + r * seg
    inside = (t >= start) & (t < start + seg) & (t < length) & (r < per)
    e1 = lax.broadcasted_iota(jnp.int32, (rows, 1), 0)
    r1 = jnp.bitwise_and(e1, 7)
    start1 = jnp.right_shift(e1, 3) * TILE + r1 * seg
    count = jnp.where(r1 < per, jnp.clip(length - start1, 0, seg), 0)
    inverse = 1.0 / jnp.maximum(count, 1).astype(F32)
    return jnp.where(inside, 1.0, 0.0).astype(BF), inverse


def unpool(matrix, value):
    high = value.astype(BF)
    low = (value - high.astype(F32)).astype(BF)
    return dot_tn(jnp.concatenate([matrix, matrix], axis=0), jnp.concatenate([high, low], axis=0))


def tile_bias(tile, odd, length, wide):
    seg, per = seg_sizes(wide)
    row = lax.broadcasted_iota(jnp.int32, (ROWS, 1), 0)
    col = lax.broadcasted_iota(jnp.int32, (1, KEYS), 1)
    anchor = tile * TILE
    is_frame = row < TILE
    extra = row - TILE
    shift = jnp.where(wide, 4, 3).astype(jnp.int32)
    r = jnp.where(is_frame, jnp.right_shift(row, shift), jnp.bitwise_and(extra, 7))
    owned = is_frame | ((jnp.right_shift(extra, 3) == odd) & (r < per))
    key = col - (16 + FRONT)
    low = jnp.where(owned, r * seg - LEFT, 100000)
    high = jnp.minimum(r * seg + seg + RIGHT, length - anchor)
    frame_ok = (key >= jnp.maximum(low, -anchor)) & (key < high) & (col >= 16)
    c = jnp.bitwise_and(col, 7)
    slot = jnp.where((col < 16) & (c < per), jnp.where(col < 8, c - per, c), -100000)
    slot = jnp.where((col < 8) & (anchor == 0), -100000, slot)
    mem_ok = (slot >= r - MEM) & (slot < jnp.where(is_frame, r, -100000))
    return jnp.where(frame_ok | mem_ok, 0.0, -1e30).astype(F32)


def head_masks(rows):
    lane = jnp.right_shift(lax.broadcasted_iota(jnp.int32, (rows, 256), 1), 6)
    return [lane == h for h in range(4)]


def spread_heads(tile, masks):
    zero = jnp.zeros_like(tile)
    return jnp.concatenate([jnp.where(m, tile, zero) for m in masks], axis=0)


def gather_heads(stack, masks):
    total = jnp.where(masks[0], stack[:ROWS], 0.0)
    for h in range(1, 4):
        total = jnp.where(masks[h], stack[h * ROWS : (h + 1) * ROWS], total)
    return total


def key_window(tile, lanes, frames_ref, even_ref, pad_ref):
    first = tile // 2 * 16
    memory = even_ref[first : first + 16, lanes] if tile % 2 else pad_ref[first : first + 16, lanes]
    return jnp.concatenate([memory, frames_ref[tile * TILE : tile * TILE + KEYS - 16, lanes]], axis=0)


def fill_windows(all_rows, frames_ref, even_ref, pad_ref, mem_rows, slot):
    width = all_rows.shape[1]
    memory = all_rows[:mem_rows].astype(F32)
    blank = jnp.zeros((8, width), F32)
    even_ref[...] = memory.astype(BF)
    pad_ref[...] = jnp.concatenate([blank, memory, blank], axis=0).astype(BF)
    frames_ref[:FRONT] = jnp.zeros((FRONT, width), BF)
    frames_ref[FRONT : FRONT + slot] = all_rows[mem_rows:].astype(BF)
    frames_ref[FRONT + slot :] = jnp.zeros((16, width), BF)


CHUNK = 32
G0, G1, G2, S0, S1, S2, QB, VB, OB, DB, UB = range(11)
KEPT = ("uc", "mem", "q", "k", "v", "prob", "mix", "xh0", "xh1", "h", "rs", "g", "gp", "xh2")
GRADS = ("gd", "gf", "gz", "gq", "gk", "gv")


def forward_kernel(utt, lower, pos_ref, len_ref, grp_ref, x_ref, mem_ref, gain, shift, wq, wk, wv, qvb, ob, ub, db,
                   wo_far, wu_far, wd_far, *refs):
    n = len(KEPT)
    far = dict(zip(KEPT, refs[-(2 * n + 13) - 2 : -(n + 13) - 2]))
    y, memnext = refs[-(n + 13) - 2 : -(n + 13)]
    near = dict(zip(KEPT, refs[-(n + 13) : -13]))
    wo, wu, wd, kf, ke, kp, vf, ve, vp, after, in_sem, out_sem, y_near = refs[-13:]
    slot, width = x_ref.shape
    mem_rows = slot // 8
    pos = pos_ref[0]
    length = len_ref[utt]
    wide = grp_ref[utt] == 1
    loads = [pltpu.make_async_copy(a, b, in_sem.at[i]) for i, (a, b) in
             enumerate(((wo_far, wo), (wu_far, wu), (wd_far, wd)))]
    for copy in loads:
        copy.start()
    stores = []

    def keep(*names):
        for name in names:
            copy = pltpu.make_async_copy(near[name], far[name].at[pos], out_sem.at[KEPT.index(name)])
            copy.start()
            stores.append(copy)

    uc, mem, q, k, v, prob, mix = (near[name] for name in KEPT[:7])
    rs = near["rs"]
    lane = lax.broadcasted_iota(jnp.int32, (1, 128), 1)
    for i in range(0, slot, CHUNK):
        r = slice(i, i + CHUNK)
        xhat, scale = normed(x_ref[r].astype(F32))
        near["xh0"][r] = xhat.astype(BF)
        uc[r] = (xhat * gain[0:1] + shift[0:1]).astype(BF)
        rs[r] = jnp.broadcast_to(scale, (CHUNK, 128))
    pm, inverse = pool_matrix(length, wide, slot)
    uc[slot:] = (dot(pm, uc[:slot]) * inverse).astype(BF)
    if lower:
        mem[...] = (dot(pm, x_ref[...]) * inverse).astype(BF)
    else:
        mem[...] = mem_ref[...]
    keep("xh0", "uc", "mem")
    q[...] = (dot(uc[...], wq[...]) + qvb[0:1]).astype(BF)
    k[:mem_rows] = dot(mem[...], wk[...]).astype(BF)
    k[mem_rows:] = dot(uc[:slot], wk[...]).astype(BF)
    v[:mem_rows] = (dot(mem[...], wv[...]) + qvb[1:2]).astype(BF)
    v[mem_rows:] = (dot(uc[:slot], wv[...]) + qvb[1:2]).astype(BF)
    keep("q", "k", "v")
    fill_windows(k[...], kf, ke, kp, mem_rows, slot)
    fill_windows(v[...], vf, ve, vp, mem_rows, slot)
    masks = head_masks(ROWS)
    for pair in range(slot // (2 * TILE)):
        srows = slice(slot + pair * 16, slot + pair * 16 + 16)
        biases = [tile_bias(pair * 2 + odd, odd, length, wide) for odd in range(2)]
        for quad in range(width // 256):
            lanes = slice(quad * 256, quad * 256 + 256)
            extra = None
            for odd in range(2):
                tile = pair * 2 + odd
                rows = slice(tile * TILE, tile * TILE + TILE)
                qs = spread_heads(jnp.concatenate([q[rows, lanes], q[srows, lanes]], axis=0), masks)
                kw = key_window(tile, lanes, kf, ke, kp)
                vw = key_window(tile, lanes, vf, ve, vp)
                s = dot_nt(qs, kw).reshape(4, ROWS, KEYS) * 0.125 + biases[odd][None]
                peak = jnp.maximum(jnp.max(s, axis=-1, keepdims=True), -1e29)
                e = jnp.exp(s - peak)
                total = jnp.sum(e, axis=-1, keepdims=True)
                p = (e * (1.0 / jnp.maximum(total, 1e-30))).astype(BF).reshape(4 * ROWS, KEYS)
                prob[pair * 4 + quad * 2 + odd] = p
                o = gather_heads(dot(p, vw), masks)
                mix[rows, lanes] = o[:TILE].astype(BF)
                extra = o[TILE:] if extra is None else extra + o[TILE:]
            mix[srows, lanes] = extra.astype(BF)
    keep("prob", "mix")
    loads[0].wait()
    z = dot(mix[...], wo[...]) + ob[...]
    memnext[...] = z[slot:].astype(BF)
    after[...] = z[:slot]
    for i in range(0, slot, CHUNK):
        r = slice(i, i + CHUNK)
        a = x_ref[r].astype(F32) + after[r]
        after[r] = a + db[...]
        xhat, scale = normed(a)
        near["xh1"][r] = xhat.astype(BF)
        near["h"][r] = (xhat * gain[1:2] + shift[1:2]).astype(BF)
        rs[r] = jnp.where(lane == 0, rs[r], jnp.broadcast_to(scale, (CHUNK, 128)))
    keep("xh1", "h")
    loads[1].wait()
    for c in range(wu.shape[1] // 512):
        cols = slice(c * 512, c * 512 + 512)
        act, slope = gelu_parts(dot(near["h"][...], wu[:, cols]) + ub[:, cols])
        act = act.astype(BF)
        near["g"][:, cols] = act
        near["gp"][:, cols] = slope.astype(BF)
        if c == 0:
            loads[2].wait()
        after[...] += dot(act, wd[cols])
    keep("g", "gp")
    for i in range(0, slot, CHUNK):
        r = slice(i, i + CHUNK)
        xhat, scale = normed(after[r])
        near["xh2"][r] = xhat.astype(BF)
        rs[r] = jnp.where(lane == 2, jnp.broadcast_to(scale, (CHUNK, 128)), rs[r])
        t = lax.broadcasted_iota(jnp.int32, (CHUNK, 1), 0) + i
        valid = jnp.where(t < length, 1.0, 0.0)
        y[r] = ((xhat * gain[2:3] + shift[2:3]) * valid).astype(BF)
    keep("xh2", "rs")
    for copy in stores:
        copy.wait()


def backward_kernel(utt, lower, do_ffn, do_att, pos_ref, len_ref, grp_ref, cot, gmem, ga_in, gain,
                    wq_far, wk_far, wv_far, wo_far, wu_far, wd_far, *refs):
    kept = dict(zip(KEPT, refs[: len(KEPT)]))
    n = len(GRADS)
    spare = 27
    names = [g for g in GRADS if (do_ffn and g in GRADS[:3]) or (do_att and g in GRADS[2:])]
    far = dict(zip(names, refs[-(spare + n) - 4 - len(names) : -(spare + n) - 4]))
    gx, gm, ga_out, small = refs[-(spare + n) - 4 : -(spare + n)]
    near = dict(zip(GRADS, refs[-(spare + n) : -spare]))
    (wq, wk, wv, wo, wu, wd, q, k, v, prob, xh0, xh1, rs, gp, xh2, kf, ke, kp, vf, ve, vp, gom, akf, akm, acc,
     in_sem, out_sem) = refs[-spare:]
    slot, width = cot.shape
    mem_rows = slot // 8
    pos = pos_ref[0]
    length = len_ref[utt]
    wide = grp_ref[utt] == 1
    gz, gq, gk, gv = near["gz"], near["gq"], near["gk"], near["gv"]
    plan = []
    if do_ffn:
        plan += [("rs", kept["rs"].at[pos], rs), ("xh2", kept["xh2"].at[pos], xh2), ("wd", wd_far, wd),
                 ("gp", kept["gp"].at[pos], gp), ("wu", wu_far, wu), ("xh1", kept["xh1"].at[pos], xh1)]
    else:
        plan += [("rs", kept["rs"].at[pos], rs),
                 ("gz", far["gz"].at[pos, pl.ds(0, slot)], gz.at[pl.ds(0, slot)])]
    if do_att:
        plan += [("wo", wo_far, wo)] + [(name, kept[name].at[pos], ref) for name, ref in
                                        (("k", k), ("v", v), ("q", q), ("prob", prob))]
        plan += [("wk", wk_far, wk), ("wv", wv_far, wv), ("wq", wq_far, wq), ("xh0", kept["xh0"].at[pos], xh0)]
    loads = {}
    for i, (name, src, dst) in enumerate(plan):
        loads[name] = pltpu.make_async_copy(src, dst, in_sem.at[i])
        loads[name].start()
    need = lambda *which: [loads[name].wait() for name in which]
    stores = []

    def send(src, dst):
        copy = pltpu.make_async_copy(src, dst, out_sem.at[len(stores)])
        copy.start()
        stores.append(copy)

    acc[...] = jnp.zeros_like(acc)
    need("rs")
    if do_ffn:
        need("xh2")
        for i in range(0, slot, CHUNK):
            r = slice(i, i + CHUNK)
            t = lax.broadcasted_iota(jnp.int32, (CHUNK, 1), 0) + i
            gy = cot[r].astype(F32) * jnp.where(t < length, 1.0, 0.0)
            xhat = xh2[r].astype(F32)
            acc[G2] += fold8(gy * xhat)
            acc[S2] += fold8(gy)
            ga2 = norm_back(gy * gain[2:3], xhat, rs[r, 2:3])
            ga_out[r] = ga2
            low = ga2.astype(BF)
            near["gd"][r] = low
            acc[DB] += fold8(low.astype(F32))
        send(near["gd"], far["gd"].at[pos])
        need("wd", "gp", "wu")
        gdl = near["gd"]
        back = None
        for c in range(wu.shape[1] // 512):
            cols = slice(c * 512, c * 512 + 512)
            gfl = (dot_nt(gdl[...], wd[cols]) * gp[:, cols].astype(F32)).astype(BF)
            near["gf"][:, cols] = gfl
            acc[UB + c] += fold8(gfl.astype(F32))
            part = dot_nt(gfl, wu[:, cols])
            if c == 0:
                akf[:slot] = part
            else:
                akf[:slot] += part
        send(near["gf"], far["gf"].at[pos])
        need("xh1")
        for i in range(0, slot, CHUNK):
            r = slice(i, i + CHUNK)
            back = akf[r]
            xhat = xh1[r].astype(F32)
            acc[G1] += fold8(back * xhat)
            acc[S1] += fold8(back)
            total = ga_out[r] + norm_back(back * gain[1:2], xhat, rs[r, 1:2])
            ga_out[r] = total
            low = total.astype(BF)
            gz[r] = low
            acc[OB] += fold8(low.astype(F32))
        send(gz.at[pl.ds(0, slot)], far["gz"].at[pos, pl.ds(0, slot)])
        ga = ga_out
    else:
        ga = ga_in
        need("gz")
    if do_att:
        gz[slot:] = gmem[...] if lower else jnp.zeros((mem_rows, width), BF)
        send(gz.at[pl.ds(slot, mem_rows)], far["gz"].at[pos, pl.ds(slot, mem_rows)])
        if lower:
            acc[OB] += fold8(gmem[...].astype(F32))
        need("wo", "k", "v", "q", "prob")
        gom[...] = dot_nt(gz[...], wo[...]).astype(BF)
        fill_windows(k[...], kf, ke, kp, mem_rows, slot)
        fill_windows(v[...], vf, ve, vp, mem_rows, slot)
        masks = head_masks(ROWS)
        for quad in range(width // 256):
            lanes = slice(quad * 256, quad * 256 + 256)
            akf[...] = jnp.zeros_like(akf)
            akm[...] = jnp.zeros_like(akm)
            for pair in range(slot // (2 * TILE)):
                srows = slice(slot + pair * 16, slot + pair * 16 + 16)
                extra = None
                for odd in range(2):
                    tile = pair * 2 + odd
                    rows = slice(tile * TILE, tile * TILE + TILE)
                    qs = spread_heads(jnp.concatenate([q[rows, lanes], q[srows, lanes]], axis=0), masks)
                    go = spread_heads(jnp.concatenate([gom[rows, lanes], gom[srows, lanes]], axis=0), masks)
                    kw = key_window(tile, lanes, kf, ke, kp)
                    vw = key_window(tile, lanes, vf, ve, vp)
                    p = prob[pair * 4 + quad * 2 + odd]
                    gprob = dot_nt(go, vw) * p.astype(F32)
                    gs = (gprob - p.astype(F32) * jnp.sum(gprob, axis=-1, keepdims=True)).astype(BF)
                    gqt = gather_heads(dot(gs, kw), masks) * 0.125
                    gq[rows, lanes] = gqt[:TILE].astype(BF)
                    extra = gqt[TILE:] if extra is None else extra + gqt[TILE:]
                    for place, got in ((0, dot_tn(gs, qs) * 0.125), (256, dot_tn(p, go))):
                        cols = slice(place, place + 256)
                        akm[tile * 8 : tile * 8 + 16, cols] += got[:16]
                        akf[tile * TILE : tile * TILE + KEYS - 16, cols] += got[16:]
                gq[srows, lanes] = extra.astype(BF)
            for out, place in ((gk, 0), (gv, 256)):
                cols = slice(place, place + 256)
                out[:mem_rows, lanes] = akm[8 : 8 + mem_rows, cols].astype(BF)
                out[mem_rows:, lanes] = akf[FRONT : FRONT + slot, cols].astype(BF)
        for name in ("gq", "gk", "gv"):
            send(near[name], far[name].at[pos])
        pm, inverse = pool_matrix(length, wide, slot)
        need("wk", "wv", "wq", "xh0")
        gmf = dot_nt(gk[:mem_rows], wk[...]) + dot_nt(gv[:mem_rows], wv[...])
        gm[...] = gmf.astype(BF)
        gc = dot_nt(gq[slot:], wq[...]) * inverse
        akf[:slot] = (dot_nt(gk[mem_rows:], wk[...]) + dot_nt(gv[mem_rows:], wv[...]) + dot_nt(gq[:slot], wq[...])
                      + unpool(pm, gc))
        spread = unpool(pm, gmf * inverse) if lower else None
        for i in range(0, slot, CHUNK):
            r = slice(i, i + CHUNK)
            w = akf[r]
            xhat = xh0[r].astype(F32)
            acc[G0] += fold8(w * xhat)
            acc[S0] += fold8(w)
            total = ga[r] + norm_back(w * gain[0:1], xhat, rs[r, 0:1])
            if lower:
                total = total + spread[i : i + CHUNK]
            gx[r] = total.astype(BF)
        acc[QB] += fold8(gq[...].astype(F32))
        acc[VB] += fold8(gv[...].astype(F32))
    else:
        gx[...] = jnp.zeros_like(gx)
        gm[...] = jnp.zeros_like(gm)
    small[...] = jnp.sum(acc[...], axis=1)
    for copy in stores:
        copy.wait()


ROOMS = 3


def full(shape):
    return pl.BlockSpec(shape, lambda *_: (0,) * len(shape))


def sds(shape, dtype):
    return jax.ShapeDtypeStruct(shape, dtype)


def cost_of(flops, moved, special=0):
    return pl.CostEstimate(flops=int(flops), bytes_accessed=int(moved), transcendentals=int(special))


def kernel_params():
    return pltpu.CompilerParams(vmem_limit_bytes=VMEM_LIMIT, dimension_semantics=("arbitrary",))


FAR = pl.BlockSpec(memory_space=pl.ANY)


def window_scratch(slot, width):
    mem_rows = slot // 8
    one = [pltpu.VMEM((FRONT + slot + 16, width), BF), pltpu.VMEM((mem_rows, width), BF),
           pltpu.VMEM((mem_rows + 16, width), BF)]
    return one + one


def kept_shapes(slot, width, hid):
    every = slot + slot // 8
    shapes = [((every, width), BF), ((slot // 8, width), BF)] + [((every, width), BF)] * 3
    shapes += [((slot // TILE * (width // 256), 4 * ROWS, KEYS), BF), ((every, width), BF)] + [((slot, width), BF)] * 3
    return shapes + [((slot, 128), F32)] + [((slot, hid), BF)] * 2 + [((slot, width), BF)]


def grad_shapes(slot, width, hid):
    every = slot + slot // 8
    return [((slot, width), BF), ((slot, hid), BF)] + [((every, width), BF)] * 4


def forward(weights, utt, lower, scalars, frames, memory, kept):
    (gain, shift, wq, wk, wv, qvb, wo, ob, wu, ub, wd, db) = weights
    _, slot, width = frames.shape
    hid = wu.shape[1]
    mem_rows = slot // 8
    every = slot + mem_rows
    entry = utt if lower else 0
    shapes = kept_shapes(slot, width, hid)
    near = [memory, gain, shift, wq, wk, wv, qvb, ob, ub, db]
    ins = [frames] + near + [wo, wu, wd]
    in_specs = [pl.BlockSpec((None, slot, width), lambda *_: (entry, 0, 0))] + [full(a.shape) for a in near] + [FAR] * 3
    extra = list(kept) if kept is not None else []
    aliases = {len(scalars) + len(ins) + i: i for i in range(len(extra))}
    vmem = lambda pair: pltpu.VMEM(*pair)
    scratch = [vmem(s) for s in shapes] + [vmem((w.shape, BF)) for w in (wo, wu, wd)] + window_scratch(slot, width) + [
        pltpu.VMEM((slot, width), F32), pltpu.SemaphoreType.DMA((3,)), pltpu.SemaphoreType.DMA((len(KEPT),)),
        pltpu.VMEM((8, 128), BF)]
    res = pl.pallas_call(
        functools.partial(forward_kernel, utt, lower),
        grid_spec=pltpu.PrefetchScalarGridSpec(
            num_scalar_prefetch=len(scalars), grid=(1,), in_specs=in_specs + [FAR] * len(extra),
            out_specs=[FAR] * len(KEPT) + [full((slot, width)), full((mem_rows, width))], scratch_shapes=scratch),
        out_shape=[sds((ROOMS,) + s, t) for s, t in shapes] + [sds((slot, width), BF), sds((mem_rows, width), BF)],
        input_output_aliases=aliases, compiler_params=kernel_params(),
        cost_estimate=cost_of(8 * every * width * width + 4 * slot * width * hid, 30 << 20, slot * hid * 2),
    )(*scalars, *ins, *extra)
    return res[-2], res[-1], res[: len(KEPT)]


def backward(weights, utt, lower, parts, scalars, cot, gmem, ga, kept, grads):
    do_ffn, do_att = parts
    (gain, shift, wq, wk, wv, qvb, wo, ob, wu, ub, wd, db) = weights
    _, slot, width = cot.shape
    hid = wu.shape[1]
    mem_rows = slot // 8
    every = slot + mem_rows
    entry = 0 if lower else utt
    kinds = dict(zip(KEPT, kept_shapes(slot, width, hid)))
    shapes = grad_shapes(slot, width, hid)
    ga_spec = full((slot, width)) if ga is not None else full((8, 128))
    ga_in = ga if ga is not None else jnp.zeros((8, 128), F32)
    ins = [cot, gmem, ga_in, gain, wq, wk, wv, wo, wu, wd] + list(kept)
    in_specs = [pl.BlockSpec((None, slot, width), lambda *_: (entry, 0, 0)), full(gmem.shape), ga_spec, full(gain.shape)]
    in_specs += [FAR] * (6 + len(kept))
    names = [g for g in GRADS if (do_ffn and g in GRADS[:3]) or (do_att and g in GRADS[2:])]
    extra = [grads[g] for g in names if grads[g] is not None]
    aliases = {}
    for i, g in enumerate(names):
        if grads[g] is not None:
            aliases[len(scalars) + len(ins) + len(aliases)] = i
    every_kind = dict(zip(GRADS, shapes))
    vmem = lambda pair: pltpu.VMEM(*pair)
    scratch = [vmem(s) for s in shapes] + [vmem((w.shape, BF)) for w in (wq, wk, wv, wo, wu, wd)]
    scratch += [vmem(kinds[name]) for name in ("q", "k", "v", "prob", "xh0", "xh1", "rs", "gp", "xh2")]
    scratch += window_scratch(slot, width)
    scratch += [pltpu.VMEM((every, width), BF), pltpu.VMEM((FRONT + slot + 16, width), F32),
                pltpu.VMEM((mem_rows + 16, width), F32), pltpu.VMEM((16, 8, width), F32),
                pltpu.SemaphoreType.DMA((16,)), pltpu.SemaphoreType.DMA((8,))]
    ga_out = (slot, width) if do_ffn else (8, 128)
    flops = (4 * slot * width * hid if do_ffn else 0) + (8 * every * width * width if do_att else 0)
    res = pl.pallas_call(
        functools.partial(backward_kernel, utt, lower, do_ffn, do_att),
        grid_spec=pltpu.PrefetchScalarGridSpec(
            num_scalar_prefetch=len(scalars), grid=(1,), in_specs=in_specs + [FAR] * len(extra),
            out_specs=[FAR] * len(names) + [full((slot, width)), full((mem_rows, width)), full(ga_out), full((16, width))],
            scratch_shapes=scratch),
        out_shape=[sds((ROOMS,) + every_kind[g][0], BF) for g in names] + [
            sds((slot, width), BF), sds((mem_rows, width), BF), sds(ga_out, F32), sds((16, width), F32)],
        input_output_aliases=aliases, compiler_params=kernel_params(),
        cost_estimate=cost_of(flops, 20 << 20),
    )(*scalars, *ins, *extra)
    grads = dict(grads)
    grads.update(zip(names, res))
    gx, gm, ga, small = res[len(names) :]
    return grads, gx, gm, ga, small


LANES_OUT = 4
STAGES = 4


def emit_group(value, me, more, out, part):
    part[...] = value
    sub = jnp.bitwise_and(me, LANES_OUT - 1)
    rows = value.shape[0] // LANES_OUT
    for r in range(LANES_OUT):
        got = part[pl.ds(pl.multiple_of(jnp.bitwise_xor(sub, r) * rows, rows), rows)]
        if more is not None:
            got = got + more[0, r].astype(F32)
        out[0, r] = got.astype(out.dtype)


def pair_weights(has_more, me_ref, left, right, *refs):
    more = refs[0] if has_more else None
    out, part = refs[-2:]
    emit_group(sum(dot_tn(left[u], right[u]) for u in range(left.shape[0])), me_ref[0], more, out, part)


def ffn_group_grads(slots, groups, chunk_left, me, left, right, more):
    _, slot, _ = left.shape
    width = min(left.shape[2], right.shape[2])
    low, count = groups
    place = lambda j, me: jnp.bitwise_xor(j + low, jnp.right_shift(me[0], 2))
    whole = pl.BlockSpec((slots, slot, width), lambda j, me: (0, 0, 0))
    chunk = pl.BlockSpec((slots, slot, width), lambda j, me: (0, 0, place(j, me)))
    block = (1, LANES_OUT, width // LANES_OUT, width)
    out_spec = pl.BlockSpec(block, lambda j, me: (j, 0, 0, 0))
    extra = [] if more is None else [more]
    return pl.pallas_call(
        functools.partial(pair_weights, more is not None),
        grid_spec=pltpu.PrefetchScalarGridSpec(
            num_scalar_prefetch=1, grid=(count,),
            in_specs=[chunk if chunk_left else whole, whole if chunk_left else chunk] + [out_spec] * len(extra),
            out_specs=out_spec,
            scratch_shapes=[pltpu.VMEM((width, width), F32)]),
        out_shape=sds((count,) + block[1:], BF),
        compiler_params=pltpu.CompilerParams(vmem_limit_bytes=VMEM_LIMIT, dimension_semantics=("arbitrary",)),
        cost_estimate=cost_of(2 * slots * slot * count * width * width, 2 * slots * slot * (count + 1) * width),
    )(me, left, right, *extra)


def attention_weights(low, has_more, me_ref, uc, mem, mix, gq, gk, gv, gz, *refs):
    more = refs[0] if has_more else None
    out, part = refs[-2:]
    slots, every, width = uc.shape
    mem_rows = every // 9
    slot = every - mem_rows
    me = me_ref[0]
    which = jnp.bitwise_xor(pl.program_id(0) + low, jnp.right_shift(me, 2))

    @pl.when(which == 0)
    def _():
        part[...] = sum(dot_tn(uc[u], gq[u]) for u in range(slots))

    for place, ref in ((1, gk), (2, gv)):
        @pl.when(which == place)
        def _():
            part[...] = sum(dot_tn(mem[u], ref[u, :mem_rows]) + dot_tn(uc[u, :slot], ref[u, mem_rows:])
                            for u in range(slots))

    @pl.when(which == 3)
    def _():
        part[...] = sum(dot_tn(mix[u], gz[u]) for u in range(slots))

    sub = jnp.bitwise_and(me, LANES_OUT - 1)
    rows = width // LANES_OUT
    for r in range(LANES_OUT):
        got = part[pl.ds(pl.multiple_of(jnp.bitwise_xor(sub, r) * rows, rows), rows)]
        if more is not None:
            got = got + more[0, r].astype(F32)
        out[0, r] = got.astype(out.dtype)


def attention_group_grads(slots, groups, me, arrays, more):
    _, every, width = arrays[0].shape
    low, count = groups
    block = (1, LANES_OUT, width // LANES_OUT, width)
    out_spec = pl.BlockSpec(block, lambda j, me: (j, 0, 0, 0))
    extra = [] if more is None else [more]
    return pl.pallas_call(
        functools.partial(attention_weights, low, more is not None),
        grid_spec=pltpu.PrefetchScalarGridSpec(
            num_scalar_prefetch=1, grid=(count,),
            in_specs=[pl.BlockSpec((slots,) + a.shape[1:], lambda j, me: (0, 0, 0)) for a in arrays]
            + [out_spec] * len(extra),
            out_specs=out_spec,
            scratch_shapes=[pltpu.VMEM((width, width), F32)]),
        out_shape=sds((count,) + block[1:], BF),
        compiler_params=pltpu.CompilerParams(vmem_limit_bytes=VMEM_LIMIT, dimension_semantics=("arbitrary",)),
        cost_estimate=cost_of(2 * count * slots * every * width * width, 16 * slots * every * width),
    )(me, *arrays, *extra)


def restore_group(own, far, me, value):
    gme = jnp.right_shift(me, 2)
    sub = jnp.bitwise_and(me, LANES_OUT - 1)
    rows = own.shape[2]
    place = jnp.bitwise_xor(pl.program_id(0), gme)
    half = own.shape[0]
    for ref, low in ((own, 0), (far, half)):
        @pl.when((place >= low) & (place < low + half))
        def _():
            for r in range(LANES_OUT):
                value(r, ref[place - low, jnp.bitwise_xor(sub, r)].astype(F32))


def restore_wide(me_ref, own, far, out):
    rows = own.shape[2]

    def put(r, got):
        out[0, r * rows : (r + 1) * rows] = got

    restore_group(own, far, me_ref[0], put)


def restore_square(me_ref, own, far, *outs):
    rows = own.shape[2]

    def put(r, got):
        for matrix, out in enumerate(outs):
            @pl.when(pl.program_id(0) == matrix)
            def _():
                out[0, r * rows : (r + 1) * rows] = got

    restore_group(own, far, me_ref[0], put)


def restore(me, own, far, kind):
    half, _, rows, width = own.shape
    whole = pl.BlockSpec(own.shape, lambda j, me: (0, 0, 0, 0))
    groups = 2 * half
    if kind == "down":
        body, shapes = restore_wide, [(1, groups * width, width)]
        specs = [pl.BlockSpec((1, width, width), lambda j, me: (0, j, 0))]
    elif kind == "up":
        body, shapes = restore_wide, [(1, width, groups * width)]
        specs = [pl.BlockSpec((1, width, width), lambda j, me: (0, 0, j))]
    else:
        body, shapes = restore_square, [(1, width, width)] * groups
        specs = [pl.BlockSpec((1, width, width), lambda j, me: (0, 0, 0))] * groups
    return pl.pallas_call(
        body,
        grid_spec=pltpu.PrefetchScalarGridSpec(num_scalar_prefetch=1, grid=(groups,), in_specs=[whole, whole],
                                               out_specs=specs),
        out_shape=[sds(s, F32) for s in shapes],
        compiler_params=pltpu.CompilerParams(vmem_limit_bytes=VMEM_LIMIT, dimension_semantics=("arbitrary",)),
        cost_estimate=cost_of(0, 6 * groups * width * width),
    )(me, own, far)


def swap(value, bit):
    n = lax.axis_size("dp")
    return lax.ppermute(value, "dp", [(i, i ^ (1 << bit)) for i in range(n)])


def finish_sum(value, extra_bits):
    added = lambda a, b: (a.astype(F32) + b.astype(F32)).astype(BF)
    for bit in range(1, STAGES):
        half = value.shape[0] // 2
        value = added(value[:half], swap(value[half:], bit))
    for bit in extra_bits:
        value = added(value, swap(value, bit))
    for bit in reversed(range(1, STAGES)):
        value = jnp.concatenate([value, swap(value, bit)], axis=0)
    return value


def shifted(block, axis, distance):
    devices = range(lax.axis_size(axis))
    route = [(i - distance, i) for i in devices if i - distance in devices]
    return lax.ppermute(block, axis, route)


def on_device(ends, lengths, seg_group, norm_gain, norm_shift, w_query, w_key, w_value, qv_bias, w_out, out_bias,
              w_up, up_bias, w_down, down_bias):
    weights = (norm_gain[0], norm_shift[0], w_query[0], w_key[0], w_value[0], qv_bias[0], w_out[0], out_bias,
               w_up[0], up_bias, w_down[0], down_bias)
    section = lax.axis_index("section")
    first = section == 0
    slots = lengths.shape[0]
    width = ends.shape[2]
    slot = ends.shape[1] // slots
    mem_rows = slot // 8
    hid = w_up.shape[2]
    local = ends.reshape(slots, slot, width)
    lower = [(jnp.where(first, b, ROOMS - 1).astype(jnp.int32).reshape(1), lengths, seg_group) for b in range(slots)]
    upper = [(jnp.where(first, ROOMS - 1, b).astype(jnp.int32).reshape(1), lengths, seg_group) for b in range(slots)]
    blank = jnp.zeros((mem_rows, width), BF)

    bits = lax.axis_size("dp").bit_length() - 1
    place = lax.axis_index("dp").astype(jnp.int32)
    me = sum((jnp.bitwise_and(jnp.right_shift(place, s), 1) << (STAGES - 1 - s)) for s in range(STAGES)).reshape(1)

    def sum_groups(value):
        shape = value.shape
        return finish_sum(value.reshape((-1,) + shape[2:]), range(STAGES, bits)).reshape(shape)

    def ffn_sums(g, gd, h, gf):
        far_down = swap(ffn_group_grads(slots, (2, 2), True, me, g, gd, None), 0)
        far_up = swap(ffn_group_grads(slots, (2, 2), False, me, h, gf, None), 0)
        down = sum_groups(ffn_group_grads(slots, (0, 2), True, me, g, gd, far_down))
        return down, sum_groups(ffn_group_grads(slots, (0, 2), False, me, h, gf, far_up))

    kept = None
    sent = []
    for b in range(slots):
        y, memory, kept = forward(weights, b, True, lower[b], local, blank, kept)
        sent.append(shifted((y, memory), "section", 1))
    finals = []
    for b in range(slots):
        y, _, kept = forward(weights, b, False, upper[b], sent[b][0][None], sent[b][1], kept)
        finals.append(y)

    held = dict(zip(KEPT, kept))
    grads = dict.fromkeys(GRADS)
    smalls = [[], []]
    sent = []
    for b in range(slots):
        grads, gx, gm, _, small = backward(weights, b, False, (True, True), upper[b], local, blank, None, kept, grads)
        smalls[1].append(small)
        sent.append(shifted((gx, gm), "section", -1))
    inputs_back = []
    for b in range(slots):
        cot, gmem = sent[b][0][None], sent[b][1]
        if b < slots - 1:
            grads, gx, gm, _, small = backward(weights, b, True, (True, True), lower[b], cot, gmem, None, kept, grads)
        else:
            grads, _, _, ga, small = backward(weights, b, True, (True, False), lower[b], cot, gmem, None, kept, grads)
            smalls[0].append(small)
            down, up = ffn_sums(held["g"], grads["gd"], held["h"], grads["gf"])
            grads, gx, gm, _, small = backward(weights, b, True, (False, True), lower[b], cot, gmem, ga, kept, grads)
        smalls[0].append(small)
        inputs_back.append(gx)
    arrays = tuple(held[name] for name in ("uc", "mem", "mix")) + tuple(grads[name] for name in ("gq", "gk", "gv", "gz"))
    away = attention_group_grads(slots, (2, 2), me, arrays, None)
    square = sum_groups(attention_group_grads(slots, (0, 2), me, arrays, swap(away, 0)))

    small = jnp.where(first, sum(smalls[0]), sum(smalls[1]))
    for bit in range(bits):
        small = small + swap(small, bit)
    ends_out = jnp.where(first, jnp.stack(inputs_back), jnp.stack(finals)).reshape(1, slots * slot, width)
    (down,) = restore(me, down, swap(down, 0), "down")
    (up,) = restore(me, up, swap(up, 0), "up")
    grad_q, grad_k, grad_v, grad_o = restore(me, square, swap(square, 0), "square")
    return (ends_out, small[None, 0:3], small[None, 3:6], grad_q, grad_k, grad_v, small[None, 6:8],
            grad_o, small[8:9], up, small[10 : 10 + hid // width].reshape(1, hid), down, small[9:10])


def solution(mesh):
    placed = (
        P("section", "dp", None), P("dp"), P("dp"),
        P("section", None, None), P("section", None, None), P("section", None, None), P("section", None, None),
        P("section", None, None), P("section", None, None), P("section", None, None), P("section", None),
        P("section", None, None), P("section", None), P("section", None, None), P("section", None),
    )
    return jax.shard_map(
        on_device,
        mesh=mesh,
        in_specs=placed,
        out_specs=(
            P("section", "dp", None), P("section", None, None), P("section", None, None), P("section", None, None),
            P("section", None, None), P("section", None, None), P("section", None, None), P("section", None, None),
            P("section", None), P("section", None, None), P("section", None), P("section", None, None),
            P("section", None),
        ),
        check_vma=False,
    )
```

```python
import functools
import jax
import jax.numpy as jnp
from jax import lax
from jax.experimental import pallas as pl
from jax.experimental.pallas import tpu as pltpu
from jax.sharding import PartitionSpec as P

LEFT = 30
RIGHT = 4
MEM = 4
TILE = 64
KEYS = 128
ROWS = 80
FRONT = 32
BF = jnp.bfloat16
F32 = jnp.float32
VMEM_LIMIT = 10 * 1024 * 1024


def dot(a, b):
    return lax.dot_general(a, b, (((1,), (0,)), ((), ())), preferred_element_type=F32)


def dot_nt(a, b):
    return lax.dot_general(a, b, (((1,), (1,)), ((), ())), preferred_element_type=F32)


def dot_tn(a, b):
    return lax.dot_general(a, b, (((0,), (0,)), ((), ())), preferred_element_type=F32)


def normed(value):
    center = value - jnp.mean(value, axis=-1, keepdims=True)
    rs = lax.rsqrt(jnp.mean(center * center, axis=-1, keepdims=True) + 1e-05)
    return center * rs, rs


def norm_back(w, xhat, rs):
    return (w - jnp.mean(w, axis=-1, keepdims=True) - xhat * jnp.mean(w * xhat, axis=-1, keepdims=True)) * rs


def fold8(value):
    rows, width = value.shape
    return jnp.sum(value.reshape(rows // 8, 8, width), axis=0)


def gelu_parts(f):
    phi = 0.5 + 0.5 * lax.erf(f * 0.7071067811865476)
    return f * phi, phi + f * (jnp.exp(f * f * -0.5) * 0.3989422804014327)


def seg_sizes(wide):
    return jnp.where(wide, 16, 8).astype(jnp.int32), jnp.where(wide, 4, 8).astype(jnp.int32)


def pool_matrix(length, wide, slot):
    seg, per = seg_sizes(wide)
    rows = slot // 8
    e = lax.broadcasted_iota(jnp.int32, (rows, slot), 0)
    t = lax.broadcasted_iota(jnp.int32, (rows, slot), 1)
    r = jnp.bitwise_and(e, 7)
    start = jnp.right_shift(e, 3) * TILE + r * seg
    inside = (t >= start) & (t < start + seg) & (t < length) & (r < per)
    e1 = lax.broadcasted_iota(jnp.int32, (rows, 1), 0)
    r1 = jnp.bitwise_and(e1, 7)
    start1 = jnp.right_shift(e1, 3) * TILE + r1 * seg
    count = jnp.where(r1 < per, jnp.clip(length - start1, 0, seg), 0)
    inverse = 1.0 / jnp.maximum(count, 1).astype(F32)
    return jnp.where(inside, 1.0, 0.0).astype(BF), inverse


def unpool(matrix, value):
    high = value.astype(BF)
    low = (value - high.astype(F32)).astype(BF)
    return dot_tn(jnp.concatenate([matrix, matrix], axis=0), jnp.concatenate([high, low], axis=0))


def tile_bias(tile, odd, length, wide):
    seg, per = seg_sizes(wide)
    row = lax.broadcasted_iota(jnp.int32, (ROWS, 1), 0)
    col = lax.broadcasted_iota(jnp.int32, (1, KEYS), 1)
    anchor = tile * TILE
    is_frame = row < TILE
    extra = row - TILE
    shift = jnp.where(wide, 4, 3).astype(jnp.int32)
    r = jnp.where(is_frame, jnp.right_shift(row, shift), jnp.bitwise_and(extra, 7))
    owned = is_frame | ((jnp.right_shift(extra, 3) == odd) & (r < per))
    key = col - (16 + FRONT)
    low = jnp.where(owned, r * seg - LEFT, 100000)
    high = jnp.minimum(r * seg + seg + RIGHT, length - anchor)
    frame_ok = (key >= jnp.maximum(low, -anchor)) & (key < high) & (col >= 16)
    c = jnp.bitwise_and(col, 7)
    slot = jnp.where((col < 16) & (c < per), jnp.where(col < 8, c - per, c), -100000)
    slot = jnp.where((col < 8) & (anchor == 0), -100000, slot)
    mem_ok = (slot >= r - MEM) & (slot < jnp.where(is_frame, r, -100000))
    return jnp.where(frame_ok | mem_ok, 0.0, -1e30).astype(F32)


def head_masks(rows):
    lane = jnp.right_shift(lax.broadcasted_iota(jnp.int32, (rows, 256), 1), 6)
    return [lane == h for h in range(4)]


def spread_heads(tile, masks):
    zero = jnp.zeros_like(tile)
    return jnp.concatenate([jnp.where(m, tile, zero) for m in masks], axis=0)


def gather_heads(stack, masks):
    total = jnp.where(masks[0], stack[:ROWS], 0.0)
    for h in range(1, 4):
        total = jnp.where(masks[h], stack[h * ROWS : (h + 1) * ROWS], total)
    return total


def key_window(tile, lanes, frames_ref, even_ref, pad_ref):
    first = tile // 2 * 16
    memory = even_ref[first : first + 16, lanes] if tile % 2 else pad_ref[first : first + 16, lanes]
    return jnp.concatenate([memory, frames_ref[tile * TILE : tile * TILE + KEYS - 16, lanes]], axis=0)


def fill_windows(all_rows, frames_ref, even_ref, pad_ref, mem_rows, slot):
    width = all_rows.shape[1]
    memory = all_rows[:mem_rows].astype(F32)
    blank = jnp.zeros((8, width), F32)
    even_ref[...] = memory.astype(BF)
    pad_ref[...] = jnp.concatenate([blank, memory, blank], axis=0).astype(BF)
    frames_ref[:FRONT] = jnp.zeros((FRONT, width), BF)
    frames_ref[FRONT : FRONT + slot] = all_rows[mem_rows:].astype(BF)
    frames_ref[FRONT + slot :] = jnp.zeros((16, width), BF)


CHUNK = 32
G0, G1, G2, S0, S1, S2, QB, VB, OB, DB, UB = range(11)
KEPT = ("uc", "mem", "q", "k", "v", "prob", "mix", "xh0", "xh1", "h", "rs", "g", "gp", "xh2")
GRADS = ("gd", "gf", "gz", "gq", "gk", "gv")


def grads_of(do_ffn, do_att):
    return [g for g in GRADS if (do_ffn and g in GRADS[:3]) or (do_att and g in GRADS[2:])]


def forward_kernel(utt, lower, fetch, on_ref, vec, x_ref, wq, wk, wv, wo, wu, wd, *refs):
    n = len(KEPT)
    slots = (on_ref.shape[0] - 1) // 2
    loads = []
    if fetch:
        sem = refs[-1]
        far = (x_ref.at[utt], wq, wk, wv, wo, wu, wd)
        x_ref, wq, wk, wv, wo, wu, wd = refs[-8:-1]
        refs = refs[:-8]
        loads = [pltpu.make_async_copy(a, b, sem.at[i])
                 for i, (a, b) in enumerate(zip(far, (x_ref, wq, wk, wv, wo, wu, wd)))]
        for copy in loads:
            copy.start()
    elif lower:
        x_ref = x_ref.at[utt]
    kf, ke, kp, vf, ve, vp, after = refs[-7:]
    y = refs[-8]
    near = {name: ref.at[utt] for name, ref in zip(KEPT, refs[-8 - n : -8])}
    slot, width = after.shape
    mem_rows = slot // 8
    length = on_ref[1 + utt]
    wide = on_ref[1 + slots + utt] == 1
    gain, shift, qvb, ob, db = vec.at[0:3], vec.at[3:6], vec.at[6:8], vec.at[8:9], vec.at[9:10]

    def need(*which):
        for i in which if fetch else ():
            loads[i].wait()

    uc, mem, q, k, v, prob, mix = (near[name] for name in KEPT[:7])
    rs = near["rs"]
    lane = lax.broadcasted_iota(jnp.int32, (1, 128), 1)
    phase = pl.when(on_ref[0] == 1)

    need(0)

    @phase
    def _():
        for i in range(0, slot, CHUNK):
            r = slice(i, i + CHUNK)
            xhat, scale = normed(x_ref[r].astype(F32))
            near["xh0"][r] = xhat.astype(BF)
            uc[r] = (xhat * gain[0:1] + shift[0:1]).astype(BF)
            rs[r] = jnp.broadcast_to(scale, (CHUNK, 128))
        pm, inverse = pool_matrix(length, wide, slot)
        uc[slot:] = (dot(pm, uc[:slot]) * inverse).astype(BF)
        if lower:
            mem[...] = (dot(pm, x_ref[:slot]) * inverse).astype(BF)
        else:
            mem[...] = x_ref[slot:]


    need(1, 2, 3)

    @phase
    def _():
        q[...] = (dot(uc[...], wq[...]) + qvb[0:1]).astype(BF)
        k[:mem_rows] = dot(mem[...], wk[...]).astype(BF)
        k[mem_rows:] = dot(uc[:slot], wk[...]).astype(BF)
        v[:mem_rows] = (dot(mem[...], wv[...]) + qvb[1:2]).astype(BF)
        v[mem_rows:] = (dot(uc[:slot], wv[...]) + qvb[1:2]).astype(BF)
        fill_windows(k[...], kf, ke, kp, mem_rows, slot)
        fill_windows(v[...], vf, ve, vp, mem_rows, slot)


    @phase
    def _():
        masks = head_masks(ROWS)
        for pair in range(slot // (2 * TILE)):
            srows = slice(slot + pair * 16, slot + pair * 16 + 16)
            biases = [tile_bias(pair * 2 + odd, odd, length, wide) for odd in range(2)]
            for quad in range(width // 256):
                lanes = slice(quad * 256, quad * 256 + 256)
                extra = None
                for odd in range(2):
                    tile = pair * 2 + odd
                    rows = slice(tile * TILE, tile * TILE + TILE)
                    qs = spread_heads(jnp.concatenate([q[rows, lanes], q[srows, lanes]], axis=0), masks)
                    kw = key_window(tile, lanes, kf, ke, kp)
                    vw = key_window(tile, lanes, vf, ve, vp)
                    s = dot_nt(qs, kw).reshape(4, ROWS, KEYS) * 0.125 + biases[odd][None]
                    peak = jnp.maximum(jnp.max(s, axis=-1, keepdims=True), -1e29)
                    e = jnp.exp(s - peak)
                    total = jnp.sum(e, axis=-1, keepdims=True)
                    p = (e * (1.0 / jnp.maximum(total, 1e-30))).astype(BF).reshape(4 * ROWS, KEYS)
                    prob[pair * 4 + quad * 2 + odd] = p
                    o = gather_heads(dot(p, vw), masks)
                    mix[rows, lanes] = o[:TILE].astype(BF)
                    extra = o[TILE:] if extra is None else extra + o[TILE:]
                mix[srows, lanes] = extra.astype(BF)


    need(4)

    @phase
    def _():
        z = dot(mix[...], wo[...]) + ob[...]
        y[slot:] = z[slot:].astype(BF)
        after[...] = z[:slot]
        for i in range(0, slot, CHUNK):
            r = slice(i, i + CHUNK)
            a = x_ref[r].astype(F32) + after[r]
            after[r] = a + db[...]
            xhat, scale = normed(a)
            near["xh1"][r] = xhat.astype(BF)
            near["h"][r] = (xhat * gain[1:2] + shift[1:2]).astype(BF)
            rs[r] = jnp.where(lane == 0, rs[r], jnp.broadcast_to(scale, (CHUNK, 128)))

    need(5, 6)
    for c in range(wu.shape[1] // 512):
        cols = slice(c * 512, c * 512 + 512)

        @phase
        def _():
            act, slope = gelu_parts(dot(near["h"][...], wu[:, cols]) + vec[UB + c : UB + c + 1])
            act = act.astype(BF)
            near["g"][:, cols] = act
            near["gp"][:, cols] = slope.astype(BF)
            after[...] += dot(act, wd[cols])

    @phase
    def _():
        for i in range(0, slot, CHUNK):
            r = slice(i, i + CHUNK)
            xhat, scale = normed(after[r])
            near["xh2"][r] = xhat.astype(BF)
            rs[r] = jnp.where(lane == 2, jnp.broadcast_to(scale, (CHUNK, 128)), rs[r])
            t = lax.broadcasted_iota(jnp.int32, (CHUNK, 1), 0) + i
            valid = jnp.where(t < length, 1.0, 0.0)
            y[r] = ((xhat * gain[2:3] + shift[2:3]) * valid).astype(BF)


def backward_kernel(utt, lower, do_ffn, do_att, on_ref, vec, cot, ga_in,
                    wq, wk, wv, wo, wu, wd, *refs):
    kept = {name: ref.at[utt] for name, ref in zip(KEPT, refs)}
    names = grads_of(do_ffn, do_att)
    kf, ke, kp, vf, ve, vp, gom, akf, akm, acc = refs[-10:]
    gx, ga_out, small = refs[-13:-10]
    near = {name: ref.at[utt] for name, ref in zip(names, refs[-13 - len(names) : -13])}
    slot, width = kept["xh0"].shape
    mem_rows = slot // 8
    slots = (on_ref.shape[0] - 1) // 2
    length = on_ref[1 + utt]
    wide = on_ref[1 + slots + utt] == 1
    gain = vec.at[0:3]
    cot = cot if lower else cot.at[utt]
    gz = near["gz"]
    q, k, v, prob, xh0, xh1, xh2, rs, gp = (kept[name] for name in
                                            ("q", "k", "v", "prob", "xh0", "xh1", "xh2", "rs", "gp"))
    phase = pl.when(on_ref[0] == 1)

    @phase
    def _():
        acc[...] = jnp.zeros_like(acc)

    if do_ffn:
        gd, gf = near["gd"], near["gf"]
        ga = ga_out

        @phase
        def _():
            for i in range(0, slot, CHUNK):
                r = slice(i, i + CHUNK)
                t = lax.broadcasted_iota(jnp.int32, (CHUNK, 1), 0) + i
                gy = cot[r].astype(F32) * jnp.where(t < length, 1.0, 0.0)
                xhat = xh2[r].astype(F32)
                acc[G2] += fold8(gy * xhat)
                acc[S2] += fold8(gy)
                ga2 = norm_back(gy * gain[2:3], xhat, rs[r, 2:3])
                ga[r] = ga2
                low = ga2.astype(BF)
                gd[r] = low
                acc[DB] += fold8(low.astype(F32))

        for c in range(wu.shape[1] // 512):
            cols = slice(c * 512, c * 512 + 512)

            @phase
            def _():
                gfl = (dot_nt(gd[...], wd[cols]) * gp[:, cols].astype(F32)).astype(BF)
                gf[:, cols] = gfl
                acc[UB + c] += fold8(gfl.astype(F32))
                part = dot_nt(gfl, wu[:, cols])
                if c == 0:
                    akf[:slot] = part
                else:
                    akf[:slot] += part

        @phase
        def _():
            for i in range(0, slot, CHUNK):
                r = slice(i, i + CHUNK)
                back = akf[r]
                xhat = xh1[r].astype(F32)
                acc[G1] += fold8(back * xhat)
                acc[S1] += fold8(back)
                total = ga[r] + norm_back(back * gain[1:2], xhat, rs[r, 1:2])
                ga[r] = total
                low = total.astype(BF)
                gz[r] = low
                acc[OB] += fold8(low.astype(F32))
    else:
        ga = ga_in
    if do_att:
        gq, gk, gv = near["gq"], near["gk"], near["gv"]

        @phase
        def _():
            gz[slot:] = cot[slot:] if lower else jnp.zeros((mem_rows, width), BF)
            if lower:
                acc[OB] += fold8(cot[slot:].astype(F32))
            gom[...] = dot_nt(gz[...], wo[...]).astype(BF)
            fill_windows(k[...], kf, ke, kp, mem_rows, slot)
            fill_windows(v[...], vf, ve, vp, mem_rows, slot)

        for quad in range(width // 256):
            lanes = slice(quad * 256, quad * 256 + 256)

            @phase
            def _():
                masks = head_masks(ROWS)
                akf[...] = jnp.zeros_like(akf)
                akm[...] = jnp.zeros_like(akm)
                for pair in range(slot // (2 * TILE)):
                    srows = slice(slot + pair * 16, slot + pair * 16 + 16)
                    extra = None
                    for odd in range(2):
                        tile = pair * 2 + odd
                        rows = slice(tile * TILE, tile * TILE + TILE)
                        qs = spread_heads(jnp.concatenate([q[rows, lanes], q[srows, lanes]], axis=0), masks)
                        go = spread_heads(jnp.concatenate([gom[rows, lanes], gom[srows, lanes]], axis=0), masks)
                        kw = key_window(tile, lanes, kf, ke, kp)
                        vw = key_window(tile, lanes, vf, ve, vp)
                        p = prob[pair * 4 + quad * 2 + odd]
                        gprob = dot_nt(go, vw) * p.astype(F32)
                        gs = (gprob - p.astype(F32) * jnp.sum(gprob, axis=-1, keepdims=True)).astype(BF)
                        gqt = gather_heads(dot(gs, kw), masks) * 0.125
                        gq[rows, lanes] = gqt[:TILE].astype(BF)
                        extra = gqt[TILE:] if extra is None else extra + gqt[TILE:]
                        for place, got in ((0, dot_tn(gs, qs) * 0.125), (256, dot_tn(p, go))):
                            cols = slice(place, place + 256)
                            akm[tile * 8 : tile * 8 + 16, cols] += got[:16]
                            akf[tile * TILE : tile * TILE + KEYS - 16, cols] += got[16:]
                    gq[srows, lanes] = extra.astype(BF)
                for out, place in ((gk, 0), (gv, 256)):
                    cols = slice(place, place + 256)
                    out[:mem_rows, lanes] = akm[8 : 8 + mem_rows, cols].astype(BF)
                    out[mem_rows:, lanes] = akf[FRONT : FRONT + slot, cols].astype(BF)

        @phase
        def _():
            pm, inverse = pool_matrix(length, wide, slot)
            gmf = dot_nt(gk[:mem_rows], wk[...]) + dot_nt(gv[:mem_rows], wv[...])
            gx[slot:] = gmf.astype(BF)
            gc = dot_nt(gq[slot:], wq[...]) * inverse
            akf[:slot] = (dot_nt(gk[mem_rows:], wk[...]) + dot_nt(gv[mem_rows:], wv[...])
                          + dot_nt(gq[:slot], wq[...]) + unpool(pm, gc))
            spread = unpool(pm, gmf * inverse) if lower else None
            for i in range(0, slot, CHUNK):
                r = slice(i, i + CHUNK)
                w = akf[r]
                xhat = xh0[r].astype(F32)
                acc[G0] += fold8(w * xhat)
                acc[S0] += fold8(w)
                total = ga[r] + norm_back(w * gain[0:1], xhat, rs[r, 0:1])
                if lower:
                    total = total + spread[i : i + CHUNK]
                gx[r] = total.astype(BF)
            acc[QB] += fold8(gq[...].astype(F32))
            acc[VB] += fold8(gv[...].astype(F32))

    @phase
    def _():
        small[...] = jnp.sum(acc[...], axis=1)


def sds(shape, dtype):
    return jax.ShapeDtypeStruct(shape, dtype)


def cost_of(flops, moved, special=0):
    return pl.CostEstimate(flops=int(flops), bytes_accessed=int(moved), transcendentals=int(special))


def kernel_params(limit=VMEM_LIMIT):
    return pltpu.CompilerParams(vmem_limit_bytes=limit)


SCALAR = pl.BlockSpec(memory_space=pltpu.SMEM)
NEAR = pl.BlockSpec(memory_space=pltpu.VMEM)
FAR = pl.BlockSpec(memory_space=pl.ANY)
FETCH_LIMIT = 20 * 1024 * 1024


def window_scratch(slot, width):
    mem_rows = slot // 8
    one = [pltpu.VMEM((FRONT + slot + 16, width), BF), pltpu.VMEM((mem_rows, width), BF),
           pltpu.VMEM((mem_rows + 16, width), BF)]
    return one + one


def kept_shapes(slot, width, hid):
    every = slot + slot // 8
    shapes = [((every, width), BF), ((slot // 8, width), BF)] + [((every, width), BF)] * 3
    shapes += [((slot // TILE * (width // 256), 4 * ROWS, KEYS), BF), ((every, width), BF)] + [((slot, width), BF)] * 3
    return shapes + [((slot, 128), F32)] + [((slot, hid), BF)] * 2 + [((slot, width), BF)]


def grad_shapes(slot, width, hid):
    every = slot + slot // 8
    return [((slot, width), BF), ((slot, hid), BF)] + [((every, width), BF)] * 4


def forward(weights, utt, lower, scalars, slots, frames, kept, fetch=False):
    vec, wq, wk, wv, wo, wu, wd = weights
    width, hid = wu.shape
    slot = frames.shape[1] if lower else frames.shape[0] // 9 * 8
    every = slot + slot // 8
    shapes = kept_shapes(slot, width, hid)
    ins = [scalars, vec, frames, wq, wk, wv, wo, wu, wd]
    extra = list(kept) if kept is not None else []
    big = ins[3:]
    fetched = [pltpu.VMEM((slot, width), BF)] + [pltpu.VMEM(a.shape, BF) for a in big] + [pltpu.SemaphoreType.DMA((7,))]
    res = pl.pallas_call(
        functools.partial(forward_kernel, utt, lower, fetch),
        in_specs=[SCALAR, NEAR] + [FAR if fetch else NEAR] * 7 + [NEAR] * len(extra),
        out_specs=[NEAR] * (len(KEPT) + 1),
        out_shape=[sds((slots,) + s, t) for s, t in shapes] + [sds((every, width), BF)],
        scratch_shapes=window_scratch(slot, width) + [pltpu.VMEM((slot, width), F32)] + (fetched if fetch else []),
        input_output_aliases={len(ins) + i: i for i in range(len(extra))},
        compiler_params=kernel_params(FETCH_LIMIT if fetch else VMEM_LIMIT),
        cost_estimate=cost_of(8 * every * width * width + 4 * slot * width * hid, 30 << 20, slot * hid * 2),
    )(*ins, *extra)
    return res[-1], res[: len(KEPT)]


def backward(weights, utt, lower, parts, scalars, slots, cot, ga, kept, grads):
    do_ffn, do_att = parts
    vec, wq, wk, wv, wo, wu, wd = weights
    width, hid = wu.shape
    slot = cot.shape[0] // 9 * 8 if lower else cot.shape[1]
    mem_rows = slot // 8
    every = slot + mem_rows
    shapes = dict(zip(GRADS, grad_shapes(slot, width, hid)))
    names = grads_of(do_ffn, do_att)
    ins = [scalars, vec, cot, ga if ga is not None else vec, wq, wk, wv, wo, wu, wd] + list(kept)
    extra = [grads[g] for g in names if grads[g] is not None]
    aliases = {len(ins) + i: place for i, place in enumerate(p for p, g in enumerate(names) if grads[g] is not None)}
    tiny = (8, 128)
    out = [sds((slots,) + shapes[g][0], BF) for g in names]
    out += [sds((every, width) if do_att else tiny, BF), sds((slot, width) if do_ffn else tiny, F32), sds((16, width), F32)]
    flops = (4 * slot * width * hid if do_ffn else 0) + (8 * every * width * width if do_att else 0)
    res = pl.pallas_call(
        functools.partial(backward_kernel, utt, lower, do_ffn, do_att),
        in_specs=[SCALAR] + [NEAR] * (len(ins) - 1 + len(extra)),
        out_specs=[NEAR] * len(out), out_shape=out,
        scratch_shapes=window_scratch(slot, width) + [
            pltpu.VMEM((every, width), BF), pltpu.VMEM((FRONT + slot + 16, width), F32),
            pltpu.VMEM((mem_rows + 16, width), F32), pltpu.VMEM((16, 8, width), F32)],
        input_output_aliases=aliases, compiler_params=kernel_params(), cost_estimate=cost_of(flops, 20 << 20),
    )(*ins, *extra)
    grads = dict(grads)
    grads.update(zip(names, res))
    gx, ga, small = res[len(names) :]
    return grads, gx, ga, small


SMALL_LIMIT = 20 * 1024 * 1024
LANES_OUT = 4
STAGES = 4


def emit_group(value, me, more, out, part, j):
    if value is not None:
        part[...] = value
    sub = jnp.bitwise_and(me, LANES_OUT - 1)
    rows = part.shape[0] // LANES_OUT
    for r in range(LANES_OUT):
        got = part[pl.ds(pl.multiple_of(jnp.bitwise_xor(sub, r) * rows, rows), rows)]
        if more is not None:
            got = got + more[j, r].astype(F32)
        out[j, r] = got.astype(out.dtype)


def pair_weights(chunk_left, low, has_more, me_ref, left, right, *refs):
    more = refs[0] if has_more else None
    out, part = refs[-2:]
    me = me_ref[0]
    for j in range(out.shape[0]):
        start = jnp.bitwise_xor(j + low, jnp.right_shift(me, 2)) * 512
        chunk = pl.ds(pl.multiple_of(start, 512), 512)
        value = sum(dot_tn(left[u, :, chunk] if chunk_left else left[u], right[u] if chunk_left else right[u, :, chunk])
                    for u in range(left.shape[0]))
        emit_group(value, me, more, out, part, j)


def group_call(body, me, arrays, more, count, width, flops):
    extra = [] if more is None else [more]
    return pl.pallas_call(
        body,
        in_specs=[SCALAR] + [NEAR] * (len(arrays) + len(extra)),
        out_specs=NEAR,
        out_shape=sds((count, LANES_OUT, width // LANES_OUT, width), BF),
        scratch_shapes=[pltpu.VMEM((width, width), F32)],
        compiler_params=kernel_params(),
        cost_estimate=cost_of(flops, 4 << 20),
    )(me, *arrays, *extra)


def ffn_group_grads(groups, chunk_left, me, left, right, more):
    slots, slot, _ = left.shape
    width = min(left.shape[2], right.shape[2])
    low, count = groups
    return group_call(functools.partial(pair_weights, chunk_left, low, more is not None), me, (left, right), more, count,
                      width, 2 * slots * slot * count * width * width)


def attention_weights(low, has_more, me_ref, uc, mem, mix, gq, gk, gv, gz, *refs):
    more = refs[0] if has_more else None
    out, part = refs[-2:]
    slots, every, width = uc.shape
    mem_rows = every // 9
    slot = every - mem_rows
    me = me_ref[0]
    for j in range(out.shape[0]):
        which = jnp.bitwise_xor(j + low, jnp.right_shift(me, 2))

        @pl.when(which == 0)
        def _():
            part[...] = sum(dot_tn(uc[u], gq[u]) for u in range(slots))

        for place, ref in ((1, gk), (2, gv)):
            @pl.when(which == place)
            def _():
                part[...] = sum(dot_tn(mem[u], ref[u, :mem_rows]) + dot_tn(uc[u, :slot], ref[u, mem_rows:])
                                for u in range(slots))

        @pl.when(which == 3)
        def _():
            part[...] = sum(dot_tn(mix[u], gz[u]) for u in range(slots))

        emit_group(None, me, more, out, part, j)


def attention_group_grads(groups, me, arrays, more):
    slots, every, width = arrays[0].shape
    low, count = groups
    return group_call(functools.partial(attention_weights, low, more is not None), me, arrays, more, count, width,
                      2 * count * slots * every * width * width)


def restore_group(own, far, me, value):
    gme = jnp.right_shift(me, 2)
    sub = jnp.bitwise_and(me, LANES_OUT - 1)
    rows = own.shape[2]
    place = jnp.bitwise_xor(pl.program_id(0), gme)
    half = own.shape[0]
    for ref, low in ((own, 0), (far, half)):
        @pl.when((place >= low) & (place < low + half))
        def _():
            for r in range(LANES_OUT):
                value(r, ref[place - low, jnp.bitwise_xor(sub, r)].astype(F32))


def restore_wide(me_ref, own, far, out):
    rows = own.shape[2]

    def put(r, got):
        out[0, r * rows : (r + 1) * rows] = got

    restore_group(own, far, me_ref[0], put)


def restore_square(me_ref, own, far, *outs):
    rows = own.shape[2]

    def put(r, got):
        for matrix, out in enumerate(outs):
            @pl.when(pl.program_id(0) == matrix)
            def _():
                out[0, r * rows : (r + 1) * rows] = got

    restore_group(own, far, me_ref[0], put)


def restore(me, own, far, kind):
    half, _, rows, width = own.shape
    whole = pl.BlockSpec(own.shape, lambda j, me: (0, 0, 0, 0))
    groups = 2 * half
    if kind == "down":
        body, shapes = restore_wide, [(1, groups * width, width)]
        specs = [pl.BlockSpec((1, width, width), lambda j, me: (0, j, 0))]
    elif kind == "up":
        body, shapes = restore_wide, [(1, width, groups * width)]
        specs = [pl.BlockSpec((1, width, width), lambda j, me: (0, 0, j))]
    else:
        body, shapes = restore_square, [(1, width, width)] * groups
        specs = [pl.BlockSpec((1, width, width), lambda j, me: (0, 0, 0))] * groups
    return pl.pallas_call(
        body,
        grid_spec=pltpu.PrefetchScalarGridSpec(num_scalar_prefetch=1, grid=(groups,), in_specs=[whole, whole],
                                               out_specs=specs),
        out_shape=[sds(s, F32) for s in shapes],
        compiler_params=kernel_params(SMALL_LIMIT),
        cost_estimate=cost_of(0, 6 * groups * width * width),
    )(me, own, far)


def swap(value, bit):
    n = lax.axis_size("dp")
    return lax.ppermute(value, "dp", [(i, i ^ (1 << bit)) for i in range(n)])


def added(a, b):
    return (a.astype(F32) + b.astype(F32)).astype(BF)


class Order:
    def __init__(self):
        self.last = None

    def after(self, *values):
        if self.last is not None:
            values = lax.optimization_barrier((*values, self.last))[:-1]
        return values

    def made(self, value):
        self.last = value


class Sum:
    def __init__(self, order, bits, value, small=None):
        self.order = order
        self.bits = bits
        self.value = value.reshape((-1,) + value.shape[2:])
        self.small = small
        self.stage = 1
        self.launch()

    def launch(self):
        if self.stage < STAGES:
            half = self.value.shape[0] // 2
            out, self.value = self.value[half:], self.value[:half]
            if self.small is not None:
                width = out.shape[-1]
                high = lax.reduce_precision(self.small, exponent_bits=8, mantissa_bits=7)
                parts = [out.reshape(-1, width), high.astype(BF), (self.small - high).astype(BF)]
                out = jnp.concatenate(parts, axis=0)
            bit = self.stage
        else:
            out = self.value
            bit = 2 * STAGES - 1 - self.stage
        self.order.made(out)
        self.got = swap(out, bit)

    def step(self):
        got, value = self.order.after(self.got, self.value)
        if self.stage < STAGES:
            if self.small is not None:
                lines = value.shape[0] * value.shape[1]
                rows = self.small.shape[0]
                self.small = self.small + got[lines : lines + rows].astype(F32) + got[lines + rows :].astype(F32)
                got = got[:lines].reshape(value.shape)
            value = added(value, got)
            if self.stage == STAGES - 1:
                for bit in range(STAGES, self.bits):
                    value = added(value, swap(value, bit))
                    if self.small is not None:
                        self.small = self.small + swap(self.small, bit)
        else:
            value = jnp.concatenate([value, got], axis=0)
        self.value = value
        self.stage += 1
        self.launch()

    def restore(self, me, kind):
        groups = lambda v: v.reshape((-1, LANES_OUT) + v.shape[1:])
        got, value = self.order.after(self.got, self.value)
        return restore(me, groups(value), groups(got), kind)


def shifted(block, axis, distance):
    devices = range(lax.axis_size(axis))
    route = [(i - distance, i) for i in devices if i - distance in devices]
    return lax.ppermute(block, axis, route)


def on_device(ends, lengths, seg_group, norm_gain, norm_shift, w_query, w_key, w_value, qv_bias, w_out, out_bias,
              w_up, up_bias, w_down, down_bias):
    section = lax.axis_index("section")
    first = section == 0
    slots = lengths.shape[0]
    width = ends.shape[2]
    slot = ends.shape[1] // slots
    hid = w_up.shape[2]
    local = ends.reshape(slots, slot, width)
    section = section.astype(jnp.int32).reshape(1)
    lower = jnp.concatenate([1 - section, lengths, seg_group])
    upper = jnp.concatenate([section, lengths, seg_group])

    bits = lax.axis_size("dp").bit_length() - 1
    place = lax.axis_index("dp").astype(jnp.int32)
    me = sum((jnp.bitwise_and(jnp.right_shift(place, s), 1) << (STAGES - 1 - s)) for s in range(STAGES)).reshape(1)

    vec = jnp.concatenate([norm_gain[0], norm_shift[0], qv_bias[0], out_bias, down_bias, up_bias.reshape(-1, width)], axis=0)
    vec, lower, upper, me, first = lax.optimization_barrier((vec, lower, upper, me, first))
    weights = (vec, w_query[0], w_key[0], w_value[0], w_out[0], w_up[0], w_down[0])

    kept = None
    sent = []
    for b in range(slots):
        y, kept = forward(weights, b, True, lower, slots, local, kept, b == 0)
        sent.append(shifted(y, "section", 1))
    finals = []
    grads = dict.fromkeys(GRADS)
    smalls = [[], []]
    back = []
    for b in range(slots):
        y, kept = forward(weights, b, False, upper, slots, sent[b], kept)
        finals.append(y)
        grads, gx, _, small = backward(weights, b, False, (True, True), upper, slots, local, None, kept, grads)
        smalls[1].append(small)
        back.append(shifted(gx, "section", -1))
    held = dict(zip(KEPT, kept))
    firsts = []
    for b in range(slots - 1):
        grads, gx, _, small = backward(weights, b, True, (True, True), lower, slots, back[b], None, kept, grads)
        smalls[0].append(small)
        firsts.append(gx)
    b = slots - 1
    grads, _, ga, small = backward(weights, b, True, (True, False), lower, slots, back[b], None, kept, grads)
    smalls[0].append(small)

    order = Order()
    wide_pairs = ((True, held["g"], grads["gd"]), (False, held["h"], grads["gf"]))
    far = [swap(ffn_group_grads((2, 2), side, me, left, right, None), 0) for side, left, right in wide_pairs]
    down, up = [ffn_group_grads((0, 2), side, me, left, right, more)
                for (side, left, right), more in zip(wide_pairs, far)]
    ga, down, up = lax.optimization_barrier((ga, down, up))
    down = Sum(order, bits, down)
    up = Sum(order, bits, up)
    grads, gx, _, small = backward(weights, b, True, (False, True), lower, slots, back[b], ga, kept, grads)
    smalls[0].append(small)
    firsts.append(gx)
    small = jnp.where(first, sum(smalls[0]), sum(smalls[1]))

    down.step()
    names = ("gq", "gk", "gv", "gz")
    arrays = [held[name] for name in ("uc", "mem", "mix")] + [grads[name] for name in names]
    arrays[-1], small = order.after(arrays[-1], small)
    away = swap(attention_group_grads((2, 2), me, arrays, None), 0)
    small = small + swap(small, 0)
    down.step()
    away, small = order.after(away, small)
    square = Sum(order, bits, attention_group_grads((0, 2), me, arrays, away), small)
    for stream in (up, down, up, down, square, up, down, square, up, square, up, square, down):
        stream.step()
    (grad_down,) = down.restore(me, "down")
    square.step()
    up.step()
    (grad_up,) = up.restore(me, "up")
    square.step()
    grad_q, grad_k, grad_v, grad_o = square.restore(me, "square")
    small = square.small
    ends_out = jnp.where(first, jnp.stack([gx[:slot] for gx in firsts]), jnp.stack([y[:slot] for y in finals]))
    ends_out = ends_out.reshape(1, slots * slot, width)
    return (ends_out, small[None, 0:3], small[None, 3:6], grad_q, grad_k, grad_v, small[None, 6:8],
            grad_o, small[8:9], grad_up, small[10 : 10 + hid // width].reshape(1, hid), grad_down, small[9:10])


def solution(mesh):
    placed = (
        P("section", "dp", None), P("dp"), P("dp"),
        P("section", None, None), P("section", None, None), P("section", None, None), P("section", None, None),
        P("section", None, None), P("section", None, None), P("section", None, None), P("section", None),
        P("section", None, None), P("section", None), P("section", None, None), P("section", None),
    )
    return jax.shard_map(
        on_device,
        mesh=mesh,
        in_specs=placed,
        out_specs=(
            P("section", "dp", None), P("section", None, None), P("section", None, None), P("section", None, None),
            P("section", None, None), P("section", None, None), P("section", None, None), P("section", None, None),
            P("section", None), P("section", None, None), P("section", None), P("section", None, None),
            P("section", None),
        ),
        check_vma=False,
    )
```

```python
import functools
import jax
import jax.numpy as jnp
from jax import lax
from jax.experimental import pallas as pl
from jax.experimental.pallas import tpu as pltpu
from jax.sharding import PartitionSpec as P

LEFT = 30
RIGHT = 4
MEM = 4
TILE = 64
KEYS = 128
ROWS = 80
FRONT = 32
BF = jnp.bfloat16
F32 = jnp.float32
VMEM_LIMIT = 5 * 1024 * 1024


def dot(a, b):
    return lax.dot_general(a, b, (((1,), (0,)), ((), ())), preferred_element_type=F32)


def dot_nt(a, b):
    return lax.dot_general(a, b, (((1,), (1,)), ((), ())), preferred_element_type=F32)


def dot_tn(a, b):
    return lax.dot_general(a, b, (((0,), (0,)), ((), ())), preferred_element_type=F32)


def normed(value):
    center = value - jnp.mean(value, axis=-1, keepdims=True)
    rs = lax.rsqrt(jnp.mean(center * center, axis=-1, keepdims=True) + 1e-05)
    return center * rs, rs


def norm_back(w, xhat, rs):
    return (w - jnp.mean(w, axis=-1, keepdims=True) - xhat * jnp.mean(w * xhat, axis=-1, keepdims=True)) * rs


def fold8(value):
    rows, width = value.shape
    return jnp.sum(value.reshape(rows // 8, 8, width), axis=0)


def gelu_parts(f):
    phi = 0.5 + 0.5 * lax.erf(f * 0.7071067811865476)
    return f * phi, phi + f * (jnp.exp(f * f * -0.5) * 0.3989422804014327)


def seg_sizes(wide):
    return jnp.where(wide, 16, 8).astype(jnp.int32), jnp.where(wide, 4, 8).astype(jnp.int32)


def pool_matrix(length, wide, slot):
    seg, per = seg_sizes(wide)
    rows = slot // 8
    e = lax.broadcasted_iota(jnp.int32, (rows, slot), 0)
    t = lax.broadcasted_iota(jnp.int32, (rows, slot), 1)
    r = jnp.bitwise_and(e, 7)
    start = jnp.right_shift(e, 3) * TILE + r * seg
    inside = (t >= start) & (t < start + seg) & (t < length) & (r < per)
    e1 = lax.broadcasted_iota(jnp.int32, (rows, 1), 0)
    r1 = jnp.bitwise_and(e1, 7)
    start1 = jnp.right_shift(e1, 3) * TILE + r1 * seg
    count = jnp.where(r1 < per, jnp.clip(length - start1, 0, seg), 0)
    inverse = 1.0 / jnp.maximum(count, 1).astype(F32)
    return jnp.where(inside, 1.0, 0.0).astype(BF), inverse


def unpool(matrix, value):
    high = value.astype(BF)
    low = (value - high.astype(F32)).astype(BF)
    return dot_tn(jnp.concatenate([matrix, matrix], axis=0), jnp.concatenate([high, low], axis=0))


def tile_bias(tile, odd, length, wide):
    seg, per = seg_sizes(wide)
    row = lax.broadcasted_iota(jnp.int32, (ROWS, 1), 0)
    col = lax.broadcasted_iota(jnp.int32, (1, KEYS), 1)
    anchor = tile * TILE
    is_frame = row < TILE
    extra = row - TILE
    shift = jnp.where(wide, 4, 3).astype(jnp.int32)
    r = jnp.where(is_frame, jnp.right_shift(row, shift), jnp.bitwise_and(extra, 7))
    owned = is_frame | ((jnp.right_shift(extra, 3) == odd) & (r < per))
    key = col - (16 + FRONT)
    low = jnp.where(owned, r * seg - LEFT, 100000)
    high = jnp.minimum(r * seg + seg + RIGHT, length - anchor)
    frame_ok = (key >= jnp.maximum(low, -anchor)) & (key < high) & (col >= 16)
    c = jnp.bitwise_and(col, 7)
    slot = jnp.where((col < 16) & (c < per), jnp.where(col < 8, c - per, c), -100000)
    slot = jnp.where((col < 8) & (anchor == 0), -100000, slot)
    mem_ok = (slot >= r - MEM) & (slot < jnp.where(is_frame, r, -100000))
    return jnp.where(frame_ok | mem_ok, 0.0, -1e30).astype(F32)


def head_masks(rows):
    lane = jnp.right_shift(lax.broadcasted_iota(jnp.int32, (rows, 256), 1), 6)
    return [lane == h for h in range(4)]


def spread_heads(tile, masks):
    zero = jnp.zeros_like(tile)
    return jnp.concatenate([jnp.where(m, tile, zero) for m in masks], axis=0)


def gather_heads(stack, masks):
    total = jnp.where(masks[0], stack[:ROWS], 0.0)
    for h in range(1, 4):
        total = jnp.where(masks[h], stack[h * ROWS : (h + 1) * ROWS], total)
    return total


def key_window(tile, lanes, frames_ref, even_ref, pad_ref):
    first = tile // 2 * 16
    memory = even_ref[first : first + 16, lanes] if tile % 2 else pad_ref[first : first + 16, lanes]
    return jnp.concatenate([memory, frames_ref[tile * TILE : tile * TILE + KEYS - 16, lanes]], axis=0)


def fill_windows(all_rows, frames_ref, even_ref, pad_ref, mem_rows, slot):
    width = all_rows.shape[1]
    memory = all_rows[:mem_rows].astype(F32)
    blank = jnp.zeros((8, width), F32)
    even_ref[...] = memory.astype(BF)
    pad_ref[...] = jnp.concatenate([blank, memory, blank], axis=0).astype(BF)
    frames_ref[:FRONT] = jnp.zeros((FRONT, width), BF)
    frames_ref[FRONT : FRONT + slot] = all_rows[mem_rows:].astype(BF)
    frames_ref[FRONT + slot :] = jnp.zeros((16, width), BF)


CHUNK = 32
G0, G1, G2, S0, S1, S2, QB, VB, OB, DB, UB = range(11)
KEPT = ("uc", "mem", "q", "k", "v", "prob", "mix", "xh0", "xh1", "h", "rs", "g", "gp", "xh2")
GRADS = ("gd", "gf", "gz", "gq", "gk", "gv")


def grads_of(do_ffn, do_att):
    return [g for g in GRADS if (do_ffn and g in GRADS[:3]) or (do_att and g in GRADS[2:])]


def forward_kernel(utt, lower, on_ref, vec, ub, x_ref, wq, wk, wv, wo, wu, wd, *refs):
    n = len(KEPT)
    slots = (on_ref.shape[0] - 1) // 2
    if lower:
        x_ref = x_ref.at[utt]
    kf, ke, kp, vf, ve, vp, after = refs[-7:]
    y = refs[-8]
    near = {name: ref.at[utt] for name, ref in zip(KEPT, refs[-8 - n : -8])}
    slot, width = after.shape
    mem_rows = slot // 8
    length = on_ref[1 + utt]
    wide = on_ref[1 + slots + utt] == 1
    gain, shift, qvb, ob, db = vec.at[0:3], vec.at[3:6], vec.at[6:8], vec.at[8:9], vec.at[9:10]

    uc, mem, q, k, v, prob, mix = (near[name] for name in KEPT[:7])
    rs = near["rs"]
    lane = lax.broadcasted_iota(jnp.int32, (1, 128), 1)
    phase = pl.when(on_ref[0] == 1)


    @phase
    def _():
        for i in range(0, slot, CHUNK):
            r = slice(i, i + CHUNK)
            xhat, scale = normed(x_ref[r].astype(F32))
            near["xh0"][r] = xhat.astype(BF)
            uc[r] = (xhat * gain[0:1] + shift[0:1]).astype(BF)
            rs[r] = jnp.broadcast_to(scale, (CHUNK, 128))
        pm, inverse = pool_matrix(length, wide, slot)
        uc[slot:] = (dot(pm, uc[:slot]) * inverse).astype(BF)
        if lower:
            mem[...] = (dot(pm, x_ref[:slot]) * inverse).astype(BF)
        else:
            mem[...] = x_ref[slot:]


    @phase
    def _():
        q[...] = (dot(uc[...], wq[...]) + qvb[0:1]).astype(BF)
        k[:mem_rows] = dot(mem[...], wk[...]).astype(BF)
        k[mem_rows:] = dot(uc[:slot], wk[...]).astype(BF)
        v[:mem_rows] = (dot(mem[...], wv[...]) + qvb[1:2]).astype(BF)
        v[mem_rows:] = (dot(uc[:slot], wv[...]) + qvb[1:2]).astype(BF)
        fill_windows(k[...], kf, ke, kp, mem_rows, slot)
        fill_windows(v[...], vf, ve, vp, mem_rows, slot)


    @phase
    def _():
        masks = head_masks(ROWS)
        for pair in range(slot // (2 * TILE)):
            srows = slice(slot + pair * 16, slot + pair * 16 + 16)
            biases = [tile_bias(pair * 2 + odd, odd, length, wide) for odd in range(2)]
            for quad in range(width // 256):
                lanes = slice(quad * 256, quad * 256 + 256)
                extra = None
                for odd in range(2):
                    tile = pair * 2 + odd
                    rows = slice(tile * TILE, tile * TILE + TILE)
                    qs = spread_heads(jnp.concatenate([q[rows, lanes], q[srows, lanes]], axis=0), masks)
                    kw = key_window(tile, lanes, kf, ke, kp)
                    vw = key_window(tile, lanes, vf, ve, vp)
                    s = dot_nt(qs, kw).reshape(4, ROWS, KEYS) * 0.125 + biases[odd][None]
                    peak = jnp.maximum(jnp.max(s, axis=-1, keepdims=True), -1e29)
                    e = jnp.exp(s - peak)
                    total = jnp.sum(e, axis=-1, keepdims=True)
                    p = (e * (1.0 / jnp.maximum(total, 1e-30))).astype(BF).reshape(4 * ROWS, KEYS)
                    prob[pair * 4 + quad * 2 + odd] = p
                    o = gather_heads(dot(p, vw), masks)
                    mix[rows, lanes] = o[:TILE].astype(BF)
                    extra = o[TILE:] if extra is None else extra + o[TILE:]
                mix[srows, lanes] = extra.astype(BF)


    @phase
    def _():
        z = dot(mix[...], wo[...]) + ob[...]
        y[slot:] = z[slot:].astype(BF)
        after[...] = z[:slot]
        for i in range(0, slot, CHUNK):
            r = slice(i, i + CHUNK)
            a = x_ref[r].astype(F32) + after[r]
            after[r] = a + db[...]
            xhat, scale = normed(a)
            near["xh1"][r] = xhat.astype(BF)
            near["h"][r] = (xhat * gain[1:2] + shift[1:2]).astype(BF)
            rs[r] = jnp.where(lane == 0, rs[r], jnp.broadcast_to(scale, (CHUNK, 128)))

    for c in range(wu.shape[1] // 512):
        cols = slice(c * 512, c * 512 + 512)

        @phase
        def _():
            act, slope = gelu_parts(dot(near["h"][...], wu[:, cols]) + ub[:, cols])
            act = act.astype(BF)
            near["g"][:, cols] = act
            near["gp"][:, cols] = slope.astype(BF)
            after[...] += dot(act, wd[cols])

    @phase
    def _():
        for i in range(0, slot, CHUNK):
            r = slice(i, i + CHUNK)
            xhat, scale = normed(after[r])
            near["xh2"][r] = xhat.astype(BF)
            rs[r] = jnp.where(lane == 2, jnp.broadcast_to(scale, (CHUNK, 128)), rs[r])
            t = lax.broadcasted_iota(jnp.int32, (CHUNK, 1), 0) + i
            valid = jnp.where(t < length, 1.0, 0.0)
            y[r] = ((xhat * gain[2:3] + shift[2:3]) * valid).astype(BF)


def backward_kernel(utt, lower, do_ffn, do_att, on_ref, vec, cot, ga_in,
                    wq, wk, wv, wo, wu, wd, *refs):
    kept = {name: ref.at[utt] for name, ref in zip(KEPT, refs)}
    names = grads_of(do_ffn, do_att)
    kf, ke, kp, vf, ve, vp, gom, akf, akm, acc = refs[-10:]
    gx, ga_out, small = refs[-13:-10]
    near = {name: ref.at[utt] for name, ref in zip(names, refs[-13 - len(names) : -13])}
    slot, width = kept["xh0"].shape
    mem_rows = slot // 8
    slots = (on_ref.shape[0] - 1) // 2
    length = on_ref[1 + utt]
    wide = on_ref[1 + slots + utt] == 1
    gain = vec.at[0:3]
    cot = cot if lower else cot.at[utt]
    gz = near["gz"]
    q, k, v, prob, xh0, xh1, xh2, rs, gp = (kept[name] for name in
                                            ("q", "k", "v", "prob", "xh0", "xh1", "xh2", "rs", "gp"))
    phase = pl.when(on_ref[0] == 1)

    @phase
    def _():
        acc[...] = jnp.zeros_like(acc)

    if do_ffn:
        gd, gf = near["gd"], near["gf"]
        ga = ga_out

        @phase
        def _():
            for i in range(0, slot, CHUNK):
                r = slice(i, i + CHUNK)
                t = lax.broadcasted_iota(jnp.int32, (CHUNK, 1), 0) + i
                gy = cot[r].astype(F32) * jnp.where(t < length, 1.0, 0.0)
                xhat = xh2[r].astype(F32)
                acc[G2] += fold8(gy * xhat)
                acc[S2] += fold8(gy)
                ga2 = norm_back(gy * gain[2:3], xhat, rs[r, 2:3])
                ga[r] = ga2
                low = ga2.astype(BF)
                gd[r] = low
                acc[DB] += fold8(low.astype(F32))

        for c in range(wu.shape[1] // 512):
            cols = slice(c * 512, c * 512 + 512)

            @phase
            def _():
                gfl = (dot_nt(gd[...], wd[cols]) * gp[:, cols].astype(F32)).astype(BF)
                gf[:, cols] = gfl
                acc[UB + c] += fold8(gfl.astype(F32))
                part = dot_nt(gfl, wu[:, cols])
                if c == 0:
                    akf[:slot] = part
                else:
                    akf[:slot] += part

        @phase
        def _():
            for i in range(0, slot, CHUNK):
                r = slice(i, i + CHUNK)
                back = akf[r]
                xhat = xh1[r].astype(F32)
                acc[G1] += fold8(back * xhat)
                acc[S1] += fold8(back)
                total = ga[r] + norm_back(back * gain[1:2], xhat, rs[r, 1:2])
                ga[r] = total
                low = total.astype(BF)
                gz[r] = low
                acc[OB] += fold8(low.astype(F32))
    else:
        ga = ga_in
    if do_att:
        gq, gk, gv = near["gq"], near["gk"], near["gv"]

        @phase
        def _():
            gz[slot:] = cot[slot:] if lower else jnp.zeros((mem_rows, width), BF)
            if lower:
                acc[OB] += fold8(cot[slot:].astype(F32))
            gom[...] = dot_nt(gz[...], wo[...]).astype(BF)
            fill_windows(k[...], kf, ke, kp, mem_rows, slot)
            fill_windows(v[...], vf, ve, vp, mem_rows, slot)

        for quad in range(width // 256):
            lanes = slice(quad * 256, quad * 256 + 256)

            @phase
            def _():
                masks = head_masks(ROWS)
                akf[...] = jnp.zeros_like(akf)
                akm[...] = jnp.zeros_like(akm)
                for pair in range(slot // (2 * TILE)):
                    srows = slice(slot + pair * 16, slot + pair * 16 + 16)
                    extra = None
                    for odd in range(2):
                        tile = pair * 2 + odd
                        rows = slice(tile * TILE, tile * TILE + TILE)
                        qs = spread_heads(jnp.concatenate([q[rows, lanes], q[srows, lanes]], axis=0), masks)
                        go = spread_heads(jnp.concatenate([gom[rows, lanes], gom[srows, lanes]], axis=0), masks)
                        kw = key_window(tile, lanes, kf, ke, kp)
                        vw = key_window(tile, lanes, vf, ve, vp)
                        p = prob[pair * 4 + quad * 2 + odd]
                        gprob = dot_nt(go, vw) * p.astype(F32)
                        gs = (gprob - p.astype(F32) * jnp.sum(gprob, axis=-1, keepdims=True)).astype(BF)
                        gqt = gather_heads(dot(gs, kw), masks) * 0.125
                        gq[rows, lanes] = gqt[:TILE].astype(BF)
                        extra = gqt[TILE:] if extra is None else extra + gqt[TILE:]
                        for place, got in ((0, dot_tn(gs, qs) * 0.125), (256, dot_tn(p, go))):
                            cols = slice(place, place + 256)
                            akm[tile * 8 : tile * 8 + 16, cols] += got[:16]
                            akf[tile * TILE : tile * TILE + KEYS - 16, cols] += got[16:]
                    gq[srows, lanes] = extra.astype(BF)
                for out, place in ((gk, 0), (gv, 256)):
                    cols = slice(place, place + 256)
                    out[:mem_rows, lanes] = akm[8 : 8 + mem_rows, cols].astype(BF)
                    out[mem_rows:, lanes] = akf[FRONT : FRONT + slot, cols].astype(BF)

        @phase
        def _():
            pm, inverse = pool_matrix(length, wide, slot)
            gmf = dot_nt(gk[:mem_rows], wk[...]) + dot_nt(gv[:mem_rows], wv[...])
            gx[slot:] = gmf.astype(BF)
            gc = dot_nt(gq[slot:], wq[...]) * inverse
            akf[:slot] = (dot_nt(gk[mem_rows:], wk[...]) + dot_nt(gv[mem_rows:], wv[...])
                          + dot_nt(gq[:slot], wq[...]) + unpool(pm, gc))
            spread = unpool(pm, gmf * inverse) if lower else None
            for i in range(0, slot, CHUNK):
                r = slice(i, i + CHUNK)
                w = akf[r]
                xhat = xh0[r].astype(F32)
                acc[G0] += fold8(w * xhat)
                acc[S0] += fold8(w)
                total = ga[r] + norm_back(w * gain[0:1], xhat, rs[r, 0:1])
                if lower:
                    total = total + spread[i : i + CHUNK]
                gx[r] = total.astype(BF)
            acc[QB] += fold8(gq[...].astype(F32))
            acc[VB] += fold8(gv[...].astype(F32))

    @phase
    def _():
        small[...] = jnp.sum(acc[...], axis=1)


def sds(shape, dtype):
    return jax.ShapeDtypeStruct(shape, dtype)


def cost_of(flops, moved, special=0):
    return pl.CostEstimate(flops=int(flops), bytes_accessed=int(moved), transcendentals=int(special))


def kernel_params(limit=VMEM_LIMIT):
    return pltpu.CompilerParams(vmem_limit_bytes=limit)


SCALAR = pl.BlockSpec(memory_space=pltpu.SMEM)
NEAR = pl.BlockSpec(memory_space=pltpu.VMEM)


def window_scratch(slot, width):
    mem_rows = slot // 8
    one = [pltpu.VMEM((FRONT + slot + 16, width), BF), pltpu.VMEM((mem_rows, width), BF),
           pltpu.VMEM((mem_rows + 16, width), BF)]
    return one + one


def kept_shapes(slot, width, hid):
    every = slot + slot // 8
    shapes = [((every, width), BF), ((slot // 8, width), BF)] + [((every, width), BF)] * 3
    shapes += [((slot // TILE * (width // 256), 4 * ROWS, KEYS), BF), ((every, width), BF)] + [((slot, width), BF)] * 3
    return shapes + [((slot, 128), F32)] + [((slot, hid), BF)] * 2 + [((slot, width), BF)]


def grad_shapes(slot, width, hid):
    every = slot + slot // 8
    return [((slot, width), BF), ((slot, hid), BF)] + [((every, width), BF)] * 4


def forward(weights, utt, lower, scalars, slots, frames, kept):
    vec, ub, wq, wk, wv, wo, wu, wd = weights
    width, hid = wu.shape
    slot = frames.shape[1] if lower else frames.shape[0] // 9 * 8
    every = slot + slot // 8
    shapes = kept_shapes(slot, width, hid)
    ins = [scalars, vec, ub, frames, wq, wk, wv, wo, wu, wd]
    extra = list(kept) if kept is not None else []
    out = [sds((slots,) + s, t) for s, t in shapes] + [sds((every, width), BF)]
    res = pl.pallas_call(
        functools.partial(forward_kernel, utt, lower),
        in_specs=[SCALAR] + [NEAR] * (len(ins) - 1 + len(extra)),
        out_specs=[NEAR] * len(out),
        out_shape=out,
        scratch_shapes=window_scratch(slot, width) + [pltpu.VMEM((slot, width), F32)],
        input_output_aliases={len(ins) + i: i for i in range(len(extra))},
        compiler_params=kernel_params(),
        cost_estimate=cost_of(8 * every * width * width + 4 * slot * width * hid, 30 << 20, slot * hid * 2),
    )(*ins, *extra)
    return res[-1], res[:-1]


def pass_on(values, out):
    out[...] = values[...]


def opening(values):
    return pl.pallas_call(
        pass_on, in_specs=[NEAR], out_specs=NEAR, out_shape=sds(values.shape, values.dtype),
        compiler_params=kernel_params(1 << 20), cost_estimate=cost_of(1e12, 1 << 30),
    )(values)


def backward(weights, utt, lower, parts, scalars, slots, cot, ga, kept, grads):
    do_ffn, do_att = parts
    vec, ub, wq, wk, wv, wo, wu, wd = weights
    width, hid = wu.shape
    slot = cot.shape[0] // 9 * 8 if lower else cot.shape[1]
    mem_rows = slot // 8
    every = slot + mem_rows
    shapes = dict(zip(GRADS, grad_shapes(slot, width, hid)))
    names = grads_of(do_ffn, do_att)
    ins = [scalars, vec, cot, ga if ga is not None else vec, wq, wk, wv, wo, wu, wd] + list(kept)
    extra = [grads[g] for g in names if grads[g] is not None]
    aliases = {len(ins) + i: place for i, place in enumerate(p for p, g in enumerate(names) if grads[g] is not None)}
    tiny = (8, 128)
    out = [sds((slots,) + shapes[g][0], BF) for g in names]
    out += [sds((every, width) if do_att else tiny, BF), sds((slot, width) if do_ffn else tiny, F32), sds((16, width), F32)]
    flops = (4 * slot * width * hid if do_ffn else 0) + (8 * every * width * width if do_att else 0)
    res = pl.pallas_call(
        functools.partial(backward_kernel, utt, lower, do_ffn, do_att),
        in_specs=[SCALAR] + [NEAR] * (len(ins) - 1 + len(extra)),
        out_specs=[NEAR] * len(out), out_shape=out,
        scratch_shapes=window_scratch(slot, width) + [
            pltpu.VMEM((every, width), BF), pltpu.VMEM((FRONT + slot + 16, width), F32),
            pltpu.VMEM((mem_rows + 16, width), F32), pltpu.VMEM((16, 8, width), F32)],
        input_output_aliases=aliases, compiler_params=kernel_params(), cost_estimate=cost_of(flops, 20 << 20),
    )(*ins, *extra)
    grads = dict(grads)
    grads.update(zip(names, res))
    gx, ga, small = res[len(names) :]
    return grads, gx, ga, small


SMALL_LIMIT = 6 * 1024 * 1024
LANES_OUT = 4
STAGES = 4


def emit_group(value, me, more, out, part, j):
    if value is not None:
        part[...] = value
    sub = jnp.bitwise_and(me, LANES_OUT - 1)
    rows = part.shape[0] // LANES_OUT
    for r in range(LANES_OUT):
        got = part[pl.ds(pl.multiple_of(jnp.bitwise_xor(sub, r) * rows, rows), rows)]
        if more is not None:
            got = got + more[j, r].astype(F32)
        out[j, r] = got.astype(out.dtype)


def pair_weights(chunk_left, low, has_more, me_ref, left, right, *refs):
    more = refs[0] if has_more else None
    out, part = refs[-2:]
    me = me_ref[0]
    for j in range(out.shape[0]):
        start = jnp.bitwise_xor(j + low, jnp.right_shift(me, 2)) * 512
        chunk = pl.ds(pl.multiple_of(start, 512), 512)
        value = sum(dot_tn(left[u, :, chunk] if chunk_left else left[u], right[u] if chunk_left else right[u, :, chunk])
                    for u in range(left.shape[0]))
        emit_group(value, me, more, out, part, j)


def group_call(body, me, arrays, more, count, width, flops):
    extra = [] if more is None else [more]
    return pl.pallas_call(
        body,
        in_specs=[SCALAR] + [NEAR] * (len(arrays) + len(extra)),
        out_specs=NEAR,
        out_shape=sds((count, LANES_OUT, width // LANES_OUT, width), BF),
        scratch_shapes=[pltpu.VMEM((width, width), F32)],
        compiler_params=kernel_params(),
        cost_estimate=cost_of(flops, 4 << 20),
    )(me, *arrays, *extra)


def ffn_group_grads(groups, chunk_left, me, left, right, more):
    slots, slot, _ = left.shape
    width = min(left.shape[2], right.shape[2])
    low, count = groups
    return group_call(functools.partial(pair_weights, chunk_left, low, more is not None), me, (left, right), more, count,
                      width, 2 * slots * slot * count * width * width)


def attention_weights(low, has_more, me_ref, uc, mem, mix, gq, gk, gv, gz, *refs):
    more = refs[0] if has_more else None
    out, part = refs[-2:]
    slots, every, width = uc.shape
    mem_rows = every // 9
    slot = every - mem_rows
    me = me_ref[0]
    for j in range(out.shape[0]):
        which = jnp.bitwise_xor(j + low, jnp.right_shift(me, 2))

        @pl.when(which == 0)
        def _():
            part[...] = sum(dot_tn(uc[u], gq[u]) for u in range(slots))

        for place, ref in ((1, gk), (2, gv)):
            @pl.when(which == place)
            def _():
                part[...] = sum(dot_tn(mem[u], ref[u, :mem_rows]) + dot_tn(uc[u, :slot], ref[u, mem_rows:])
                                for u in range(slots))

        @pl.when(which == 3)
        def _():
            part[...] = sum(dot_tn(mix[u], gz[u]) for u in range(slots))

        emit_group(None, me, more, out, part, j)


def attention_group_grads(groups, me, arrays, more):
    slots, every, width = arrays[0].shape
    low, count = groups
    return group_call(functools.partial(attention_weights, low, more is not None), me, arrays, more, count, width,
                      2 * count * slots * every * width * width)


def restore_group(own, far, me, value):
    gme = jnp.right_shift(me, 2)
    sub = jnp.bitwise_and(me, LANES_OUT - 1)
    rows = own.shape[2]
    place = jnp.bitwise_xor(pl.program_id(0), gme)
    half = own.shape[0]
    for ref, low in ((own, 0), (far, half)):
        @pl.when((place >= low) & (place < low + half))
        def _():
            for r in range(LANES_OUT):
                value(r, ref[place - low, jnp.bitwise_xor(sub, r)].astype(F32))


def restore_wide(me_ref, own, far, out):
    rows = own.shape[2]

    def put(r, got):
        out[0, r * rows : (r + 1) * rows] = got

    restore_group(own, far, me_ref[0], put)


def restore_square(me_ref, own, far, *outs):
    rows = own.shape[2]

    def put(r, got):
        for matrix, out in enumerate(outs):
            @pl.when(pl.program_id(0) == matrix)
            def _():
                out[0, r * rows : (r + 1) * rows] = got

    restore_group(own, far, me_ref[0], put)


def restore(me, own, far, kind):
    half, _, rows, width = own.shape
    whole = pl.BlockSpec(own.shape, lambda j, me: (0, 0, 0, 0))
    groups = 2 * half
    if kind == "down":
        body, shapes = restore_wide, [(1, groups * width, width)]
        specs = [pl.BlockSpec((1, width, width), lambda j, me: (0, j, 0))]
    elif kind == "up":
        body, shapes = restore_wide, [(1, width, groups * width)]
        specs = [pl.BlockSpec((1, width, width), lambda j, me: (0, 0, j))]
    else:
        body, shapes = restore_square, [(1, width, width)] * groups
        specs = [pl.BlockSpec((1, width, width), lambda j, me: (0, 0, 0))] * groups
    return pl.pallas_call(
        body,
        grid_spec=pltpu.PrefetchScalarGridSpec(num_scalar_prefetch=1, grid=(groups,), in_specs=[whole, whole],
                                               out_specs=specs),
        out_shape=[sds(s, F32) for s in shapes],
        compiler_params=kernel_params(SMALL_LIMIT),
        cost_estimate=cost_of(0, 6 * groups * width * width),
    )(me, own, far)


def swap(value, bit):
    n = lax.axis_size("dp")
    return lax.ppermute(value, "dp", [(i, i ^ (1 << bit)) for i in range(n)])


def added(a, b):
    return (a.astype(F32) + b.astype(F32)).astype(BF)


PLAN = "d1d2ududsudsusudsDsuUsS"
PATHS = {"d": (0, 1, 2, 3), "u": (0, 1, 2, 3), "s": (0, 1, 2, 3)}
KINDS = {"D": ("d", "down"), "U": ("u", "up"), "S": ("s", "square")}


class Order:
    def __init__(self):
        self.last = None

    def after(self, *values):
        if self.last is not None:
            values = lax.optimization_barrier((*values, self.last))[:-1]
        return values

    def made(self, value):
        self.last = value


class Sum:
    def __init__(self, order, path, bits, value, small=None):
        self.order = order
        self.path = path
        self.bits = bits
        self.value = value.reshape((-1,) + value.shape[2:])
        self.small = small
        self.stage = 1
        self.launch()

    def launch(self):
        if self.stage < STAGES:
            half = self.value.shape[0] // 2
            out, self.value = self.value[half:], self.value[:half]
            if self.small is not None:
                width = out.shape[-1]
                high = lax.reduce_precision(self.small, exponent_bits=8, mantissa_bits=7)
                parts = [out.reshape(-1, width), high.astype(BF), (self.small - high).astype(BF)]
                out = jnp.concatenate(parts, axis=0)
            bit = self.path[self.stage]
        else:
            out = self.value
            bit = self.path[2 * STAGES - 1 - self.stage]
        self.order.made(out)
        self.got = swap(out, bit)

    def step(self):
        got, value = self.order.after(self.got, self.value)
        if self.stage < STAGES:
            if self.small is not None:
                lines = value.shape[0] * value.shape[1]
                rows = self.small.shape[0]
                self.small = self.small + got[lines : lines + rows].astype(F32) + got[lines + rows :].astype(F32)
                got = got[:lines].reshape(value.shape)
            value = added(value, got)
            if self.stage == STAGES - 1:
                for bit in range(STAGES, self.bits):
                    value = added(value, swap(value, bit))
                    if self.small is not None:
                        self.small = self.small + swap(self.small, bit)
        else:
            value = jnp.concatenate([value, got], axis=0)
        self.value = value
        self.stage += 1
        self.launch()

    def restore(self, me, kind):
        groups = lambda v: v.reshape((-1, LANES_OUT) + v.shape[1:])
        got, value = self.order.after(self.got, self.value)
        outs = restore(me, groups(value), groups(got), kind)
        self.order.made(outs[0])
        return outs


def shifted(block, axis, distance):
    devices = range(lax.axis_size(axis))
    route = [(i - distance, i) for i in devices if i - distance in devices]
    return lax.ppermute(block, axis, route)


def on_device(ends, lengths, seg_group, norm_gain, norm_shift, w_query, w_key, w_value, qv_bias, w_out, out_bias,
              w_up, up_bias, w_down, down_bias):
    section = lax.axis_index("section")
    first = section == 0
    slots = lengths.shape[0]
    width = ends.shape[2]
    slot = ends.shape[1] // slots
    hid = w_up.shape[2]
    section = section.astype(jnp.int32).reshape(1)
    lower = jnp.concatenate([1 - section, lengths, seg_group])
    upper = jnp.concatenate([section, lengths, seg_group])

    bits = lax.axis_size("dp").bit_length() - 1
    place = lax.axis_index("dp").astype(jnp.int32)
    codes = {
        name: sum(jnp.bitwise_and(jnp.right_shift(place, bit), 1) << (STAGES - 1 - s) for s, bit in enumerate(path)).reshape(1)
        for name, path in PATHS.items()}

    vec = jnp.concatenate([norm_gain[0], norm_shift[0], qv_bias[0], out_bias, down_bias], axis=0)
    vec, lower, upper, codes, first = lax.optimization_barrier((vec, lower, upper, codes, first))
    vec = opening(vec)
    weights = (vec, up_bias, w_query[0], w_key[0], w_value[0], w_out[0], w_up[0], w_down[0])
    local = ends.reshape(slots, slot, width)

    kept = None
    sent = []
    for b in range(slots):
        y, kept = forward(weights, b, True, lower, slots, local, kept)
        sent.append(shifted(y, "section", 1))
    finals = []
    grads = dict.fromkeys(GRADS)
    smalls = [[], []]
    back = []
    for b in range(slots):
        y, kept = forward(weights, b, False, upper, slots, sent[b], kept)
        finals.append(y)
        grads, gx, _, small = backward(weights, b, False, (True, True), upper, slots, local, None, kept, grads)
        smalls[1].append(small)
        back.append(shifted(gx, "section", -1))
    held = dict(zip(KEPT, kept))
    firsts = []
    for b in range(slots - 1):
        grads, gx, _, small = backward(weights, b, True, (True, True), lower, slots, back[b], None, kept, grads)
        smalls[0].append(small)
        firsts.append(gx)
    b = slots - 1
    grads, _, ga, small = backward(weights, b, True, (True, False), lower, slots, back[b], None, kept, grads)
    smalls[0].append(small)

    order = Order()
    wide_pairs = ((True, codes["d"], held["g"], grads["gd"]), (False, codes["u"], held["h"], grads["gf"]))
    far = [swap(ffn_group_grads((2, 2), side, me, left, right, None), 0) for side, me, left, right in wide_pairs]
    down, up = [ffn_group_grads((0, 2), side, me, left, right, more)
                for (side, me, left, right), more in zip(wide_pairs, far)]
    ga, down, up = lax.optimization_barrier((ga, down, up))
    down = Sum(order, PATHS["d"], bits, down)
    up = Sum(order, PATHS["u"], bits, up)
    grads, gx, _, small = backward(weights, b, True, (False, True), lower, slots, back[b], ga, kept, grads)
    smalls[0].append(small)
    firsts.append(gx)
    small = jnp.where(first, sum(smalls[0]), sum(smalls[1]))

    names = ("gq", "gk", "gv", "gz")
    arrays = [held[name] for name in ("uc", "mem", "mix")] + [grads[name] for name in names]
    streams = {"d": down, "u": up}
    outs = {}
    for event in PLAN:
        if event == "1":
            arrays[-1], small = order.after(arrays[-1], small)
            away = swap(attention_group_grads((2, 2), codes["s"], arrays, None), 0)
            small = small + swap(small, 0)
        elif event == "2":
            away, small = order.after(away, small)
            streams["s"] = Sum(order, PATHS["s"], bits, attention_group_grads((0, 2), codes["s"], arrays, away), small)
        elif event in KINDS:
            outs[event] = streams[KINDS[event][0]].restore(codes[KINDS[event][0]], KINDS[event][1])
        else:
            streams[event].step()
    (grad_down,), (grad_up,), (grad_q, grad_k, grad_v, grad_o) = outs["D"], outs["U"], outs["S"]
    square = streams["s"]
    small = square.small
    ends_out = jnp.where(first, jnp.stack([gx[:slot] for gx in firsts]), jnp.stack([y[:slot] for y in finals]))
    ends_out = ends_out.reshape(1, slots * slot, width)
    return (ends_out, small[None, 0:3], small[None, 3:6], grad_q, grad_k, grad_v, small[None, 6:8],
            grad_o, small[8:9], grad_up, small[10 : 10 + hid // width].reshape(1, hid), grad_down, small[9:10])


def solution(mesh):
    placed = (
        P("section", "dp", None), P("dp"), P("dp"),
        P("section", None, None), P("section", None, None), P("section", None, None), P("section", None, None),
        P("section", None, None), P("section", None, None), P("section", None, None), P("section", None),
        P("section", None, None), P("section", None), P("section", None, None), P("section", None),
    )
    return jax.shard_map(
        on_device,
        mesh=mesh,
        in_specs=placed,
        out_specs=(
            P("section", "dp", None), P("section", None, None), P("section", None, None), P("section", None, None),
            P("section", None, None), P("section", None, None), P("section", None, None), P("section", None, None),
            P("section", None), P("section", None, None), P("section", None), P("section", None, None),
            P("section", None),
        ),
        check_vma=False,
    )
```

```python
import functools
import jax
import jax.numpy as jnp
from jax import lax
from jax.experimental import pallas as pl
from jax.experimental.pallas import tpu as pltpu
from jax.sharding import PartitionSpec as P

LEFT = 30
RIGHT = 4
MEM = 4
TILE = 64
KEYS = 128
ROWS = 80
FRONT = 32
BF = jnp.bfloat16
F32 = jnp.float32
VMEM_LIMIT = 5 * 1024 * 1024


def dot(a, b):
    return lax.dot_general(a, b, (((1,), (0,)), ((), ())), preferred_element_type=F32)


def dot_nt(a, b):
    return lax.dot_general(a, b, (((1,), (1,)), ((), ())), preferred_element_type=F32)


def dot_tn(a, b):
    return lax.dot_general(a, b, (((0,), (0,)), ((), ())), preferred_element_type=F32)


def normed(value):
    center = value - jnp.mean(value, axis=-1, keepdims=True)
    rs = lax.rsqrt(jnp.mean(center * center, axis=-1, keepdims=True) + 1e-05)
    return center * rs, rs


def norm_back(w, xhat, rs):
    return (w - jnp.mean(w, axis=-1, keepdims=True) - xhat * jnp.mean(w * xhat, axis=-1, keepdims=True)) * rs


def fold8(value):
    rows, width = value.shape
    return jnp.sum(value.reshape(rows // 8, 8, width), axis=0)


def gelu_parts(f):
    phi = 0.5 + 0.5 * lax.erf(f * 0.7071067811865476)
    return f * phi, phi + f * (jnp.exp(f * f * -0.5) * 0.3989422804014327)


def seg_sizes(wide):
    return jnp.where(wide, 16, 8).astype(jnp.int32), jnp.where(wide, 4, 8).astype(jnp.int32)


def pool_matrix(length, wide, slot):
    seg, per = seg_sizes(wide)
    rows = slot // 8
    e = lax.broadcasted_iota(jnp.int32, (rows, slot), 0)
    t = lax.broadcasted_iota(jnp.int32, (rows, slot), 1)
    r = jnp.bitwise_and(e, 7)
    start = jnp.right_shift(e, 3) * TILE + r * seg
    inside = (t >= start) & (t < start + seg) & (t < length) & (r < per)
    e1 = lax.broadcasted_iota(jnp.int32, (rows, 1), 0)
    r1 = jnp.bitwise_and(e1, 7)
    start1 = jnp.right_shift(e1, 3) * TILE + r1 * seg
    count = jnp.where(r1 < per, jnp.clip(length - start1, 0, seg), 0)
    inverse = 1.0 / jnp.maximum(count, 1).astype(F32)
    return jnp.where(inside, 1.0, 0.0).astype(BF), inverse


def unpool(matrix, value):
    high = value.astype(BF)
    low = (value - high.astype(F32)).astype(BF)
    return dot_tn(jnp.concatenate([matrix, matrix], axis=0), jnp.concatenate([high, low], axis=0))


def tile_bias(tile, odd, length, wide):
    seg, per = seg_sizes(wide)
    row = lax.broadcasted_iota(jnp.int32, (ROWS, 1), 0)
    col = lax.broadcasted_iota(jnp.int32, (1, KEYS), 1)
    anchor = tile * TILE
    is_frame = row < TILE
    extra = row - TILE
    shift = jnp.where(wide, 4, 3).astype(jnp.int32)
    r = jnp.where(is_frame, jnp.right_shift(row, shift), jnp.bitwise_and(extra, 7))
    owned = is_frame | ((jnp.right_shift(extra, 3) == odd) & (r < per))
    key = col - (16 + FRONT)
    low = jnp.where(owned, r * seg - LEFT, 100000)
    high = jnp.minimum(r * seg + seg + RIGHT, length - anchor)
    frame_ok = (key >= jnp.maximum(low, -anchor)) & (key < high) & (col >= 16)
    c = jnp.bitwise_and(col, 7)
    slot = jnp.where((col < 16) & (c < per), jnp.where(col < 8, c - per, c), -100000)
    slot = jnp.where((col < 8) & (anchor == 0), -100000, slot)
    mem_ok = (slot >= r - MEM) & (slot < jnp.where(is_frame, r, -100000))
    return jnp.where(frame_ok | mem_ok, 0.0, -1e30).astype(F32)


def head_masks(rows):
    lane = jnp.right_shift(lax.broadcasted_iota(jnp.int32, (rows, 256), 1), 6)
    return [lane == h for h in range(4)]


def spread_heads(tile, masks):
    zero = jnp.zeros_like(tile)
    return jnp.concatenate([jnp.where(m, tile, zero) for m in masks], axis=0)


def gather_heads(stack, masks):
    total = jnp.where(masks[0], stack[:ROWS], 0.0)
    for h in range(1, 4):
        total = jnp.where(masks[h], stack[h * ROWS : (h + 1) * ROWS], total)
    return total


def key_window(tile, lanes, frames_ref, even_ref, pad_ref):
    first = tile // 2 * 16
    memory = even_ref[first : first + 16, lanes] if tile % 2 else pad_ref[first : first + 16, lanes]
    return jnp.concatenate([memory, frames_ref[tile * TILE : tile * TILE + KEYS - 16, lanes]], axis=0)


def fill_windows(all_rows, frames_ref, even_ref, pad_ref, mem_rows, slot):
    width = all_rows.shape[1]
    memory = all_rows[:mem_rows].astype(F32)
    blank = jnp.zeros((8, width), F32)
    even_ref[...] = memory.astype(BF)
    pad_ref[...] = jnp.concatenate([blank, memory, blank], axis=0).astype(BF)
    frames_ref[:FRONT] = jnp.zeros((FRONT, width), BF)
    frames_ref[FRONT : FRONT + slot] = all_rows[mem_rows:].astype(BF)
    frames_ref[FRONT + slot :] = jnp.zeros((16, width), BF)


CHUNK = 32
G0, G1, G2, S0, S1, S2, QB, VB, OB, DB, UB = range(11)
KEPT = ("uc", "mem", "q", "k", "v", "prob", "mix", "xh0", "xh1", "h", "rs", "g", "gp", "xh2")
GRADS = ("gd", "gf", "gz", "gq", "gk", "gv")


def grads_of(do_ffn, do_att):
    return [g for g in GRADS if (do_ffn and g in GRADS[:3]) or (do_att and g in GRADS[2:])]


def forward_kernel(utt, lower, on_ref, vec, ub, x_ref, wq, wk, wv, wo, wu, wd, *refs):
    n = len(KEPT)
    slots = (on_ref.shape[0] - 1) // 2
    if lower:
        x_ref = x_ref.at[utt]
    kf, ke, kp, vf, ve, vp, after = refs[-7:]
    y = refs[-8]
    near = {name: ref.at[utt] for name, ref in zip(KEPT, refs[-8 - n : -8])}
    slot, width = after.shape
    mem_rows = slot // 8
    length = on_ref[1 + utt]
    wide = on_ref[1 + slots + utt] == 1
    gain, shift, qvb, ob, db = vec.at[0:3], vec.at[3:6], vec.at[6:8], vec.at[8:9], vec.at[9:10]

    uc, mem, q, k, v, prob, mix = (near[name] for name in KEPT[:7])
    rs = near["rs"]
    lane = lax.broadcasted_iota(jnp.int32, (1, 128), 1)
    phase = pl.when(on_ref[0] == 1)


    @phase
    def _():
        for i in range(0, slot, CHUNK):
            r = slice(i, i + CHUNK)
            xhat, scale = normed(x_ref[r].astype(F32))
            near["xh0"][r] = xhat.astype(BF)
            uc[r] = (xhat * gain[0:1] + shift[0:1]).astype(BF)
            rs[r] = jnp.broadcast_to(scale, (CHUNK, 128))
        pm, inverse = pool_matrix(length, wide, slot)
        uc[slot:] = (dot(pm, uc[:slot]) * inverse).astype(BF)
        if lower:
            mem[...] = (dot(pm, x_ref[:slot]) * inverse).astype(BF)
        else:
            mem[...] = x_ref[slot:]


    @phase
    def _():
        q[...] = (dot(uc[...], wq[...]) + qvb[0:1]).astype(BF)
        k[:mem_rows] = dot(mem[...], wk[...]).astype(BF)
        k[mem_rows:] = dot(uc[:slot], wk[...]).astype(BF)
        v[:mem_rows] = (dot(mem[...], wv[...]) + qvb[1:2]).astype(BF)
        v[mem_rows:] = (dot(uc[:slot], wv[...]) + qvb[1:2]).astype(BF)
        fill_windows(k[...], kf, ke, kp, mem_rows, slot)
        fill_windows(v[...], vf, ve, vp, mem_rows, slot)


    @phase
    def _():
        masks = head_masks(ROWS)
        for pair in range(slot // (2 * TILE)):
            srows = slice(slot + pair * 16, slot + pair * 16 + 16)
            biases = [tile_bias(pair * 2 + odd, odd, length, wide) for odd in range(2)]
            for quad in range(width // 256):
                lanes = slice(quad * 256, quad * 256 + 256)
                extra = None
                for odd in range(2):
                    tile = pair * 2 + odd
                    rows = slice(tile * TILE, tile * TILE + TILE)
                    qs = spread_heads(jnp.concatenate([q[rows, lanes], q[srows, lanes]], axis=0), masks)
                    kw = key_window(tile, lanes, kf, ke, kp)
                    vw = key_window(tile, lanes, vf, ve, vp)
                    s = dot_nt(qs, kw).reshape(4, ROWS, KEYS) * 0.125 + biases[odd][None]
                    peak = jnp.maximum(jnp.max(s, axis=-1, keepdims=True), -1e29)
                    e = jnp.exp(s - peak)
                    total = jnp.sum(e, axis=-1, keepdims=True)
                    p = (e * (1.0 / jnp.maximum(total, 1e-30))).astype(BF).reshape(4 * ROWS, KEYS)
                    prob[pair * 4 + quad * 2 + odd] = p
                    o = gather_heads(dot(p, vw), masks)
                    mix[rows, lanes] = o[:TILE].astype(BF)
                    extra = o[TILE:] if extra is None else extra + o[TILE:]
                mix[srows, lanes] = extra.astype(BF)


    @phase
    def _():
        z = dot(mix[...], wo[...]) + ob[...]
        y[slot:] = z[slot:].astype(BF)
        after[...] = z[:slot]
        for i in range(0, slot, CHUNK):
            r = slice(i, i + CHUNK)
            a = x_ref[r].astype(F32) + after[r]
            after[r] = a + db[...]
            xhat, scale = normed(a)
            near["xh1"][r] = xhat.astype(BF)
            near["h"][r] = (xhat * gain[1:2] + shift[1:2]).astype(BF)
            rs[r] = jnp.where(lane == 0, rs[r], jnp.broadcast_to(scale, (CHUNK, 128)))

    for c in range(wu.shape[1] // 512):
        cols = slice(c * 512, c * 512 + 512)

        @phase
        def _():
            act, slope = gelu_parts(dot(near["h"][...], wu[:, cols]) + ub[:, cols])
            act = act.astype(BF)
            near["g"][:, cols] = act
            near["gp"][:, cols] = slope.astype(BF)
            after[...] += dot(act, wd[cols])

    @phase
    def _():
        for i in range(0, slot, CHUNK):
            r = slice(i, i + CHUNK)
            xhat, scale = normed(after[r])
            near["xh2"][r] = xhat.astype(BF)
            rs[r] = jnp.where(lane == 2, jnp.broadcast_to(scale, (CHUNK, 128)), rs[r])
            t = lax.broadcasted_iota(jnp.int32, (CHUNK, 1), 0) + i
            valid = jnp.where(t < length, 1.0, 0.0)
            y[r] = ((xhat * gain[2:3] + shift[2:3]) * valid).astype(BF)


def backward_kernel(utt, lower, do_ffn, do_att, apart, on_ref, vec, cot, gmem, ga_in,
                    wq, wk, wv, wo, wu, wd, *refs):
    kept = {name: ref.at[utt] for name, ref in zip(KEPT, refs)}
    names = grads_of(do_ffn, do_att)
    kf, ke, kp, vf, ve, vp, gom, akf, akm, acc = refs[-10:]
    gx, gm, ga_out, small = refs[-14:-10]
    near = {name: ref.at[utt] for name, ref in zip(names, refs[-14 - len(names) : -14])}
    slot, width = kept["xh0"].shape
    mem_rows = slot // 8
    slots = (on_ref.shape[0] - 1) // 2
    length = on_ref[1 + utt]
    wide = on_ref[1 + slots + utt] == 1
    gain = vec.at[0:3]
    cot = cot if lower else cot.at[utt]
    gz = near["gz"]
    q, k, v, prob, xh0, xh1, xh2, rs, gp = (kept[name] for name in
                                            ("q", "k", "v", "prob", "xh0", "xh1", "xh2", "rs", "gp"))
    phase = pl.when(on_ref[0] == 1)

    @phase
    def _():
        acc[...] = jnp.zeros_like(acc)

    if do_ffn:
        gd, gf = near["gd"], near["gf"]
        ga = ga_out

        @phase
        def _():
            for i in range(0, slot, CHUNK):
                r = slice(i, i + CHUNK)
                t = lax.broadcasted_iota(jnp.int32, (CHUNK, 1), 0) + i
                gy = cot[r].astype(F32) * jnp.where(t < length, 1.0, 0.0)
                xhat = xh2[r].astype(F32)
                acc[G2] += fold8(gy * xhat)
                acc[S2] += fold8(gy)
                ga2 = norm_back(gy * gain[2:3], xhat, rs[r, 2:3])
                ga[r] = ga2
                low = ga2.astype(BF)
                gd[r] = low
                acc[DB] += fold8(low.astype(F32))

        for c in range(wu.shape[1] // 512):
            cols = slice(c * 512, c * 512 + 512)

            @phase
            def _():
                gfl = (dot_nt(gd[...], wd[cols]) * gp[:, cols].astype(F32)).astype(BF)
                gf[:, cols] = gfl
                acc[UB + c] += fold8(gfl.astype(F32))
                part = dot_nt(gfl, wu[:, cols])
                if c == 0:
                    akf[:slot] = part
                else:
                    akf[:slot] += part

        @phase
        def _():
            for i in range(0, slot, CHUNK):
                r = slice(i, i + CHUNK)
                back = akf[r]
                xhat = xh1[r].astype(F32)
                acc[G1] += fold8(back * xhat)
                acc[S1] += fold8(back)
                total = ga[r] + norm_back(back * gain[1:2], xhat, rs[r, 1:2])
                ga[r] = total
                low = total.astype(BF)
                gz[r] = low
                acc[OB] += fold8(low.astype(F32))
    else:
        ga = ga_in
    if do_att:
        gq, gk, gv = near["gq"], near["gk"], near["gv"]

        @phase
        def _():
            far = (gmem[...] if apart else cot[slot:]) if lower else jnp.zeros((mem_rows, width), BF)
            gz[slot:] = far
            if lower:
                acc[OB] += fold8(far.astype(F32))
            gom[...] = dot_nt(gz[...], wo[...]).astype(BF)
            fill_windows(k[...], kf, ke, kp, mem_rows, slot)
            fill_windows(v[...], vf, ve, vp, mem_rows, slot)

        for quad in range(width // 256):
            lanes = slice(quad * 256, quad * 256 + 256)

            @phase
            def _():
                masks = head_masks(ROWS)
                akf[...] = jnp.zeros_like(akf)
                akm[...] = jnp.zeros_like(akm)
                for pair in range(slot // (2 * TILE)):
                    srows = slice(slot + pair * 16, slot + pair * 16 + 16)
                    extra = None
                    for odd in range(2):
                        tile = pair * 2 + odd
                        rows = slice(tile * TILE, tile * TILE + TILE)
                        qs = spread_heads(jnp.concatenate([q[rows, lanes], q[srows, lanes]], axis=0), masks)
                        go = spread_heads(jnp.concatenate([gom[rows, lanes], gom[srows, lanes]], axis=0), masks)
                        kw = key_window(tile, lanes, kf, ke, kp)
                        vw = key_window(tile, lanes, vf, ve, vp)
                        p = prob[pair * 4 + quad * 2 + odd]
                        gprob = dot_nt(go, vw) * p.astype(F32)
                        gs = (gprob - p.astype(F32) * jnp.sum(gprob, axis=-1, keepdims=True)).astype(BF)
                        gqt = gather_heads(dot(gs, kw), masks) * 0.125
                        gq[rows, lanes] = gqt[:TILE].astype(BF)
                        extra = gqt[TILE:] if extra is None else extra + gqt[TILE:]
                        for place, got in ((0, dot_tn(gs, qs) * 0.125), (256, dot_tn(p, go))):
                            cols = slice(place, place + 256)
                            akm[tile * 8 : tile * 8 + 16, cols] += got[:16]
                            akf[tile * TILE : tile * TILE + KEYS - 16, cols] += got[16:]
                    gq[srows, lanes] = extra.astype(BF)
                for out, place in ((gk, 0), (gv, 256)):
                    cols = slice(place, place + 256)
                    out[:mem_rows, lanes] = akm[8 : 8 + mem_rows, cols].astype(BF)
                    out[mem_rows:, lanes] = akf[FRONT : FRONT + slot, cols].astype(BF)

        @phase
        def _():
            pm, inverse = pool_matrix(length, wide, slot)
            gmf = dot_nt(gk[:mem_rows], wk[...]) + dot_nt(gv[:mem_rows], wv[...])
            if apart:
                gm[...] = gmf.astype(BF)
            else:
                gx[slot:] = gmf.astype(BF)
            gc = dot_nt(gq[slot:], wq[...]) * inverse
            akf[:slot] = (dot_nt(gk[mem_rows:], wk[...]) + dot_nt(gv[mem_rows:], wv[...])
                          + dot_nt(gq[:slot], wq[...]) + unpool(pm, gc))
            spread = unpool(pm, gmf * inverse) if lower else None
            for i in range(0, slot, CHUNK):
                r = slice(i, i + CHUNK)
                w = akf[r]
                xhat = xh0[r].astype(F32)
                acc[G0] += fold8(w * xhat)
                acc[S0] += fold8(w)
                total = ga[r] + norm_back(w * gain[0:1], xhat, rs[r, 0:1])
                if lower:
                    total = total + spread[i : i + CHUNK]
                gx[r] = total.astype(BF)
            acc[QB] += fold8(gq[...].astype(F32))
            acc[VB] += fold8(gv[...].astype(F32))

    @phase
    def _():
        small[...] = jnp.sum(acc[...], axis=1)


def sds(shape, dtype):
    return jax.ShapeDtypeStruct(shape, dtype)


def cost_of(flops, moved, special=0):
    return pl.CostEstimate(flops=int(flops), bytes_accessed=int(moved), transcendentals=int(special))


def kernel_params(limit=VMEM_LIMIT):
    return pltpu.CompilerParams(vmem_limit_bytes=limit)


SCALAR = pl.BlockSpec(memory_space=pltpu.SMEM)
NEAR = pl.BlockSpec(memory_space=pltpu.VMEM)


def window_scratch(slot, width):
    mem_rows = slot // 8
    one = [pltpu.VMEM((FRONT + slot + 16, width), BF), pltpu.VMEM((mem_rows, width), BF),
           pltpu.VMEM((mem_rows + 16, width), BF)]
    return one + one


def kept_shapes(slot, width, hid):
    every = slot + slot // 8
    shapes = [((every, width), BF), ((slot // 8, width), BF)] + [((every, width), BF)] * 3
    shapes += [((slot // TILE * (width // 256), 4 * ROWS, KEYS), BF), ((every, width), BF)] + [((slot, width), BF)] * 3
    return shapes + [((slot, 128), F32)] + [((slot, hid), BF)] * 2 + [((slot, width), BF)]


def grad_shapes(slot, width, hid):
    every = slot + slot // 8
    return [((slot, width), BF), ((slot, hid), BF)] + [((every, width), BF)] * 4


def forward(weights, utt, lower, scalars, slots, frames, kept):
    vec, ub, wq, wk, wv, wo, wu, wd = weights
    width, hid = wu.shape
    slot = frames.shape[1] if lower else frames.shape[0] // 9 * 8
    every = slot + slot // 8
    shapes = kept_shapes(slot, width, hid)
    ins = [scalars, vec, ub, frames, wq, wk, wv, wo, wu, wd]
    extra = list(kept) if kept is not None else []
    out = [sds((slots,) + s, t) for s, t in shapes] + [sds((every, width), BF)]
    res = pl.pallas_call(
        functools.partial(forward_kernel, utt, lower),
        in_specs=[SCALAR] + [NEAR] * (len(ins) - 1 + len(extra)),
        out_specs=[NEAR] * len(out),
        out_shape=out,
        scratch_shapes=window_scratch(slot, width) + [pltpu.VMEM((slot, width), F32)],
        input_output_aliases={len(ins) + i: i for i in range(len(extra))},
        compiler_params=kernel_params(),
        cost_estimate=cost_of(8 * every * width * width + 4 * slot * width * hid, 30 << 20, slot * hid * 2),
    )(*ins, *extra)
    return res[-1], res[:-1]


def pass_on(values, out):
    out[...] = values[...]


def opening(values):
    return pl.pallas_call(
        pass_on, in_specs=[NEAR], out_specs=NEAR, out_shape=sds(values.shape, values.dtype),
        compiler_params=kernel_params(1 << 20), cost_estimate=cost_of(1e12, 1 << 30),
    )(values)


def backward(weights, utt, lower, parts, scalars, slots, cot, gmem, ga, kept, grads):
    do_ffn, do_att = parts
    vec, ub, wq, wk, wv, wo, wu, wd = weights
    width, hid = wu.shape
    apart = gmem is not None
    slot = kept[7].shape[1]
    mem_rows = slot // 8
    every = slot + mem_rows
    shapes = dict(zip(GRADS, grad_shapes(slot, width, hid)))
    names = grads_of(do_ffn, do_att)
    ins = [scalars, vec, cot, gmem if apart else vec, ga if ga is not None else vec, wq, wk, wv, wo, wu, wd] + list(kept)
    extra = [grads[g] for g in names if grads[g] is not None]
    aliases = {len(ins) + i: place for i, place in enumerate(p for p, g in enumerate(names) if grads[g] is not None)}
    tiny = (8, 128)
    out = [sds((slots,) + shapes[g][0], BF) for g in names]
    out += [sds((slot if apart else every, width) if do_att else tiny, BF), sds((mem_rows, width) if apart and do_att else tiny, BF),
            sds((slot, width) if do_ffn else tiny, F32), sds((16, width), F32)]
    flops = (4 * slot * width * hid if do_ffn else 0) + (8 * every * width * width if do_att else 0)
    res = pl.pallas_call(
        functools.partial(backward_kernel, utt, lower, do_ffn, do_att, apart),
        in_specs=[SCALAR] + [NEAR] * (len(ins) - 1 + len(extra)),
        out_specs=[NEAR] * len(out), out_shape=out,
        scratch_shapes=window_scratch(slot, width) + [
            pltpu.VMEM((every, width), BF), pltpu.VMEM((FRONT + slot + 16, width), F32),
            pltpu.VMEM((mem_rows + 16, width), F32), pltpu.VMEM((16, 8, width), F32)],
        input_output_aliases=aliases, compiler_params=kernel_params(), cost_estimate=cost_of(flops, 20 << 20),
    )(*ins, *extra)
    grads = dict(grads)
    grads.update(zip(names, res))
    gx, gm, ga, small = res[len(names) :]
    return grads, gx, gm, ga, small


SMALL_LIMIT = 6 * 1024 * 1024
LANES_OUT = 4
STAGES = 4


def emit_group(value, me, more, out, part, j):
    if value is not None:
        part[...] = value
    sub = jnp.bitwise_and(me, LANES_OUT - 1)
    rows = part.shape[0] // LANES_OUT
    for r in range(LANES_OUT):
        got = part[pl.ds(pl.multiple_of(jnp.bitwise_xor(sub, r) * rows, rows), rows)]
        for ref, place in more:
            got = got + ref[place + j, r].astype(F32)
        out[j, r] = got.astype(out.dtype)


def pair_weights(chunk_left, low, span, places, me_ref, left, right, *refs):
    more = list(zip(refs, places))
    out, part = refs[-2:]
    me = me_ref[0]
    for j in range(out.shape[0]):
        start = jnp.bitwise_xor(j + low, jnp.right_shift(me, 2)) * 512
        chunk = pl.ds(pl.multiple_of(start, 512), 512)
        value = sum(dot_tn(left[u, :, chunk] if chunk_left else left[u], right[u] if chunk_left else right[u, :, chunk])
                    for u in span)
        emit_group(value, me, more, out, part, j)


def group_call(body, me, arrays, more, count, width, flops):
    return pl.pallas_call(
        functools.partial(body, tuple(place for _, place in more)),
        in_specs=[SCALAR] + [NEAR] * (len(arrays) + len(more)),
        out_specs=NEAR,
        out_shape=sds((count, LANES_OUT, width // LANES_OUT, width), BF),
        scratch_shapes=[pltpu.VMEM((width, width), F32)],
        compiler_params=kernel_params(),
        cost_estimate=cost_of(flops, 4 << 20),
    )(me, *arrays, *[a for a, _ in more])


def ffn_group_grads(groups, chunk_left, me, left, right, span, more=()):
    _, slot, _ = left.shape
    width = min(left.shape[2], right.shape[2])
    low, count = groups
    return group_call(functools.partial(pair_weights, chunk_left, low, span), me, (left, right), more, count,
                      width, 2 * len(span) * slot * count * width * width)


def attention_weights(low, span, places, me_ref, uc, mem, mix, gq, gk, gv, gz, *refs):
    more = list(zip(refs, places))
    out, part = refs[-2:]
    _, every, width = uc.shape
    mem_rows = every // 9
    slot = every - mem_rows
    me = me_ref[0]
    for j in range(out.shape[0]):
        which = jnp.bitwise_xor(j + low, jnp.right_shift(me, 2))

        @pl.when(which == 0)
        def _():
            part[...] = sum(dot_tn(uc[u], gq[u]) for u in span)

        for place, ref in ((1, gk), (2, gv)):
            @pl.when(which == place)
            def _():
                part[...] = sum(dot_tn(mem[u], ref[u, :mem_rows]) + dot_tn(uc[u, :slot], ref[u, mem_rows:])
                                for u in span)

        @pl.when(which == 3)
        def _():
            part[...] = sum(dot_tn(mix[u], gz[u]) for u in span)

        emit_group(None, me, more, out, part, j)


def attention_group_grads(groups, me, arrays, span, more=()):
    _, every, width = arrays[0].shape
    low, count = groups
    return group_call(functools.partial(attention_weights, low, span), me, arrays, more, count, width,
                      2 * count * len(span) * every * width * width)


def restore_group(own, far, me, value):
    gme = jnp.right_shift(me, 2)
    sub = jnp.bitwise_and(me, LANES_OUT - 1)
    rows = own.shape[2]
    place = jnp.bitwise_xor(pl.program_id(0), gme)
    half = own.shape[0]
    for ref, low in ((own, 0), (far, half)):
        @pl.when((place >= low) & (place < low + half))
        def _():
            for r in range(LANES_OUT):
                value(r, ref[place - low, jnp.bitwise_xor(sub, r)].astype(F32))


def restore_wide(me_ref, own, far, out):
    rows = own.shape[2]

    def put(r, got):
        out[0, r * rows : (r + 1) * rows] = got

    restore_group(own, far, me_ref[0], put)


def restore_square(me_ref, own, far, *outs):
    rows = own.shape[2]

    def put(r, got):
        for matrix, out in enumerate(outs):
            @pl.when(pl.program_id(0) == matrix)
            def _():
                out[0, r * rows : (r + 1) * rows] = got

    restore_group(own, far, me_ref[0], put)


def restore(me, own, far, kind):
    half, _, rows, width = own.shape
    whole = pl.BlockSpec(own.shape, lambda j, me: (0, 0, 0, 0))
    groups = 2 * half
    if kind == "down":
        body, shapes = restore_wide, [(1, groups * width, width)]
        specs = [pl.BlockSpec((1, width, width), lambda j, me: (0, j, 0))]
    elif kind == "up":
        body, shapes = restore_wide, [(1, width, groups * width)]
        specs = [pl.BlockSpec((1, width, width), lambda j, me: (0, 0, j))]
    else:
        body, shapes = restore_square, [(1, width, width)] * groups
        specs = [pl.BlockSpec((1, width, width), lambda j, me: (0, 0, 0))] * groups
    return pl.pallas_call(
        body,
        grid_spec=pltpu.PrefetchScalarGridSpec(num_scalar_prefetch=1, grid=(groups,), in_specs=[whole, whole],
                                               out_specs=specs),
        out_shape=[sds(s, F32) for s in shapes],
        compiler_params=kernel_params(SMALL_LIMIT),
        cost_estimate=cost_of(0, 6 * groups * width * width),
    )(me, own, far)


def swap(value, bit):
    n = lax.axis_size("dp")
    return lax.ppermute(value, "dp", [(i, i ^ (1 << bit)) for i in range(n)])


def added(a, b):
    return (a.astype(F32) + b.astype(F32)).astype(BF)


PLAN = "d1d2ududsudsusudsDsuUsS"
PATHS = {"d": (0, 1, 2, 3), "u": (0, 1, 2, 3), "s": (0, 1, 2, 3)}
KINDS = {"D": ("d", "down"), "U": ("u", "up"), "S": ("s", "square")}


class Order:
    def __init__(self):
        self.last = None

    def after(self, *values):
        if self.last is not None:
            values = lax.optimization_barrier((*values, self.last))[:-1]
        return values

    def made(self, value):
        self.last = value


class Sum:
    def __init__(self, order, path, bits, value, small=None):
        self.order = order
        self.path = path
        self.bits = bits
        self.value = value.reshape((-1,) + value.shape[2:])
        self.small = small
        self.stage = 1
        self.launch()

    def launch(self):
        if self.stage < STAGES:
            half = self.value.shape[0] // 2
            out, self.value = self.value[half:], self.value[:half]
            if self.small is not None:
                width = out.shape[-1]
                high = lax.reduce_precision(self.small, exponent_bits=8, mantissa_bits=7)
                parts = [out.reshape(-1, width), high.astype(BF), (self.small - high).astype(BF)]
                out = jnp.concatenate(parts, axis=0)
            bit = self.path[self.stage]
        else:
            out = self.value
            bit = self.path[2 * STAGES - 1 - self.stage]
        self.order.made(out)
        self.got = swap(out, bit)

    def step(self):
        got, value = self.order.after(self.got, self.value)
        if self.stage < STAGES:
            if self.small is not None:
                lines = value.shape[0] * value.shape[1]
                rows = self.small.shape[0]
                self.small = self.small + got[lines : lines + rows].astype(F32) + got[lines + rows :].astype(F32)
                got = got[:lines].reshape(value.shape)
            value = added(value, got)
            if self.stage == STAGES - 1:
                for bit in range(STAGES, self.bits):
                    value = added(value, swap(value, bit))
                    if self.small is not None:
                        self.small = self.small + swap(self.small, bit)
        else:
            value = jnp.concatenate([value, got], axis=0)
        self.value = value
        self.stage += 1
        self.launch()

    def restore(self, me, kind):
        groups = lambda v: v.reshape((-1, LANES_OUT) + v.shape[1:])
        got, value = self.order.after(self.got, self.value)
        outs = restore(me, groups(value), groups(got), kind)
        self.order.made(outs[0])
        return outs


def shifted(block, axis, distance):
    devices = range(lax.axis_size(axis))
    route = [(i - distance, i) for i in devices if i - distance in devices]
    return lax.ppermute(block, axis, route)


def on_device(ends, lengths, seg_group, norm_gain, norm_shift, w_query, w_key, w_value, qv_bias, w_out, out_bias,
              w_up, up_bias, w_down, down_bias):
    section = lax.axis_index("section")
    first = section == 0
    slots = lengths.shape[0]
    width = ends.shape[2]
    slot = ends.shape[1] // slots
    hid = w_up.shape[2]
    section = section.astype(jnp.int32).reshape(1)
    lower = jnp.concatenate([1 - section, lengths, seg_group])
    upper = jnp.concatenate([section, lengths, seg_group])

    bits = lax.axis_size("dp").bit_length() - 1
    place = lax.axis_index("dp").astype(jnp.int32)
    codes = {
        name: sum(jnp.bitwise_and(jnp.right_shift(place, bit), 1) << (STAGES - 1 - s) for s, bit in enumerate(path)).reshape(1)
        for name, path in PATHS.items()}

    vec = jnp.concatenate([norm_gain[0], norm_shift[0], qv_bias[0], out_bias, down_bias], axis=0)
    vec, lower, upper, codes, first = lax.optimization_barrier((vec, lower, upper, codes, first))
    vec = opening(vec)
    weights = (vec, up_bias, w_query[0], w_key[0], w_value[0], w_out[0], w_up[0], w_down[0])
    local = ends.reshape(slots, slot, width)

    kept = None
    sent = []
    for b in range(slots):
        y, kept = forward(weights, b, True, lower, slots, local, kept)
        sent.append(shifted(y, "section", 1))
    finals = []
    grads = dict.fromkeys(GRADS)
    smalls = [[], []]
    back = []
    for b in range(slots):
        y, kept = forward(weights, b, False, upper, slots, sent[b], kept)
        finals.append(y)
        apart = vec if b == slots - 1 else None
        grads, gx, gm, _, small = backward(weights, b, False, (True, True), upper, slots, local, apart, None, kept, grads)
        smalls[1].append(small)
        back.append(shifted(gx, "section", -1))
    memory_back = shifted(gm, "section", -1)
    held = dict(zip(KEPT, kept))
    firsts = []
    for b in range(slots - 1):
        grads, gx, _, _, small = backward(weights, b, True, (True, True), lower, slots, back[b], None, None, kept, grads)
        smalls[0].append(small)
        firsts.append(gx)
    b = slots - 1
    sides = (("d", True, "g", "gd"), ("u", False, "h", "gf"))
    early = tuple(ffn_group_grads((0, 4), side, codes[name], held[left], grads[right], range(b))
                  for name, side, left, right in sides)
    arrays = [held[name] for name in ("uc", "mem", "mix")] + [grads[name] for name in ("gq", "gk", "gv", "gz")]
    early += (attention_group_grads((0, 4), codes["s"], arrays, range(b)),)
    last, *early = lax.optimization_barrier((back[b], *early))
    grads, _, _, ga, small = backward(weights, b, True, (True, False), lower, slots, last, vec, None, kept, grads)
    smalls[0].append(small)

    order = Order()
    now = range(b, slots)
    far = [swap(ffn_group_grads((2, 2), side, codes[name], held[left], grads[right], now, [(part, 2)]), 0)
           for (name, side, left, right), part in zip(sides, early)]
    down, up = [ffn_group_grads((0, 2), side, codes[name], held[left], grads[right], now, [(part, 0), (more, 0)])
                for (name, side, left, right), part, more in zip(sides, early, far)]
    ga, down, up = lax.optimization_barrier((ga, down, up))
    down = Sum(order, PATHS["d"], bits, down)
    up = Sum(order, PATHS["u"], bits, up)
    grads, gx, _, _, small = backward(weights, b, True, (False, True), lower, slots, last, memory_back, ga, kept, grads)
    smalls[0].append(small)
    firsts.append(gx)
    small = jnp.where(first, sum(smalls[0]), sum(smalls[1]))

    names = ("gq", "gk", "gv", "gz")
    arrays = [held[name] for name in ("uc", "mem", "mix")] + [grads[name] for name in names]
    streams = {"d": down, "u": up}
    outs = {}
    for event in PLAN:
        if event == "1":
            arrays[-1], small = order.after(arrays[-1], small)
            away = swap(attention_group_grads((2, 2), codes["s"], arrays, now, [(early[2], 2)]), 0)
            small = small + swap(small, 0)
        elif event == "2":
            away, small = order.after(away, small)
            streams["s"] = Sum(order, PATHS["s"], bits, attention_group_grads((0, 2), codes["s"], arrays, now, [(early[2], 0), (away, 0)]), small)
        elif event in KINDS:
            if event == "U":
                small = streams["s"].small
                small_outs = (small[None, 0:3], small[None, 3:6], small[None, 6:8], small[8:9], small[9:10],
                              small[10 : 10 + hid // width].reshape(1, hid))
                streams["u"].got, *small_outs = order.after(streams["u"].got, *small_outs)
            outs[event] = streams[KINDS[event][0]].restore(codes[KINDS[event][0]], KINDS[event][1])
        else:
            streams[event].step()
    (grad_down,), (grad_up,), (grad_q, grad_k, grad_v, grad_o) = outs["D"], outs["U"], outs["S"]
    grad_gain, grad_shift, grad_qv, grad_out, grad_down_bias, grad_up_bias = small_outs
    ends_out = jnp.where(first, jnp.stack([gx[:slot] for gx in firsts]), jnp.stack([y[:slot] for y in finals]))
    ends_out = ends_out.reshape(1, slots * slot, width)
    return (ends_out, grad_gain, grad_shift, grad_q, grad_k, grad_v, grad_qv, grad_o, grad_out, grad_up, grad_up_bias,
            grad_down, grad_down_bias)


def solution(mesh):
    placed = (
        P("section", "dp", None), P("dp"), P("dp"),
        P("section", None, None), P("section", None, None), P("section", None, None), P("section", None, None),
        P("section", None, None), P("section", None, None), P("section", None, None), P("section", None),
        P("section", None, None), P("section", None), P("section", None, None), P("section", None),
    )
    return jax.shard_map(
        on_device,
        mesh=mesh,
        in_specs=placed,
        out_specs=(
            P("section", "dp", None), P("section", None, None), P("section", None, None), P("section", None, None),
            P("section", None, None), P("section", None, None), P("section", None, None), P("section", None, None),
            P("section", None), P("section", None, None), P("section", None), P("section", None, None),
            P("section", None),
        ),
        check_vma=False,
    )
```

```python
import functools
import jax
import jax.numpy as jnp
from jax import lax
from jax.experimental import pallas as pl
from jax.experimental.pallas import tpu as pltpu
from jax.sharding import PartitionSpec as P

LEFT = 30
RIGHT = 4
MEM = 4
TILE = 64
KEYS = 128
ROWS = 80
FRONT = 32
BF = jnp.bfloat16
F32 = jnp.float32
VMEM_LIMIT = 5 * 1024 * 1024


def dot(a, b):
    return lax.dot_general(a, b, (((1,), (0,)), ((), ())), preferred_element_type=F32)


def dot_nt(a, b):
    return lax.dot_general(a, b, (((1,), (1,)), ((), ())), preferred_element_type=F32)


def dot_tn(a, b):
    return lax.dot_general(a, b, (((0,), (0,)), ((), ())), preferred_element_type=F32)


def normed(value):
    center = value - jnp.mean(value, axis=-1, keepdims=True)
    rs = lax.rsqrt(jnp.mean(center * center, axis=-1, keepdims=True) + 1e-05)
    return center * rs, rs


def norm_back(w, xhat, rs):
    return (w - jnp.mean(w, axis=-1, keepdims=True) - xhat * jnp.mean(w * xhat, axis=-1, keepdims=True)) * rs


def fold8(value):
    rows, width = value.shape
    return jnp.sum(value.reshape(rows // 8, 8, width), axis=0)


def gelu_parts(f):
    phi = 0.5 + 0.5 * lax.erf(f * 0.7071067811865476)
    return f * phi, phi + f * (jnp.exp(f * f * -0.5) * 0.3989422804014327)


def seg_sizes(wide):
    return jnp.where(wide, 16, 8).astype(jnp.int32), jnp.where(wide, 4, 8).astype(jnp.int32)


def pool_matrix(length, wide, slot):
    seg, per = seg_sizes(wide)
    rows = slot // 8
    e = lax.broadcasted_iota(jnp.int32, (rows, slot), 0)
    t = lax.broadcasted_iota(jnp.int32, (rows, slot), 1)
    r = jnp.bitwise_and(e, 7)
    start = jnp.right_shift(e, 3) * TILE + r * seg
    inside = (t >= start) & (t < start + seg) & (t < length) & (r < per)
    e1 = lax.broadcasted_iota(jnp.int32, (rows, 1), 0)
    r1 = jnp.bitwise_and(e1, 7)
    start1 = jnp.right_shift(e1, 3) * TILE + r1 * seg
    count = jnp.where(r1 < per, jnp.clip(length - start1, 0, seg), 0)
    inverse = 1.0 / jnp.maximum(count, 1).astype(F32)
    return jnp.where(inside, 1.0, 0.0).astype(BF), inverse


def unpool(matrix, value):
    high = value.astype(BF)
    low = (value - high.astype(F32)).astype(BF)
    return dot_tn(jnp.concatenate([matrix, matrix], axis=0), jnp.concatenate([high, low], axis=0))


def tile_bias(tile, odd, length, wide):
    seg, per = seg_sizes(wide)
    row = lax.broadcasted_iota(jnp.int32, (ROWS, 1), 0)
    col = lax.broadcasted_iota(jnp.int32, (1, KEYS), 1)
    anchor = tile * TILE
    is_frame = row < TILE
    extra = row - TILE
    shift = jnp.where(wide, 4, 3).astype(jnp.int32)
    r = jnp.where(is_frame, jnp.right_shift(row, shift), jnp.bitwise_and(extra, 7))
    owned = is_frame | ((jnp.right_shift(extra, 3) == odd) & (r < per))
    key = col - (16 + FRONT)
    low = jnp.where(owned, r * seg - LEFT, 100000)
    high = jnp.minimum(r * seg + seg + RIGHT, length - anchor)
    frame_ok = (key >= jnp.maximum(low, -anchor)) & (key < high) & (col >= 16)
    c = jnp.bitwise_and(col, 7)
    slot = jnp.where((col < 16) & (c < per), jnp.where(col < 8, c - per, c), -100000)
    slot = jnp.where((col < 8) & (anchor == 0), -100000, slot)
    mem_ok = (slot >= r - MEM) & (slot < jnp.where(is_frame, r, -100000))
    return jnp.where(frame_ok | mem_ok, 0.0, -1e30).astype(F32)


def head_masks(rows):
    lane = jnp.right_shift(lax.broadcasted_iota(jnp.int32, (rows, 256), 1), 6)
    return [lane == h for h in range(4)]


def spread_heads(tile, masks):
    zero = jnp.zeros_like(tile)
    return jnp.concatenate([jnp.where(m, tile, zero) for m in masks], axis=0)


def gather_heads(stack, masks):
    total = jnp.where(masks[0], stack[:ROWS], 0.0)
    for h in range(1, 4):
        total = jnp.where(masks[h], stack[h * ROWS : (h + 1) * ROWS], total)
    return total


def key_window(tile, lanes, frames_ref, even_ref, pad_ref):
    first = tile // 2 * 16
    memory = even_ref[first : first + 16, lanes] if tile % 2 else pad_ref[first : first + 16, lanes]
    return jnp.concatenate([memory, frames_ref[tile * TILE : tile * TILE + KEYS - 16, lanes]], axis=0)


def fill_windows(all_rows, frames_ref, even_ref, pad_ref, mem_rows, slot):
    width = all_rows.shape[1]
    memory = all_rows[:mem_rows].astype(F32)
    blank = jnp.zeros((8, width), F32)
    even_ref[...] = memory.astype(BF)
    pad_ref[...] = jnp.concatenate([blank, memory, blank], axis=0).astype(BF)
    frames_ref[:FRONT] = jnp.zeros((FRONT, width), BF)
    frames_ref[FRONT : FRONT + slot] = all_rows[mem_rows:].astype(BF)
    frames_ref[FRONT + slot :] = jnp.zeros((16, width), BF)


CHUNK = 32
G0, G1, G2, S0, S1, S2, QB, VB, OB, DB, UB = range(11)
KEPT = ("uc", "mem", "q", "k", "v", "prob", "mix", "xh0", "xh1", "h", "rs", "g", "gp", "xh2")
GRADS = ("gd", "gf", "gz", "gq", "gk", "gv")


def grads_of(do_ffn, do_att):
    return [g for g in GRADS if (do_ffn and g in GRADS[:3]) or (do_att and g in GRADS[2:])]


def forward_kernel(utt, lower, on_ref, vec, ub, x_ref, wq, wk, wv, wo, wu, wd, *refs):
    n = len(KEPT)
    slots = (on_ref.shape[0] - 1) // 2
    if lower:
        x_ref = x_ref.at[utt]
    kf, ke, kp, vf, ve, vp, after = refs[-7:]
    y = refs[-8]
    near = {name: ref.at[utt] for name, ref in zip(KEPT, refs[-8 - n : -8])}
    slot, width = after.shape
    mem_rows = slot // 8
    length = on_ref[1 + utt]
    wide = on_ref[1 + slots + utt] == 1
    gain, shift, qvb, ob, db = vec.at[0:3], vec.at[3:6], vec.at[6:8], vec.at[8:9], vec.at[9:10]

    uc, mem, q, k, v, prob, mix = (near[name] for name in KEPT[:7])
    rs = near["rs"]
    lane = lax.broadcasted_iota(jnp.int32, (1, 128), 1)
    phase = pl.when(on_ref[0] == 1)


    @phase
    def _():
        for i in range(0, slot, CHUNK):
            r = slice(i, i + CHUNK)
            xhat, scale = normed(x_ref[r].astype(F32))
            near["xh0"][r] = xhat.astype(BF)
            uc[r] = (xhat * gain[0:1] + shift[0:1]).astype(BF)
            rs[r] = jnp.broadcast_to(scale, (CHUNK, 128))
        pm, inverse = pool_matrix(length, wide, slot)
        uc[slot:] = (dot(pm, uc[:slot]) * inverse).astype(BF)
        if lower:
            mem[...] = (dot(pm, x_ref[:slot]) * inverse).astype(BF)
        else:
            mem[...] = x_ref[slot:]


    @phase
    def _():
        q[...] = (dot(uc[...], wq[...]) + qvb[0:1]).astype(BF)
        k[:mem_rows] = dot(mem[...], wk[...]).astype(BF)
        k[mem_rows:] = dot(uc[:slot], wk[...]).astype(BF)
        v[:mem_rows] = (dot(mem[...], wv[...]) + qvb[1:2]).astype(BF)
        v[mem_rows:] = (dot(uc[:slot], wv[...]) + qvb[1:2]).astype(BF)
        fill_windows(k[...], kf, ke, kp, mem_rows, slot)
        fill_windows(v[...], vf, ve, vp, mem_rows, slot)


    @phase
    def _():
        masks = head_masks(ROWS)
        for pair in range(slot // (2 * TILE)):
            srows = slice(slot + pair * 16, slot + pair * 16 + 16)
            biases = [tile_bias(pair * 2 + odd, odd, length, wide) for odd in range(2)]
            for quad in range(width // 256):
                lanes = slice(quad * 256, quad * 256 + 256)
                extra = None
                for odd in range(2):
                    tile = pair * 2 + odd
                    rows = slice(tile * TILE, tile * TILE + TILE)
                    qs = spread_heads(jnp.concatenate([q[rows, lanes], q[srows, lanes]], axis=0), masks)
                    kw = key_window(tile, lanes, kf, ke, kp)
                    vw = key_window(tile, lanes, vf, ve, vp)
                    s = dot_nt(qs, kw).reshape(4, ROWS, KEYS) * 0.125 + biases[odd][None]
                    peak = jnp.maximum(jnp.max(s, axis=-1, keepdims=True), -1e29)
                    e = jnp.exp(s - peak)
                    total = jnp.sum(e, axis=-1, keepdims=True)
                    p = (e * (1.0 / jnp.maximum(total, 1e-30))).astype(BF).reshape(4 * ROWS, KEYS)
                    prob[pair * 4 + quad * 2 + odd] = p
                    o = gather_heads(dot(p, vw), masks)
                    mix[rows, lanes] = o[:TILE].astype(BF)
                    extra = o[TILE:] if extra is None else extra + o[TILE:]
                mix[srows, lanes] = extra.astype(BF)


    @phase
    def _():
        z = dot(mix[...], wo[...]) + ob[...]
        y[slot:] = z[slot:].astype(BF)
        after[...] = z[:slot]
        for i in range(0, slot, CHUNK):
            r = slice(i, i + CHUNK)
            a = x_ref[r].astype(F32) + after[r]
            after[r] = a + db[...]
            xhat, scale = normed(a)
            near["xh1"][r] = xhat.astype(BF)
            near["h"][r] = (xhat * gain[1:2] + shift[1:2]).astype(BF)
            rs[r] = jnp.where(lane == 0, rs[r], jnp.broadcast_to(scale, (CHUNK, 128)))

    for c in range(wu.shape[1] // 512):
        cols = slice(c * 512, c * 512 + 512)

        @phase
        def _():
            act, slope = gelu_parts(dot(near["h"][...], wu[:, cols]) + ub[:, cols])
            act = act.astype(BF)
            near["g"][:, cols] = act
            near["gp"][:, cols] = slope.astype(BF)
            after[...] += dot(act, wd[cols])

    @phase
    def _():
        for i in range(0, slot, CHUNK):
            r = slice(i, i + CHUNK)
            xhat, scale = normed(after[r])
            near["xh2"][r] = xhat.astype(BF)
            rs[r] = jnp.where(lane == 2, jnp.broadcast_to(scale, (CHUNK, 128)), rs[r])
            t = lax.broadcasted_iota(jnp.int32, (CHUNK, 1), 0) + i
            valid = jnp.where(t < length, 1.0, 0.0)
            y[r] = ((xhat * gain[2:3] + shift[2:3]) * valid).astype(BF)


def backward_kernel(utt, lower, do_ffn, do_att, apart, on_ref, vec, cot, gmem, ga_in,
                    wq, wk, wv, wo, wu, wd, *refs):
    kept = {name: ref.at[utt] for name, ref in zip(KEPT, refs)}
    names = grads_of(do_ffn, do_att)
    kf, ke, kp, vf, ve, vp, gom, akf, akm, acc = refs[-10:]
    gx, gm, ga_out, small = refs[-14:-10]
    near = {name: ref.at[utt] for name, ref in zip(names, refs[-14 - len(names) : -14])}
    slot, width = kept["xh0"].shape
    mem_rows = slot // 8
    slots = (on_ref.shape[0] - 1) // 2
    length = on_ref[1 + utt]
    wide = on_ref[1 + slots + utt] == 1
    gain = vec.at[0:3]
    cot = cot if lower else cot.at[utt]
    gz = near["gz"]
    q, k, v, prob, xh0, xh1, xh2, rs, gp = (kept[name] for name in
                                            ("q", "k", "v", "prob", "xh0", "xh1", "xh2", "rs", "gp"))
    phase = pl.when(on_ref[0] == 1)

    @phase
    def _():
        acc[...] = jnp.zeros_like(acc)

    if do_ffn:
        gd, gf = near["gd"], near["gf"]
        ga = ga_out

        @phase
        def _():
            for i in range(0, slot, CHUNK):
                r = slice(i, i + CHUNK)
                t = lax.broadcasted_iota(jnp.int32, (CHUNK, 1), 0) + i
                gy = cot[r].astype(F32) * jnp.where(t < length, 1.0, 0.0)
                xhat = xh2[r].astype(F32)
                acc[G2] += fold8(gy * xhat)
                acc[S2] += fold8(gy)
                ga2 = norm_back(gy * gain[2:3], xhat, rs[r, 2:3])
                ga[r] = ga2
                low = ga2.astype(BF)
                gd[r] = low
                acc[DB] += fold8(low.astype(F32))

        for c in range(wu.shape[1] // 512):
            cols = slice(c * 512, c * 512 + 512)

            @phase
            def _():
                gfl = (dot_nt(gd[...], wd[cols]) * gp[:, cols].astype(F32)).astype(BF)
                gf[:, cols] = gfl
                acc[UB + c] += fold8(gfl.astype(F32))
                part = dot_nt(gfl, wu[:, cols])
                if c == 0:
                    akf[:slot] = part
                else:
                    akf[:slot] += part

        @phase
        def _():
            for i in range(0, slot, CHUNK):
                r = slice(i, i + CHUNK)
                back = akf[r]
                xhat = xh1[r].astype(F32)
                acc[G1] += fold8(back * xhat)
                acc[S1] += fold8(back)
                total = ga[r] + norm_back(back * gain[1:2], xhat, rs[r, 1:2])
                ga[r] = total
                low = total.astype(BF)
                gz[r] = low
                acc[OB] += fold8(low.astype(F32))
    else:
        ga = ga_in
    if do_att:
        gq, gk, gv = near["gq"], near["gk"], near["gv"]

        @phase
        def _():
            far = (gmem[...] if apart else cot[slot:]) if lower else jnp.zeros((mem_rows, width), BF)
            gz[slot:] = far
            if lower:
                acc[OB] += fold8(far.astype(F32))
            gom[...] = dot_nt(gz[...], wo[...]).astype(BF)
            fill_windows(k[...], kf, ke, kp, mem_rows, slot)
            fill_windows(v[...], vf, ve, vp, mem_rows, slot)

        for quad in range(width // 256):
            lanes = slice(quad * 256, quad * 256 + 256)

            @phase
            def _():
                masks = head_masks(ROWS)
                akf[...] = jnp.zeros_like(akf)
                akm[...] = jnp.zeros_like(akm)
                for pair in range(slot // (2 * TILE)):
                    srows = slice(slot + pair * 16, slot + pair * 16 + 16)
                    extra = None
                    for odd in range(2):
                        tile = pair * 2 + odd
                        rows = slice(tile * TILE, tile * TILE + TILE)
                        qs = spread_heads(jnp.concatenate([q[rows, lanes], q[srows, lanes]], axis=0), masks)
                        go = spread_heads(jnp.concatenate([gom[rows, lanes], gom[srows, lanes]], axis=0), masks)
                        kw = key_window(tile, lanes, kf, ke, kp)
                        vw = key_window(tile, lanes, vf, ve, vp)
                        p = prob[pair * 4 + quad * 2 + odd]
                        gprob = dot_nt(go, vw) * p.astype(F32)
                        gs = (gprob - p.astype(F32) * jnp.sum(gprob, axis=-1, keepdims=True)).astype(BF)
                        gqt = gather_heads(dot(gs, kw), masks) * 0.125
                        gq[rows, lanes] = gqt[:TILE].astype(BF)
                        extra = gqt[TILE:] if extra is None else extra + gqt[TILE:]
                        for place, got in ((0, dot_tn(gs, qs) * 0.125), (256, dot_tn(p, go))):
                            cols = slice(place, place + 256)
                            akm[tile * 8 : tile * 8 + 16, cols] += got[:16]
                            akf[tile * TILE : tile * TILE + KEYS - 16, cols] += got[16:]
                    gq[srows, lanes] = extra.astype(BF)
                for out, place in ((gk, 0), (gv, 256)):
                    cols = slice(place, place + 256)
                    out[:mem_rows, lanes] = akm[8 : 8 + mem_rows, cols].astype(BF)
                    out[mem_rows:, lanes] = akf[FRONT : FRONT + slot, cols].astype(BF)

        @phase
        def _():
            pm, inverse = pool_matrix(length, wide, slot)
            gmf = dot_nt(gk[:mem_rows], wk[...]) + dot_nt(gv[:mem_rows], wv[...])
            if apart:
                gm[...] = gmf.astype(BF)
            else:
                gx[slot:] = gmf.astype(BF)
            gc = dot_nt(gq[slot:], wq[...]) * inverse
            akf[:slot] = (dot_nt(gk[mem_rows:], wk[...]) + dot_nt(gv[mem_rows:], wv[...])
                          + dot_nt(gq[:slot], wq[...]) + unpool(pm, gc))
            spread = unpool(pm, gmf * inverse) if lower else None
            for i in range(0, slot, CHUNK):
                r = slice(i, i + CHUNK)
                w = akf[r]
                xhat = xh0[r].astype(F32)
                acc[G0] += fold8(w * xhat)
                acc[S0] += fold8(w)
                total = ga[r] + norm_back(w * gain[0:1], xhat, rs[r, 0:1])
                if lower:
                    total = total + spread[i : i + CHUNK]
                gx[r] = total.astype(BF)
            acc[QB] += fold8(gq[...].astype(F32))
            acc[VB] += fold8(gv[...].astype(F32))

    @phase
    def _():
        small[...] = jnp.sum(acc[...], axis=1)


def sds(shape, dtype):
    return jax.ShapeDtypeStruct(shape, dtype)


def cost_of(flops, moved, special=0):
    return pl.CostEstimate(flops=int(flops), bytes_accessed=int(moved), transcendentals=int(special))


def kernel_params(limit=VMEM_LIMIT):
    return pltpu.CompilerParams(vmem_limit_bytes=limit)


SCALAR = pl.BlockSpec(memory_space=pltpu.SMEM)
NEAR = pl.BlockSpec(memory_space=pltpu.VMEM)


def window_scratch(slot, width):
    mem_rows = slot // 8
    one = [pltpu.VMEM((FRONT + slot + 16, width), BF), pltpu.VMEM((mem_rows, width), BF),
           pltpu.VMEM((mem_rows + 16, width), BF)]
    return one + one


def kept_shapes(slot, width, hid):
    every = slot + slot // 8
    shapes = [((every, width), BF), ((slot // 8, width), BF)] + [((every, width), BF)] * 3
    shapes += [((slot // TILE * (width // 256), 4 * ROWS, KEYS), BF), ((every, width), BF)] + [((slot, width), BF)] * 3
    return shapes + [((slot, 128), F32)] + [((slot, hid), BF)] * 2 + [((slot, width), BF)]


def grad_shapes(slot, width, hid):
    every = slot + slot // 8
    return [((slot, width), BF), ((slot, hid), BF)] + [((every, width), BF)] * 4


def forward(weights, utt, lower, scalars, slots, frames, kept):
    vec, ub, wq, wk, wv, wo, wu, wd = weights
    width, hid = wu.shape
    slot = frames.shape[1] if lower else frames.shape[0] // 9 * 8
    every = slot + slot // 8
    shapes = kept_shapes(slot, width, hid)
    ins = [scalars, vec, ub, frames, wq, wk, wv, wo, wu, wd]
    extra = list(kept) if kept is not None else []
    out = [sds((slots,) + s, t) for s, t in shapes] + [sds((every, width), BF)]
    res = pl.pallas_call(
        functools.partial(forward_kernel, utt, lower),
        in_specs=[SCALAR] + [NEAR] * (len(ins) - 1 + len(extra)),
        out_specs=[NEAR] * len(out),
        out_shape=out,
        scratch_shapes=window_scratch(slot, width) + [pltpu.VMEM((slot, width), F32)],
        input_output_aliases={len(ins) + i: i for i in range(len(extra))},
        compiler_params=kernel_params(),
        cost_estimate=cost_of(8 * every * width * width + 4 * slot * width * hid, 30 << 20, slot * hid * 2),
    )(*ins, *extra)
    return res[-1], res[:-1]


def pass_on(values, out):
    out[...] = values[...]


def opening(values):
    return pl.pallas_call(
        pass_on, in_specs=[NEAR], out_specs=NEAR, out_shape=sds(values.shape, values.dtype),
        compiler_params=kernel_params(1 << 20), cost_estimate=cost_of(1e12, 1 << 30),
    )(values)


def backward(weights, utt, lower, parts, scalars, slots, cot, gmem, ga, kept, grads):
    do_ffn, do_att = parts
    vec, ub, wq, wk, wv, wo, wu, wd = weights
    width, hid = wu.shape
    apart = gmem is not None
    slot = kept[7].shape[1]
    mem_rows = slot // 8
    every = slot + mem_rows
    shapes = dict(zip(GRADS, grad_shapes(slot, width, hid)))
    names = grads_of(do_ffn, do_att)
    ins = [scalars, vec, cot, gmem if apart else vec, ga if ga is not None else vec, wq, wk, wv, wo, wu, wd] + list(kept)
    extra = [grads[g] for g in names if grads[g] is not None]
    aliases = {len(ins) + i: place for i, place in enumerate(p for p, g in enumerate(names) if grads[g] is not None)}
    tiny = (8, 128)
    out = [sds((slots,) + shapes[g][0], BF) for g in names]
    out += [sds((slot if apart else every, width) if do_att else tiny, BF), sds((mem_rows, width) if apart and do_att else tiny, BF),
            sds((slot, width) if do_ffn else tiny, F32), sds((16, width), F32)]
    flops = (4 * slot * width * hid if do_ffn else 0) + (8 * every * width * width if do_att else 0)
    res = pl.pallas_call(
        functools.partial(backward_kernel, utt, lower, do_ffn, do_att, apart),
        in_specs=[SCALAR] + [NEAR] * (len(ins) - 1 + len(extra)),
        out_specs=[NEAR] * len(out), out_shape=out,
        scratch_shapes=window_scratch(slot, width) + [
            pltpu.VMEM((every, width), BF), pltpu.VMEM((FRONT + slot + 16, width), F32),
            pltpu.VMEM((mem_rows + 16, width), F32), pltpu.VMEM((16, 8, width), F32)],
        input_output_aliases=aliases, compiler_params=kernel_params(), cost_estimate=cost_of(flops, 20 << 20),
    )(*ins, *extra)
    grads = dict(grads)
    grads.update(zip(names, res))
    gx, gm, ga, small = res[len(names) :]
    return grads, gx, gm, ga, small


SMALL_LIMIT = 6 * 1024 * 1024
LANES_OUT = 4
STAGES = 4


def emit_group(value, me, more, out, part, j):
    if value is not None:
        part[...] = value
    sub = jnp.bitwise_and(me, LANES_OUT - 1)
    rows = part.shape[0] // LANES_OUT
    for r in range(LANES_OUT):
        got = part[pl.ds(pl.multiple_of(jnp.bitwise_xor(sub, r) * rows, rows), rows)]
        for ref, place in more:
            got = got + ref[place + j, r].astype(F32)
        out[j, r] = got.astype(out.dtype)


def pair_weights(chunk_left, low, span, places, me_ref, left, right, *refs):
    more = list(zip(refs, places))
    out, part = refs[-2:]
    me = me_ref[0]
    for j in range(out.shape[0]):
        start = jnp.bitwise_xor(j + low, jnp.right_shift(me, 2)) * 512
        chunk = pl.ds(pl.multiple_of(start, 512), 512)
        value = sum(dot_tn(left[u, :, chunk] if chunk_left else left[u], right[u] if chunk_left else right[u, :, chunk])
                    for u in span)
        emit_group(value, me, more, out, part, j)


def group_call(body, me, arrays, more, count, width, flops):
    return pl.pallas_call(
        functools.partial(body, tuple(place for _, place in more)),
        in_specs=[SCALAR] + [NEAR] * (len(arrays) + len(more)),
        out_specs=NEAR,
        out_shape=sds((count, LANES_OUT, width // LANES_OUT, width), BF),
        scratch_shapes=[pltpu.VMEM((width, width), F32)],
        compiler_params=kernel_params(),
        cost_estimate=cost_of(flops, 4 << 20),
    )(me, *arrays, *[a for a, _ in more])


def ffn_group_grads(groups, chunk_left, me, left, right, span, more=()):
    _, slot, _ = left.shape
    width = min(left.shape[2], right.shape[2])
    low, count = groups
    return group_call(functools.partial(pair_weights, chunk_left, low, span), me, (left, right), more, count,
                      width, 2 * len(span) * slot * count * width * width)


def attention_weights(low, span, places, me_ref, uc, mem, mix, gq, gk, gv, gz, *refs):
    more = list(zip(refs, places))
    out, part = refs[-2:]
    _, every, width = uc.shape
    mem_rows = every // 9
    slot = every - mem_rows
    me = me_ref[0]
    for j in range(out.shape[0]):
        which = jnp.bitwise_xor(j + low, jnp.right_shift(me, 2))

        @pl.when(which == 0)
        def _():
            part[...] = sum(dot_tn(uc[u], gq[u]) for u in span)

        for place, ref in ((1, gk), (2, gv)):
            @pl.when(which == place)
            def _():
                part[...] = sum(dot_tn(mem[u], ref[u, :mem_rows]) + dot_tn(uc[u, :slot], ref[u, mem_rows:])
                                for u in span)

        @pl.when(which == 3)
        def _():
            part[...] = sum(dot_tn(mix[u], gz[u]) for u in span)

        emit_group(None, me, more, out, part, j)


def attention_group_grads(groups, me, arrays, span, more=()):
    _, every, width = arrays[0].shape
    low, count = groups
    return group_call(functools.partial(attention_weights, low, span), me, arrays, more, count, width,
                      2 * count * len(span) * every * width * width)


def restore_group(parts, me, value):
    place = jnp.bitwise_xor(pl.program_id(0), jnp.right_shift(me, 2))
    sub = jnp.bitwise_and(me, LANES_OUT - 1)
    for i, ref in enumerate(parts):
        @pl.when(place == i)
        def _():
            for r in range(LANES_OUT):
                value(r, ref[jnp.bitwise_xor(sub, r)].astype(F32))


def restore_wide(me_ref, *refs):
    *parts, out = refs
    rows = parts[0].shape[1]

    def put(r, got):
        out[0, r * rows : (r + 1) * rows] = got

    restore_group(parts, me_ref[0], put)


def restore_square(me_ref, *refs):
    parts, outs = refs[:4], refs[4:]
    rows = parts[0].shape[1]

    def put(r, got):
        for matrix, out in enumerate(outs):
            @pl.when(pl.program_id(0) == matrix)
            def _():
                out[0, r * rows : (r + 1) * rows] = got

    restore_group(parts, me_ref[0], put)


def restore(me, parts, kind):
    groups = len(parts)
    width = parts[0].shape[2]
    whole = pl.BlockSpec(parts[0].shape, lambda j, me: (0, 0, 0))
    if kind == "down":
        body, shapes = restore_wide, [(1, groups * width, width)]
        specs = [pl.BlockSpec((1, width, width), lambda j, me: (0, j, 0))]
    elif kind == "up":
        body, shapes = restore_wide, [(1, width, groups * width)]
        specs = [pl.BlockSpec((1, width, width), lambda j, me: (0, 0, j))]
    else:
        body, shapes = restore_square, [(1, width, width)] * groups
        specs = [pl.BlockSpec((1, width, width), lambda j, me: (0, 0, 0))] * groups
    return pl.pallas_call(
        body,
        grid_spec=pltpu.PrefetchScalarGridSpec(num_scalar_prefetch=1, grid=(groups,), in_specs=[whole] * groups,
                                               out_specs=specs),
        out_shape=[sds(s, F32) for s in shapes],
        compiler_params=pltpu.CompilerParams(vmem_limit_bytes=SMALL_LIMIT, dimension_semantics=("arbitrary",)),
        cost_estimate=cost_of(0, 6 * groups * width * width),
    )(me, *parts)


def swap(value, bit):
    n = lax.axis_size("dp")
    return lax.ppermute(value, "dp", [(i, i ^ (1 << bit)) for i in range(n)])


def added(a, b):
    return (a.astype(F32) + b.astype(F32)).astype(BF)


PLAN = "d1d2ududsudsusudsDsuUsS"
PATHS = {"d": (0, 1, 2, 3), "u": (0, 1, 2, 3), "s": (0, 1, 2, 3)}
KINDS = {"D": ("d", "down"), "U": ("u", "up"), "S": ("s", "square")}


class Order:
    def __init__(self):
        self.last = None

    def after(self, *values):
        if self.last is not None:
            values = lax.optimization_barrier((*values, self.last))[:-1]
        return values

    def made(self, value):
        self.last = value


class Sum:
    def __init__(self, order, path, bits, value, small=None):
        self.order = order
        self.path = path
        self.bits = bits
        self.value = value.reshape((-1,) + value.shape[2:])
        self.small = small
        self.stage = 1
        self.launch()

    def launch(self):
        if self.stage < STAGES:
            half = self.value.shape[0] // 2
            out, self.value = self.value[half:], self.value[:half]
            if self.small is not None:
                width = out.shape[-1]
                high = lax.reduce_precision(self.small, exponent_bits=8, mantissa_bits=7)
                parts = [out.reshape(-1, width), high.astype(BF), (self.small - high).astype(BF)]
                out = jnp.concatenate(parts, axis=0)
            bit = self.path[self.stage]
        else:
            out = self.value
            bit = self.path[2 * STAGES - 1 - self.stage]
        self.order.made(out)
        self.got = swap(out, bit)
        if self.stage == 2 * STAGES - 2:
            self.far = [swap(out, self.path[0])]

    def step(self):
        got, value = self.order.after(self.got, self.value)
        if self.stage < STAGES:
            if self.small is not None:
                lines = value.shape[0] * value.shape[1]
                rows = self.small.shape[0]
                self.small = self.small + got[lines : lines + rows].astype(F32) + got[lines + rows :].astype(F32)
                got = got[:lines].reshape(value.shape)
            value = added(value, got)
            if self.stage == STAGES - 1:
                for bit in range(STAGES, self.bits):
                    value = added(value, swap(value, bit))
                    if self.small is not None:
                        self.small = self.small + swap(self.small, bit)
        elif self.stage < 2 * STAGES - 2:
            value = jnp.concatenate([value, got], axis=0)
        else:
            self.far.append(swap(got, self.path[0]))
            self.order.made(got)
            self.parts = [value, got] + self.far
            return
        self.value = value
        self.stage += 1
        self.launch()

    def restore(self, me, kind):
        parts = self.order.after(*self.parts)
        outs = restore(me, parts, kind)
        self.order.made(outs[0])
        return outs


def shifted(block, axis, distance):
    devices = range(lax.axis_size(axis))
    route = [(i - distance, i) for i in devices if i - distance in devices]
    return lax.ppermute(block, axis, route)


def on_device(ends, lengths, seg_group, norm_gain, norm_shift, w_query, w_key, w_value, qv_bias, w_out, out_bias,
              w_up, up_bias, w_down, down_bias):
    section = lax.axis_index("section")
    first = section == 0
    slots = lengths.shape[0]
    width = ends.shape[2]
    slot = ends.shape[1] // slots
    hid = w_up.shape[2]
    section = section.astype(jnp.int32).reshape(1)
    lower = jnp.concatenate([1 - section, lengths, seg_group])
    upper = jnp.concatenate([section, lengths, seg_group])

    bits = lax.axis_size("dp").bit_length() - 1
    place = lax.axis_index("dp").astype(jnp.int32)
    codes = {
        name: sum(jnp.bitwise_and(jnp.right_shift(place, bit), 1) << (STAGES - 1 - s) for s, bit in enumerate(path)).reshape(1)
        for name, path in PATHS.items()}

    vec = jnp.concatenate([norm_gain[0], norm_shift[0], qv_bias[0], out_bias, down_bias], axis=0)
    vec, lower, upper, codes, first = lax.optimization_barrier((vec, lower, upper, codes, first))
    vec = opening(vec)
    weights = (vec, up_bias, w_query[0], w_key[0], w_value[0], w_out[0], w_up[0], w_down[0])
    local = ends.reshape(slots, slot, width)

    kept = None
    sent = []
    for b in range(slots):
        y, kept = forward(weights, b, True, lower, slots, local, kept)
        sent.append(shifted(y, "section", 1))
    finals = []
    grads = dict.fromkeys(GRADS)
    smalls = [[], []]
    back = []
    for b in range(slots):
        y, kept = forward(weights, b, False, upper, slots, sent[b], kept)
        finals.append(y)
        apart = vec if b == slots - 1 else None
        grads, gx, gm, _, small = backward(weights, b, False, (True, True), upper, slots, local, apart, None, kept, grads)
        smalls[1].append(small)
        back.append(shifted(gx, "section", -1))
    memory_back = shifted(gm, "section", -1)
    held = dict(zip(KEPT, kept))
    firsts = []
    for b in range(slots - 1):
        grads, gx, _, _, small = backward(weights, b, True, (True, True), lower, slots, back[b], None, None, kept, grads)
        smalls[0].append(small)
        firsts.append(gx)
    b = slots - 1
    sides = (("d", True, "g", "gd"), ("u", False, "h", "gf"))
    early = tuple(ffn_group_grads((0, 4), side, codes[name], held[left], grads[right], range(b))
                  for name, side, left, right in sides)
    arrays = [held[name] for name in ("uc", "mem", "mix")] + [grads[name] for name in ("gq", "gk", "gv", "gz")]
    early += (attention_group_grads((0, 4), codes["s"], arrays, range(b)),)
    last, *early = lax.optimization_barrier((back[b], *early))
    grads, _, _, ga, small = backward(weights, b, True, (True, False), lower, slots, last, vec, None, kept, grads)
    smalls[0].append(small)

    order = Order()
    now = range(b, slots)
    far = [swap(ffn_group_grads((2, 2), side, codes[name], held[left], grads[right], now, [(part, 2)]), 0)
           for (name, side, left, right), part in zip(sides, early)]
    down, up = [ffn_group_grads((0, 2), side, codes[name], held[left], grads[right], now, [(part, 0), (more, 0)])
                for (name, side, left, right), part, more in zip(sides, early, far)]
    ga, down, up = lax.optimization_barrier((ga, down, up))
    down = Sum(order, PATHS["d"], bits, down)
    up = Sum(order, PATHS["u"], bits, up)
    grads, gx, _, _, small = backward(weights, b, True, (False, True), lower, slots, last, memory_back, ga, kept, grads)
    smalls[0].append(small)
    firsts.append(gx)
    small = jnp.where(first, sum(smalls[0]), sum(smalls[1]))

    names = ("gq", "gk", "gv", "gz")
    arrays = [held[name] for name in ("uc", "mem", "mix")] + [grads[name] for name in names]
    streams = {"d": down, "u": up}
    outs = {}
    for event in PLAN:
        if event == "1":
            arrays[-1], small = order.after(arrays[-1], small)
            away = swap(attention_group_grads((2, 2), codes["s"], arrays, now, [(early[2], 2)]), 0)
            small = small + swap(small, 0)
        elif event == "2":
            away, small = order.after(away, small)
            streams["s"] = Sum(order, PATHS["s"], bits, attention_group_grads((0, 2), codes["s"], arrays, now, [(early[2], 0), (away, 0)]), small)
        elif event in KINDS:
            if event == "U":
                small = streams["s"].small
                small_outs = (small[None, 0:3], small[None, 3:6], small[None, 6:8], small[8:9], small[9:10],
                              small[10 : 10 + hid // width].reshape(1, hid))
                streams["u"].parts[0], *small_outs = order.after(streams["u"].parts[0], *small_outs)
            outs[event] = streams[KINDS[event][0]].restore(codes[KINDS[event][0]], KINDS[event][1])
        else:
            streams[event].step()
    (grad_down,), (grad_up,), (grad_q, grad_k, grad_v, grad_o) = outs["D"], outs["U"], outs["S"]
    grad_gain, grad_shift, grad_qv, grad_out, grad_down_bias, grad_up_bias = small_outs
    ends_out = jnp.where(first, jnp.stack([gx[:slot] for gx in firsts]), jnp.stack([y[:slot] for y in finals]))
    ends_out = ends_out.reshape(1, slots * slot, width)
    return (ends_out, grad_gain, grad_shift, grad_q, grad_k, grad_v, grad_qv, grad_o, grad_out, grad_up, grad_up_bias,
            grad_down, grad_down_bias)


def solution(mesh):
    placed = (
        P("section", "dp", None), P("dp"), P("dp"),
        P("section", None, None), P("section", None, None), P("section", None, None), P("section", None, None),
        P("section", None, None), P("section", None, None), P("section", None, None), P("section", None),
        P("section", None, None), P("section", None), P("section", None, None), P("section", None),
    )
    return jax.shard_map(
        on_device,
        mesh=mesh,
        in_specs=placed,
        out_specs=(
            P("section", "dp", None), P("section", None, None), P("section", None, None), P("section", None, None),
            P("section", None, None), P("section", None, None), P("section", None, None), P("section", None, None),
            P("section", None), P("section", None, None), P("section", None), P("section", None, None),
            P("section", None),
        ),
        check_vma=False,
    )
```

```python
import functools
import jax
import jax.numpy as jnp
from jax import lax
from jax.experimental import pallas as pl
from jax.experimental.pallas import tpu as pltpu
from jax.sharding import PartitionSpec as P

LEFT = 30
RIGHT = 4
MEM = 4
TILE = 64
KEYS = 128
ROWS = 80
FRONT = 32
BF = jnp.bfloat16
F32 = jnp.float32
VMEM_LIMIT = 5 * 1024 * 1024


def dot(a, b):
    return lax.dot_general(a, b, (((1,), (0,)), ((), ())), preferred_element_type=F32)


def dot_nt(a, b):
    return lax.dot_general(a, b, (((1,), (1,)), ((), ())), preferred_element_type=F32)


def dot_tn(a, b):
    return lax.dot_general(a, b, (((0,), (0,)), ((), ())), preferred_element_type=F32)


def normed(value):
    center = value - jnp.mean(value, axis=-1, keepdims=True)
    rs = lax.rsqrt(jnp.mean(center * center, axis=-1, keepdims=True) + 1e-05)
    return center * rs, rs


def norm_back(w, xhat, rs):
    return (w - jnp.mean(w, axis=-1, keepdims=True) - xhat * jnp.mean(w * xhat, axis=-1, keepdims=True)) * rs


def fold8(value):
    rows, width = value.shape
    return jnp.sum(value.reshape(rows // 8, 8, width), axis=0)


def gelu_parts(f):
    phi = 0.5 + 0.5 * lax.erf(f * 0.7071067811865476)
    return f * phi, phi + f * (jnp.exp(f * f * -0.5) * 0.3989422804014327)


def seg_sizes(wide):
    return jnp.where(wide, 16, 8).astype(jnp.int32), jnp.where(wide, 4, 8).astype(jnp.int32)


def pool_matrix(length, wide, slot):
    seg, per = seg_sizes(wide)
    rows = slot // 8
    e = lax.broadcasted_iota(jnp.int32, (rows, slot), 0)
    t = lax.broadcasted_iota(jnp.int32, (rows, slot), 1)
    r = jnp.bitwise_and(e, 7)
    start = jnp.right_shift(e, 3) * TILE + r * seg
    inside = (t >= start) & (t < start + seg) & (t < length) & (r < per)
    e1 = lax.broadcasted_iota(jnp.int32, (rows, 1), 0)
    r1 = jnp.bitwise_and(e1, 7)
    start1 = jnp.right_shift(e1, 3) * TILE + r1 * seg
    count = jnp.where(r1 < per, jnp.clip(length - start1, 0, seg), 0)
    inverse = 1.0 / jnp.maximum(count, 1).astype(F32)
    return jnp.where(inside, 1.0, 0.0).astype(BF), inverse


def unpool(matrix, value):
    high = value.astype(BF)
    low = (value - high.astype(F32)).astype(BF)
    return dot_tn(jnp.concatenate([matrix, matrix], axis=0), jnp.concatenate([high, low], axis=0))


def tile_bias(tile, odd, length, wide):
    seg, per = seg_sizes(wide)
    row = lax.broadcasted_iota(jnp.int32, (ROWS, 1), 0)
    col = lax.broadcasted_iota(jnp.int32, (1, KEYS), 1)
    anchor = tile * TILE
    is_frame = row < TILE
    extra = row - TILE
    shift = jnp.where(wide, 4, 3).astype(jnp.int32)
    r = jnp.where(is_frame, jnp.right_shift(row, shift), jnp.bitwise_and(extra, 7))
    owned = is_frame | ((jnp.right_shift(extra, 3) == odd) & (r < per))
    key = col - (16 + FRONT)
    low = jnp.where(owned, r * seg - LEFT, 100000)
    high = jnp.minimum(r * seg + seg + RIGHT, length - anchor)
    frame_ok = (key >= jnp.maximum(low, -anchor)) & (key < high) & (col >= 16)
    c = jnp.bitwise_and(col, 7)
    slot = jnp.where((col < 16) & (c < per), jnp.where(col < 8, c - per, c), -100000)
    slot = jnp.where((col < 8) & (anchor == 0), -100000, slot)
    mem_ok = (slot >= r - MEM) & (slot < jnp.where(is_frame, r, -100000))
    return jnp.where(frame_ok | mem_ok, 0.0, -1e30).astype(F32)


def head_masks(rows):
    lane = jnp.right_shift(lax.broadcasted_iota(jnp.int32, (rows, 256), 1), 6)
    return [lane == h for h in range(4)]


def spread_heads(tile, masks):
    zero = jnp.zeros_like(tile)
    return jnp.concatenate([jnp.where(m, tile, zero) for m in masks], axis=0)


def gather_heads(stack, masks):
    total = jnp.where(masks[0], stack[:ROWS], 0.0)
    for h in range(1, 4):
        total = jnp.where(masks[h], stack[h * ROWS : (h + 1) * ROWS], total)
    return total


def key_window(tile, lanes, frames_ref, even_ref, pad_ref):
    first = tile // 2 * 16
    memory = even_ref[first : first + 16, lanes] if tile % 2 else pad_ref[first : first + 16, lanes]
    return jnp.concatenate([memory, frames_ref[tile * TILE : tile * TILE + KEYS - 16, lanes]], axis=0)


def fill_windows(all_rows, frames_ref, even_ref, pad_ref, mem_rows, slot):
    width = all_rows.shape[1]
    memory = all_rows[:mem_rows].astype(F32)
    blank = jnp.zeros((8, width), F32)
    even_ref[...] = memory.astype(BF)
    pad_ref[...] = jnp.concatenate([blank, memory, blank], axis=0).astype(BF)
    frames_ref[:FRONT] = jnp.zeros((FRONT, width), BF)
    frames_ref[FRONT : FRONT + slot] = all_rows[mem_rows:].astype(BF)
    frames_ref[FRONT + slot :] = jnp.zeros((16, width), BF)


CHUNK = 32
G0, G1, G2, S0, S1, S2, QB, VB, OB, DB, UB = range(11)
KEPT = ("uc", "mem", "q", "k", "v", "prob", "mix", "xh0", "xh1", "h", "rs", "g", "gp", "xh2")
GRADS = ("gd", "gf", "gz", "gq", "gk", "gv")


def grads_of(do_ffn, do_att):
    return [g for g in GRADS if (do_ffn and g in GRADS[:3]) or (do_att and g in GRADS[2:])]


def forward_kernel(utt, lower, on_ref, vec, ub, x_ref, wq, wk, wv, wo, wu, wd, *refs):
    n = len(KEPT)
    slots = (on_ref.shape[0] - 1) // 2
    if lower:
        x_ref = x_ref.at[utt]
    kf, ke, kp, vf, ve, vp, after = refs[-7:]
    y = refs[-8]
    near = {name: ref.at[utt] for name, ref in zip(KEPT, refs[-8 - n : -8])}
    slot, width = after.shape
    mem_rows = slot // 8
    length = on_ref[1 + utt]
    wide = on_ref[1 + slots + utt] == 1
    gain, shift, qvb, ob, db = vec.at[0:3], vec.at[3:6], vec.at[6:8], vec.at[8:9], vec.at[9:10]

    uc, mem, q, k, v, prob, mix = (near[name] for name in KEPT[:7])
    rs = near["rs"]
    lane = lax.broadcasted_iota(jnp.int32, (1, 128), 1)
    phase = pl.when(on_ref[0] == 1)


    @phase
    def _():
        for i in range(0, slot, CHUNK):
            r = slice(i, i + CHUNK)
            xhat, scale = normed(x_ref[r].astype(F32))
            near["xh0"][r] = xhat.astype(BF)
            uc[r] = (xhat * gain[0:1] + shift[0:1]).astype(BF)
            rs[r] = jnp.broadcast_to(scale, (CHUNK, 128))
        pm, inverse = pool_matrix(length, wide, slot)
        uc[slot:] = (dot(pm, uc[:slot]) * inverse).astype(BF)
        if lower:
            mem[...] = (dot(pm, x_ref[:slot]) * inverse).astype(BF)
        else:
            mem[...] = x_ref[slot:]


    @phase
    def _():
        q[...] = (dot(uc[...], wq[...]) + qvb[0:1]).astype(BF)
        k[:mem_rows] = dot(mem[...], wk[...]).astype(BF)
        k[mem_rows:] = dot(uc[:slot], wk[...]).astype(BF)
        v[:mem_rows] = (dot(mem[...], wv[...]) + qvb[1:2]).astype(BF)
        v[mem_rows:] = (dot(uc[:slot], wv[...]) + qvb[1:2]).astype(BF)
        fill_windows(k[...], kf, ke, kp, mem_rows, slot)
        fill_windows(v[...], vf, ve, vp, mem_rows, slot)


    @phase
    def _():
        masks = head_masks(ROWS)
        for pair in range(slot // (2 * TILE)):
            srows = slice(slot + pair * 16, slot + pair * 16 + 16)
            biases = [tile_bias(pair * 2 + odd, odd, length, wide) for odd in range(2)]
            for quad in range(width // 256):
                lanes = slice(quad * 256, quad * 256 + 256)
                extra = None
                for odd in range(2):
                    tile = pair * 2 + odd
                    rows = slice(tile * TILE, tile * TILE + TILE)
                    qs = spread_heads(jnp.concatenate([q[rows, lanes], q[srows, lanes]], axis=0), masks)
                    kw = key_window(tile, lanes, kf, ke, kp)
                    vw = key_window(tile, lanes, vf, ve, vp)
                    s = dot_nt(qs, kw).reshape(4, ROWS, KEYS) * 0.125 + biases[odd][None]
                    peak = jnp.maximum(jnp.max(s, axis=-1, keepdims=True), -1e29)
                    e = jnp.exp(s - peak)
                    total = jnp.sum(e, axis=-1, keepdims=True)
                    p = (e * (1.0 / jnp.maximum(total, 1e-30))).astype(BF).reshape(4 * ROWS, KEYS)
                    prob[pair * 4 + quad * 2 + odd] = p
                    o = gather_heads(dot(p, vw), masks)
                    mix[rows, lanes] = o[:TILE].astype(BF)
                    extra = o[TILE:] if extra is None else extra + o[TILE:]
                mix[srows, lanes] = extra.astype(BF)


    @phase
    def _():
        z = dot(mix[...], wo[...]) + ob[...]
        y[slot:] = z[slot:].astype(BF)
        after[...] = z[:slot]
        for i in range(0, slot, CHUNK):
            r = slice(i, i + CHUNK)
            a = x_ref[r].astype(F32) + after[r]
            after[r] = a + db[...]
            xhat, scale = normed(a)
            near["xh1"][r] = xhat.astype(BF)
            near["h"][r] = (xhat * gain[1:2] + shift[1:2]).astype(BF)
            rs[r] = jnp.where(lane == 0, rs[r], jnp.broadcast_to(scale, (CHUNK, 128)))

    for c in range(wu.shape[1] // 512):
        cols = slice(c * 512, c * 512 + 512)

        @phase
        def _():
            act, slope = gelu_parts(dot(near["h"][...], wu[:, cols]) + ub[:, cols])
            act = act.astype(BF)
            near["g"][:, cols] = act
            near["gp"][:, cols] = slope.astype(BF)
            after[...] += dot(act, wd[cols])

    @phase
    def _():
        for i in range(0, slot, CHUNK):
            r = slice(i, i + CHUNK)
            xhat, scale = normed(after[r])
            near["xh2"][r] = xhat.astype(BF)
            rs[r] = jnp.where(lane == 2, jnp.broadcast_to(scale, (CHUNK, 128)), rs[r])
            t = lax.broadcasted_iota(jnp.int32, (CHUNK, 1), 0) + i
            valid = jnp.where(t < length, 1.0, 0.0)
            y[r] = ((xhat * gain[2:3] + shift[2:3]) * valid).astype(BF)


def backward_kernel(utt, lower, do_ffn, do_att, apart, on_ref, vec, cot, gmem, ga_in,
                    wq, wk, wv, wo, wu, wd, *refs):
    kept = {name: ref.at[utt] for name, ref in zip(KEPT, refs)}
    names = grads_of(do_ffn, do_att)
    kf, ke, kp, vf, ve, vp, gom, akf, akm, acc = refs[-10:]
    gx, gm, ga_out, small = refs[-14:-10]
    near = {name: ref.at[utt] for name, ref in zip(names, refs[-14 - len(names) : -14])}
    slot, width = kept["xh0"].shape
    mem_rows = slot // 8
    slots = (on_ref.shape[0] - 1) // 2
    length = on_ref[1 + utt]
    wide = on_ref[1 + slots + utt] == 1
    gain = vec.at[0:3]
    cot = cot if lower else cot.at[utt]
    gz = near["gz"]
    q, k, v, prob, xh0, xh1, xh2, rs, gp = (kept[name] for name in
                                            ("q", "k", "v", "prob", "xh0", "xh1", "xh2", "rs", "gp"))
    phase = pl.when(on_ref[0] == 1)

    @phase
    def _():
        acc[...] = jnp.zeros_like(acc)

    if do_ffn:
        gd, gf = near["gd"], near["gf"]
        ga = ga_out

        @phase
        def _():
            for i in range(0, slot, CHUNK):
                r = slice(i, i + CHUNK)
                t = lax.broadcasted_iota(jnp.int32, (CHUNK, 1), 0) + i
                gy = cot[r].astype(F32) * jnp.where(t < length, 1.0, 0.0)
                xhat = xh2[r].astype(F32)
                acc[G2] += fold8(gy * xhat)
                acc[S2] += fold8(gy)
                ga2 = norm_back(gy * gain[2:3], xhat, rs[r, 2:3])
                ga[r] = ga2
                low = ga2.astype(BF)
                gd[r] = low
                acc[DB] += fold8(low.astype(F32))

        for c in range(wu.shape[1] // 512):
            cols = slice(c * 512, c * 512 + 512)

            @phase
            def _():
                gfl = (dot_nt(gd[...], wd[cols]) * gp[:, cols].astype(F32)).astype(BF)
                gf[:, cols] = gfl
                acc[UB + c] += fold8(gfl.astype(F32))
                part = dot_nt(gfl, wu[:, cols])
                if c == 0:
                    akf[:slot] = part
                else:
                    akf[:slot] += part

        @phase
        def _():
            for i in range(0, slot, CHUNK):
                r = slice(i, i + CHUNK)
                back = akf[r]
                xhat = xh1[r].astype(F32)
                acc[G1] += fold8(back * xhat)
                acc[S1] += fold8(back)
                total = ga[r] + norm_back(back * gain[1:2], xhat, rs[r, 1:2])
                ga[r] = total
                low = total.astype(BF)
                gz[r] = low
                acc[OB] += fold8(low.astype(F32))
    else:
        ga = ga_in
    if do_att:
        gq, gk, gv = near["gq"], near["gk"], near["gv"]

        @phase
        def _():
            far = (gmem[...] if apart else cot[slot:]) if lower else jnp.zeros((mem_rows, width), BF)
            gz[slot:] = far
            if lower:
                acc[OB] += fold8(far.astype(F32))
            gom[...] = dot_nt(gz[...], wo[...]).astype(BF)
            fill_windows(k[...], kf, ke, kp, mem_rows, slot)
            fill_windows(v[...], vf, ve, vp, mem_rows, slot)

        for quad in range(width // 256):
            lanes = slice(quad * 256, quad * 256 + 256)

            @phase
            def _():
                masks = head_masks(ROWS)
                akf[...] = jnp.zeros_like(akf)
                akm[...] = jnp.zeros_like(akm)
                for pair in range(slot // (2 * TILE)):
                    srows = slice(slot + pair * 16, slot + pair * 16 + 16)
                    extra = None
                    for odd in range(2):
                        tile = pair * 2 + odd
                        rows = slice(tile * TILE, tile * TILE + TILE)
                        qs = spread_heads(jnp.concatenate([q[rows, lanes], q[srows, lanes]], axis=0), masks)
                        go = spread_heads(jnp.concatenate([gom[rows, lanes], gom[srows, lanes]], axis=0), masks)
                        kw = key_window(tile, lanes, kf, ke, kp)
                        vw = key_window(tile, lanes, vf, ve, vp)
                        p = prob[pair * 4 + quad * 2 + odd]
                        gprob = dot_nt(go, vw) * p.astype(F32)
                        gs = (gprob - p.astype(F32) * jnp.sum(gprob, axis=-1, keepdims=True)).astype(BF)
                        gqt = gather_heads(dot(gs, kw), masks) * 0.125
                        gq[rows, lanes] = gqt[:TILE].astype(BF)
                        extra = gqt[TILE:] if extra is None else extra + gqt[TILE:]
                        for place, got in ((0, dot_tn(gs, qs) * 0.125), (256, dot_tn(p, go))):
                            cols = slice(place, place + 256)
                            akm[tile * 8 : tile * 8 + 16, cols] += got[:16]
                            akf[tile * TILE : tile * TILE + KEYS - 16, cols] += got[16:]
                    gq[srows, lanes] = extra.astype(BF)
                for out, place in ((gk, 0), (gv, 256)):
                    cols = slice(place, place + 256)
                    out[:mem_rows, lanes] = akm[8 : 8 + mem_rows, cols].astype(BF)
                    out[mem_rows:, lanes] = akf[FRONT : FRONT + slot, cols].astype(BF)

        @phase
        def _():
            pm, inverse = pool_matrix(length, wide, slot)
            gmf = dot_nt(gk[:mem_rows], wk[...]) + dot_nt(gv[:mem_rows], wv[...])
            if apart:
                gm[...] = gmf.astype(BF)
            else:
                gx[slot:] = gmf.astype(BF)
            gc = dot_nt(gq[slot:], wq[...]) * inverse
            akf[:slot] = (dot_nt(gk[mem_rows:], wk[...]) + dot_nt(gv[mem_rows:], wv[...])
                          + dot_nt(gq[:slot], wq[...]) + unpool(pm, gc))
            spread = unpool(pm, gmf * inverse) if lower else None
            for i in range(0, slot, CHUNK):
                r = slice(i, i + CHUNK)
                w = akf[r]
                xhat = xh0[r].astype(F32)
                acc[G0] += fold8(w * xhat)
                acc[S0] += fold8(w)
                total = ga[r] + norm_back(w * gain[0:1], xhat, rs[r, 0:1])
                if lower:
                    total = total + spread[i : i + CHUNK]
                gx[r] = total.astype(BF)
            acc[QB] += fold8(gq[...].astype(F32))
            acc[VB] += fold8(gv[...].astype(F32))

    @phase
    def _():
        small[...] = jnp.sum(acc[...], axis=1)


def sds(shape, dtype):
    return jax.ShapeDtypeStruct(shape, dtype)


def cost_of(flops, moved, special=0):
    return pl.CostEstimate(flops=int(flops), bytes_accessed=int(moved), transcendentals=int(special))


def kernel_params(limit=VMEM_LIMIT):
    return pltpu.CompilerParams(vmem_limit_bytes=limit)


SCALAR = pl.BlockSpec(memory_space=pltpu.SMEM)
NEAR = pl.BlockSpec(memory_space=pltpu.VMEM)


def window_scratch(slot, width):
    mem_rows = slot // 8
    one = [pltpu.VMEM((FRONT + slot + 16, width), BF), pltpu.VMEM((mem_rows, width), BF),
           pltpu.VMEM((mem_rows + 16, width), BF)]
    return one + one


def kept_shapes(slot, width, hid):
    every = slot + slot // 8
    shapes = [((every, width), BF), ((slot // 8, width), BF)] + [((every, width), BF)] * 3
    shapes += [((slot // TILE * (width // 256), 4 * ROWS, KEYS), BF), ((every, width), BF)] + [((slot, width), BF)] * 3
    return shapes + [((slot, 128), F32)] + [((slot, hid), BF)] * 2 + [((slot, width), BF)]


def grad_shapes(slot, width, hid):
    every = slot + slot // 8
    return [((slot, width), BF), ((slot, hid), BF)] + [((every, width), BF)] * 4


def forward(weights, utt, lower, scalars, slots, frames, kept):
    vec, ub, wq, wk, wv, wo, wu, wd = weights
    width, hid = wu.shape
    slot = frames.shape[1] if lower else frames.shape[0] // 9 * 8
    every = slot + slot // 8
    shapes = kept_shapes(slot, width, hid)
    ins = [scalars, vec, ub, frames, wq, wk, wv, wo, wu, wd]
    extra = list(kept) if kept is not None else []
    out = [sds((slots,) + s, t) for s, t in shapes] + [sds((every, width), BF)]
    res = pl.pallas_call(
        functools.partial(forward_kernel, utt, lower),
        in_specs=[SCALAR] + [NEAR] * (len(ins) - 1 + len(extra)),
        out_specs=[NEAR] * len(out),
        out_shape=out,
        scratch_shapes=window_scratch(slot, width) + [pltpu.VMEM((slot, width), F32)],
        input_output_aliases={len(ins) + i: i for i in range(len(extra))},
        compiler_params=kernel_params(),
        cost_estimate=cost_of(8 * every * width * width + 4 * slot * width * hid, 30 << 20, slot * hid * 2),
    )(*ins, *extra)
    return res[-1], res[:-1]


def pass_on(values, out):
    out[...] = values[...]


def opening(values):
    return pl.pallas_call(
        pass_on, in_specs=[NEAR], out_specs=NEAR, out_shape=sds(values.shape, values.dtype),
        compiler_params=kernel_params(1 << 20), cost_estimate=cost_of(1e12, 1 << 30),
    )(values)


def backward(weights, utt, lower, parts, scalars, slots, cot, gmem, ga, kept, grads):
    do_ffn, do_att = parts
    vec, ub, wq, wk, wv, wo, wu, wd = weights
    width, hid = wu.shape
    apart = gmem is not None
    slot = kept[7].shape[1]
    mem_rows = slot // 8
    every = slot + mem_rows
    shapes = dict(zip(GRADS, grad_shapes(slot, width, hid)))
    names = grads_of(do_ffn, do_att)
    ins = [scalars, vec, cot, gmem if apart else vec, ga if ga is not None else vec, wq, wk, wv, wo, wu, wd] + list(kept)
    extra = [grads[g] for g in names if grads[g] is not None]
    aliases = {len(ins) + i: place for i, place in enumerate(p for p, g in enumerate(names) if grads[g] is not None)}
    tiny = (8, 128)
    out = [sds((slots,) + shapes[g][0], BF) for g in names]
    out += [sds((slot if apart else every, width) if do_att else tiny, BF), sds((mem_rows, width) if apart and do_att else tiny, BF),
            sds((slot, width) if do_ffn else tiny, F32), sds((16, width), F32)]
    flops = (4 * slot * width * hid if do_ffn else 0) + (8 * every * width * width if do_att else 0)
    res = pl.pallas_call(
        functools.partial(backward_kernel, utt, lower, do_ffn, do_att, apart),
        in_specs=[SCALAR] + [NEAR] * (len(ins) - 1 + len(extra)),
        out_specs=[NEAR] * len(out), out_shape=out,
        scratch_shapes=window_scratch(slot, width) + [
            pltpu.VMEM((every, width), BF), pltpu.VMEM((FRONT + slot + 16, width), F32),
            pltpu.VMEM((mem_rows + 16, width), F32), pltpu.VMEM((16, 8, width), F32)],
        input_output_aliases=aliases, compiler_params=kernel_params(), cost_estimate=cost_of(flops, 20 << 20),
    )(*ins, *extra)
    grads = dict(grads)
    grads.update(zip(names, res))
    gx, gm, ga, small = res[len(names) :]
    return grads, gx, gm, ga, small


SMALL_LIMIT = 6 * 1024 * 1024
LANES_OUT = 4
STAGES = 4


def emit_group(value, me, more, out, part, j):
    if value is not None:
        part[...] = value
    sub = jnp.bitwise_and(me, LANES_OUT - 1)
    rows = part.shape[0] // LANES_OUT
    for r in range(LANES_OUT):
        got = part[pl.ds(pl.multiple_of(jnp.bitwise_xor(sub, r) * rows, rows), rows)]
        for ref, place in more:
            got = got + ref[place + j, r].astype(F32)
        out[j, r] = got.astype(out.dtype)


def pair_weights(chunk_left, low, span, places, me_ref, left, right, *refs):
    more = list(zip(refs, places))
    out, part = refs[-2:]
    me = me_ref[0]
    for j in range(out.shape[0]):
        start = jnp.bitwise_xor(j + low, jnp.right_shift(me, 2)) * 512
        chunk = pl.ds(pl.multiple_of(start, 512), 512)
        value = sum(dot_tn(left[u, :, chunk] if chunk_left else left[u], right[u] if chunk_left else right[u, :, chunk])
                    for u in span)
        emit_group(value, me, more, out, part, j)


def group_call(body, me, arrays, more, count, width, flops):
    return pl.pallas_call(
        functools.partial(body, tuple(place for _, place in more)),
        in_specs=[SCALAR] + [NEAR] * (len(arrays) + len(more)),
        out_specs=NEAR,
        out_shape=sds((count, LANES_OUT, width // LANES_OUT, width), BF),
        scratch_shapes=[pltpu.VMEM((width, width), F32)],
        compiler_params=kernel_params(),
        cost_estimate=cost_of(flops, 4 << 20),
    )(me, *arrays, *[a for a, _ in more])


def ffn_group_grads(groups, chunk_left, me, left, right, span, more=()):
    _, slot, _ = left.shape
    width = min(left.shape[2], right.shape[2])
    low, count = groups
    return group_call(functools.partial(pair_weights, chunk_left, low, span), me, (left, right), more, count,
                      width, 2 * len(span) * slot * count * width * width)


def attention_weights(low, span, places, me_ref, uc, mem, mix, gq, gk, gv, gz, *refs):
    more = list(zip(refs, places))
    out, part = refs[-2:]
    _, every, width = uc.shape
    mem_rows = every // 9
    slot = every - mem_rows
    me = me_ref[0]
    for j in range(out.shape[0]):
        which = jnp.bitwise_xor(j + low, jnp.right_shift(me, 2))

        @pl.when(which == 0)
        def _():
            part[...] = sum(dot_tn(uc[u], gq[u]) for u in span)

        for place, ref in ((1, gk), (2, gv)):
            @pl.when(which == place)
            def _():
                part[...] = sum(dot_tn(mem[u], ref[u, :mem_rows]) + dot_tn(uc[u, :slot], ref[u, mem_rows:])
                                for u in span)

        @pl.when(which == 3)
        def _():
            part[...] = sum(dot_tn(mix[u], gz[u]) for u in span)

        emit_group(None, me, more, out, part, j)


def attention_group_grads(groups, me, arrays, span, more=()):
    _, every, width = arrays[0].shape
    low, count = groups
    return group_call(functools.partial(attention_weights, low, span), me, arrays, more, count, width,
                      2 * count * len(span) * every * width * width)


def restore_group(parts, me, value):
    place = jnp.bitwise_xor(pl.program_id(0), jnp.right_shift(me, 2))
    sub = jnp.bitwise_and(me, LANES_OUT - 1)
    for i, ref in enumerate(parts):
        @pl.when(place == i)
        def _():
            for r in range(LANES_OUT):
                value(r, ref[jnp.bitwise_xor(sub, r)].astype(F32))


def restore_wide(me_ref, *refs):
    *parts, out = refs
    rows = parts[0].shape[1]

    def put(r, got):
        out[0, r * rows : (r + 1) * rows] = got

    restore_group(parts, me_ref[0], put)


def restore_square(me_ref, *refs):
    parts, outs = refs[:4], refs[4:]
    rows = parts[0].shape[1]

    def put(r, got):
        for matrix, out in enumerate(outs):
            @pl.when(pl.program_id(0) == matrix)
            def _():
                out[0, r * rows : (r + 1) * rows] = got

    restore_group(parts, me_ref[0], put)


def restore(me, parts, kind):
    groups = len(parts)
    width = parts[0].shape[2]
    whole = pl.BlockSpec(parts[0].shape, lambda j, me: (0, 0, 0))
    if kind == "down":
        body, shapes = restore_wide, [(1, groups * width, width)]
        specs = [pl.BlockSpec((1, width, width), lambda j, me: (0, j, 0))]
    elif kind == "up":
        body, shapes = restore_wide, [(1, width, groups * width)]
        specs = [pl.BlockSpec((1, width, width), lambda j, me: (0, 0, j))]
    else:
        body, shapes = restore_square, [(1, width, width)] * groups
        specs = [pl.BlockSpec((1, width, width), lambda j, me: (0, 0, 0))] * groups
    return pl.pallas_call(
        body,
        grid_spec=pltpu.PrefetchScalarGridSpec(num_scalar_prefetch=1, grid=(groups,), in_specs=[whole] * groups,
                                               out_specs=specs),
        out_shape=[sds(s, F32) for s in shapes],
        compiler_params=pltpu.CompilerParams(vmem_limit_bytes=SMALL_LIMIT, dimension_semantics=("arbitrary",)),
        cost_estimate=cost_of(0, 6 * groups * width * width),
    )(me, *parts)


def swap(value, bit):
    n = lax.axis_size("dp")
    return lax.ppermute(value, "dp", [(i, i ^ (1 << bit)) for i in range(n)])


def added(a, b):
    return (a.astype(F32) + b.astype(F32)).astype(BF)


PLAN = "d1d2ududsudsusudsDsuUsS"
SPLIT = "d"
PATHS = {"d": (0, 1, 2, 3), "u": (0, 1, 2, 3), "s": (0, 1, 2, 3)}
KINDS = {"D": ("d", "down"), "U": ("u", "up"), "S": ("s", "square")}


class Order:
    def __init__(self):
        self.last = None

    def after(self, *values):
        if self.last is not None:
            values = lax.optimization_barrier((*values, self.last))[:-1]
        return values

    def made(self, value):
        self.last = value


class Sum:
    def __init__(self, order, name, bits, value, small=None):
        self.order = order
        self.path = PATHS[name]
        self.bits = bits
        self.value = value.reshape((-1,) + value.shape[2:])
        self.small = small
        self.split = name in SPLIT
        self.ahead = None
        self.stage = 1
        self.launch()

    def launch(self):
        if self.stage < STAGES:
            half = self.value.shape[0] // 2
            out, self.value = self.value[half:], self.value[:half]
            if self.small is not None:
                width = out.shape[-1]
                high = lax.reduce_precision(self.small, exponent_bits=8, mantissa_bits=7)
                parts = [out.reshape(-1, width), high.astype(BF), (self.small - high).astype(BF)]
                out = jnp.concatenate(parts, axis=0)
            bit = self.path[self.stage]
        else:
            out = self.value
            bit = self.path[2 * STAGES - 1 - self.stage]
        self.order.made(out)
        if self.stage == 2 * STAGES - 2:
            self.far = [swap(out, self.path[0])]
            out = out[self.ahead.shape[0] :] if self.ahead is not None else out
        self.got = swap(out, bit)
        if self.stage == 2 * STAGES - 3 and self.split:
            self.ahead = swap(out, self.path[1])

    def step(self):
        got, value = self.order.after(self.got, self.value)
        if self.stage == 2 * STAGES - 3 and self.split:
            got, value, self.ahead = self.order.after(self.got, self.value, self.ahead)
        if self.stage < STAGES:
            if self.small is not None:
                lines = value.shape[0] * value.shape[1]
                rows = self.small.shape[0]
                self.small = self.small + got[lines : lines + rows].astype(F32) + got[lines + rows :].astype(F32)
                got = got[:lines].reshape(value.shape)
            value = added(value, got)
            if self.stage == STAGES - 1:
                for bit in range(STAGES, self.bits):
                    value = added(value, swap(value, bit))
                    if self.small is not None:
                        self.small = self.small + swap(self.small, bit)
        elif self.stage < 2 * STAGES - 2:
            value = jnp.concatenate([value, got], axis=0)
        else:
            got = got if self.ahead is None else jnp.concatenate([self.ahead, got], axis=0)
            self.far.append(swap(got, self.path[0]))
            self.order.made(got)
            self.parts = [value, got] + self.far
            return
        self.value = value
        self.stage += 1
        self.launch()

    def restore(self, me, kind):
        parts = self.order.after(*self.parts)
        outs = restore(me, parts, kind)
        self.order.made(outs[0])
        return outs


def shifted(block, axis, distance):
    devices = range(lax.axis_size(axis))
    route = [(i - distance, i) for i in devices if i - distance in devices]
    return lax.ppermute(block, axis, route)


def on_device(ends, lengths, seg_group, norm_gain, norm_shift, w_query, w_key, w_value, qv_bias, w_out, out_bias,
              w_up, up_bias, w_down, down_bias):
    section = lax.axis_index("section")
    first = section == 0
    slots = lengths.shape[0]
    width = ends.shape[2]
    slot = ends.shape[1] // slots
    hid = w_up.shape[2]
    section = section.astype(jnp.int32).reshape(1)
    lower = jnp.concatenate([1 - section, lengths, seg_group])
    upper = jnp.concatenate([section, lengths, seg_group])

    bits = lax.axis_size("dp").bit_length() - 1
    place = lax.axis_index("dp").astype(jnp.int32)
    codes = {
        name: sum(jnp.bitwise_and(jnp.right_shift(place, bit), 1) << (STAGES - 1 - s) for s, bit in enumerate(path)).reshape(1)
        for name, path in PATHS.items()}

    vec = jnp.concatenate([norm_gain[0], norm_shift[0], qv_bias[0], out_bias, down_bias], axis=0)
    vec, lower, upper, codes, first = lax.optimization_barrier((vec, lower, upper, codes, first))
    vec = opening(vec)
    weights = (vec, up_bias, w_query[0], w_key[0], w_value[0], w_out[0], w_up[0], w_down[0])
    local = ends.reshape(slots, slot, width)

    kept = None
    sent = []
    for b in range(slots):
        y, kept = forward(weights, b, True, lower, slots, local, kept)
        sent.append(shifted(y, "section", 1))
    finals = []
    grads = dict.fromkeys(GRADS)
    smalls = [[], []]
    back = []
    for b in range(slots):
        y, kept = forward(weights, b, False, upper, slots, sent[b], kept)
        finals.append(y)
        apart = vec if b == slots - 1 else None
        grads, gx, gm, _, small = backward(weights, b, False, (True, True), upper, slots, local, apart, None, kept, grads)
        smalls[1].append(small)
        back.append(shifted(gx, "section", -1))
    memory_back = shifted(gm, "section", -1)
    held = dict(zip(KEPT, kept))
    firsts = []
    for b in range(slots - 1):
        grads, gx, _, _, small = backward(weights, b, True, (True, True), lower, slots, back[b], None, None, kept, grads)
        smalls[0].append(small)
        firsts.append(gx)
    b = slots - 1
    sides = (("d", True, "g", "gd"), ("u", False, "h", "gf"))
    early = tuple(ffn_group_grads((0, 4), side, codes[name], held[left], grads[right], range(b))
                  for name, side, left, right in sides)
    arrays = [held[name] for name in ("uc", "mem", "mix")] + [grads[name] for name in ("gq", "gk", "gv", "gz")]
    early += (attention_group_grads((0, 4), codes["s"], arrays, range(b)),)
    last, *early = lax.optimization_barrier((back[b], *early))
    grads, _, _, ga, small = backward(weights, b, True, (True, False), lower, slots, last, vec, None, kept, grads)
    smalls[0].append(small)

    order = Order()
    now = range(b, slots)
    far = [swap(ffn_group_grads((2, 2), side, codes[name], held[left], grads[right], now, [(part, 2)]), 0)
           for (name, side, left, right), part in zip(sides, early)]
    down, up = [ffn_group_grads((0, 2), side, codes[name], held[left], grads[right], now, [(part, 0), (more, 0)])
                for (name, side, left, right), part, more in zip(sides, early, far)]
    ga, down, up = lax.optimization_barrier((ga, down, up))
    down = Sum(order, "d", bits, down)
    up = Sum(order, "u", bits, up)
    grads, gx, _, _, small = backward(weights, b, True, (False, True), lower, slots, last, memory_back, ga, kept, grads)
    smalls[0].append(small)
    firsts.append(gx)
    small = jnp.where(first, sum(smalls[0]), sum(smalls[1]))

    names = ("gq", "gk", "gv", "gz")
    arrays = [held[name] for name in ("uc", "mem", "mix")] + [grads[name] for name in names]
    streams = {"d": down, "u": up}
    outs = {}
    for event in PLAN:
        if event == "1":
            arrays[-1], small = order.after(arrays[-1], small)
            away = swap(attention_group_grads((2, 2), codes["s"], arrays, now, [(early[2], 2)]), 0)
            small = small + swap(small, 0)
        elif event == "2":
            away, small = order.after(away, small)
            streams["s"] = Sum(order, "s", bits, attention_group_grads((0, 2), codes["s"], arrays, now, [(early[2], 0), (away, 0)]), small)
        elif event in KINDS:
            if event == "U":
                small = streams["s"].small
                small_outs = (small[None, 0:3], small[None, 3:6], small[None, 6:8], small[8:9], small[9:10],
                              small[10 : 10 + hid // width].reshape(1, hid))
                streams["u"].parts[0], *small_outs = order.after(streams["u"].parts[0], *small_outs)
            outs[event] = streams[KINDS[event][0]].restore(codes[KINDS[event][0]], KINDS[event][1])
        else:
            streams[event].step()
    (grad_down,), (grad_up,), (grad_q, grad_k, grad_v, grad_o) = outs["D"], outs["U"], outs["S"]
    grad_gain, grad_shift, grad_qv, grad_out, grad_down_bias, grad_up_bias = small_outs
    ends_out = jnp.where(first, jnp.stack([gx[:slot] for gx in firsts]), jnp.stack([y[:slot] for y in finals]))
    ends_out = ends_out.reshape(1, slots * slot, width)
    return (ends_out, grad_gain, grad_shift, grad_q, grad_k, grad_v, grad_qv, grad_o, grad_out, grad_up, grad_up_bias,
            grad_down, grad_down_bias)


def solution(mesh):
    placed = (
        P("section", "dp", None), P("dp"), P("dp"),
        P("section", None, None), P("section", None, None), P("section", None, None), P("section", None, None),
        P("section", None, None), P("section", None, None), P("section", None, None), P("section", None),
        P("section", None, None), P("section", None), P("section", None, None), P("section", None),
    )
    return jax.shard_map(
        on_device,
        mesh=mesh,
        in_specs=placed,
        out_specs=(
            P("section", "dp", None), P("section", None, None), P("section", None, None), P("section", None, None),
            P("section", None, None), P("section", None, None), P("section", None, None), P("section", None, None),
            P("section", None), P("section", None, None), P("section", None), P("section", None, None),
            P("section", None),
        ),
        check_vma=False,
    )
```
